32 devices in a mesh: groups: 2 (over x), gx: 16 (over z, y, core).
Axes of the slice: x: 2, y: 2, z: 4, core: 2. Of those that a mesh axis runs over, the one named last changes fastest.
Arguments:
- probes: float32 [64, 1024, 512], P(None, ('groups', 'gx')), parts along dimension 1, as said below
- kappa: float32 [1024, 512], P(('groups', 'gx')), parts along dimension 0, may hold values from 0.1 to 0.8
- speed: float32 [1024, 512], P(('groups', 'gx')), parts along dimension 0, may hold values from 0.05 to 0.5
- friction: float32 [1024, 512], P(('groups', 'gx')), parts along dimension 0, may hold values from 0.1 to 1
- upwind: int32 [1024, 16], P(('groups', 'gx')), parts along dimension 0, may hold values from 0 to 3
- probe_sites: int32 [128], P('groups'), parts along dimension 0, may hold values from 0 to 262143
Outputs:
- basis: float32 [64, 1024, 512], P(None, ('groups', 'gx')), parts along dimension 1
- factor: float32 [128, 64], P('groups'), parts along dimension 0
The draws below stay inside these ranges and needn't reach their ends.
There are 2 independent parts, one for each index of `groups`. The reference program is written for one: setup_inputs(seed, part) draws one part's arguments, and reference() takes and returns one part's arrays. A program takes and returns all parts, laid end to end along the dimension named above; each array names one. Nothing has to cross between parts.
Inputs may be any that keep to these rules, and one draw needn't show every extreme that they name: upwind neighbour of a block of 32 cells of one row: 0 above, 1 below, 2 left, 3 right. `probe_sites`: flat index row * 512 + column of the cell of probe k's impulse. `probes`: probe fields.
All inputs are finite; a program needn't handle non-finite values.
Results may differ from the reference program's by a relative error of at most 0.0003.
Values sent between devices are 32-bit elements; how exact they have to be, the bound alone decides.
No kernel may reach another device: no remote copies, remote signals or barrier semaphores. Data moves between devices by JAX's collectives and lax.ppermute only.
A program may use at most 64 MiB of HBM per device.

```python
import math
import jax
import jax.numpy as jnp

K = 64
COLS = 512
BLOCK_COLS = 32
NX = 512


def draw_probes(key, part):
    noise_key, column_key, row_key, shared_key = jax.random.split(key, 4)
    columns = jnp.exp(math.log(10.0) * jax.random.uniform(column_key, (K,), dtype=jnp.float32))
    rising = jnp.arange(NX, dtype=jnp.float32) / max(NX - 1, 1)
    row_scale = jnp.exp(math.log(3.0) * rising + math.log(3.4) * jax.random.uniform(row_key, (NX,), dtype=jnp.float32))
    own_part = jax.random.normal(noise_key, (K, NX, COLS), dtype=jnp.float32)
    shared = jax.random.normal(shared_key, (1, NX, COLS), dtype=jnp.float32)
    noise_field = 3.0 * (shared + 0.012 * own_part)
    return (noise_field * columns[:, None, None] * row_scale[None, :, None]).astype(jnp.float32)


def plant(drawn, key, least, top_value):
    spot = [jax.random.randint(jax.random.fold_in(key, axis), (), 0, length) for axis, length in enumerate(drawn.shape)]
    longest = drawn.shape.index(max(drawn.shape))
    beside = spot[:longest] + [(spot[longest] + 1) % drawn.shape[longest]] + spot[longest + 1:]
    return drawn.at[tuple(spot)].set(least).at[tuple(beside)].set(top_value)


def levels(key, shape, cuts, least, high):
    loudness = 1.0
    for position, parts in cuts:
        draws = jax.random.uniform(jax.random.fold_in(jax.random.fold_in(key, 6), position), (parts,), jnp.float32, least / len(cuts), high / len(cuts))
        loudness = loudness * jnp.repeat(jnp.exp(draws), shape[position] // parts).reshape((-1,) + (1,) * (len(shape) - 1 - position))
    return loudness


def setup_inputs(seed: int = 0, part: int = 0) -> dict:
    key_list = jax.random.split(jax.random.key(seed), 7)
    part_keys = jax.random.split(jax.random.fold_in(key_list[6], part), 7)
    return {
        "probes": draw_probes(jax.random.fold_in(jax.random.fold_in(key_list[6], part), 71), part),
        "kappa": jnp.clip(jnp.exp(math.log(0.8) - 2.0794415 * jax.random.uniform(part_keys[1], (NX, COLS), jnp.float32) ** levels(part_keys[1], (NX, COLS), ((0, 16),), -0.2, 0.2)), 0.1, 0.8),
        "speed": jnp.clip(jnp.exp(math.log(0.5) - 2.3025851 * jax.random.uniform(part_keys[2], (NX, COLS), jnp.float32) ** levels(part_keys[2], (NX, COLS), ((0, 16),), -0.2, 0.2)), 0.05, 0.5),
        "friction": jnp.clip(jnp.exp(math.log(1.0) - 2.3025851 * jax.random.uniform(part_keys[3], (NX, COLS), jnp.float32) ** levels(part_keys[3], (NX, COLS), ((0, 16),), -0.2, 0.2)), 0.1, 1.0),
        "upwind": plant(jax.random.randint(part_keys[4], (NX, COLS // BLOCK_COLS), 0, 4), jax.random.fold_in(part_keys[4], 1), 0, 3).astype(jnp.int32),
        "probe_sites": plant(jax.random.randint(part_keys[5], (K,), 0, NX * COLS), jax.random.fold_in(part_keys[5], 1), 0, (NX * COLS) - 1).astype(jnp.int32),
    }


TIME_STEP = 0.2
IMPULSE_GAIN = 3.0

def weights_of(kappa, speed, friction, upwind):
    directions = jnp.repeat(upwind, BLOCK_COLS, axis=1)
    center = 1.0 - TIME_STEP * (4.0 * kappa + speed + friction)
    side_weights = [TIME_STEP * (kappa + speed * (directions == direction).astype(jnp.float32)) for direction in range(4)]
    return (center, side_weights)

def forward(field_in, center, side_weights):
    padded = jnp.pad(field_in, ((0, 0), (1, 1), (1, 1)))
    return center * field_in + side_weights[0] * padded[:, :-2, 1:-1] + side_weights[1] * padded[:, 2:, 1:-1] + side_weights[2] * padded[:, 1:-1, :-2] + side_weights[3] * padded[:, 1:-1, 2:]

def adjoint(field_in, center, side_weights):
    moved_terms = [jnp.pad(side_weights[direction] * field_in, ((0, 0), (1, 1), (1, 1))) for direction in range(4)]
    return center * field_in + moved_terms[0][:, 2:, 1:-1] + moved_terms[1][:, :-2, 1:-1] + moved_terms[2][:, 1:-1, 2:] + moved_terms[3][:, 1:-1, :-2]

def reference(probes, kappa, speed, friction, upwind, probe_sites):
    center, side_weights = weights_of(kappa, speed, friction, upwind)
    cell_count = NX * COLS
    impulse = (jnp.arange(cell_count, dtype=jnp.int32)[None, :] == probe_sites[:, None]).astype(jnp.float32)
    strength = IMPULSE_GAIN * math.sqrt(cell_count)
    fields = (probes.reshape(K, cell_count) + strength * impulse).reshape(K, NX, COLS)
    response = forward(forward(fields, center, side_weights), center, side_weights)
    response = adjoint(adjoint(response, center, side_weights), center, side_weights)
    matrix = response.reshape(K, cell_count).T
    q_factor, r_factor = jnp.linalg.qr(matrix)
    sign_fix = jnp.sign(jnp.diagonal(r_factor))
    q_factor = q_factor * sign_fix[None, :]
    r_factor = r_factor * sign_fix[:, None]
    cell_scale = math.sqrt(cell_count)
    basis = (q_factor.T * cell_scale).reshape(K, NX, COLS)
    return (basis, r_factor / cell_scale)
```

```python
import functools
import math

import jax
import jax.numpy as jnp
from jax import lax
from jax.experimental import pallas as pl
from jax.experimental.pallas import tpu as pltpu
from jax.sharding import PartitionSpec as P

TIME_STEP = 0.2
IMPULSE_GAIN = 3.0
AXIS = "gx"
DEPTH = 4
PACK = 8
MIB = 1024 * 1024


def rolled(row, by):
    return pltpu.roll(row, by % row.shape[-1], row.ndim - 1)


def weight_row(weights, row, layer, like):
    return jnp.broadcast_to(weights[row, layer : layer + 1, :], like)


def sweep_row(source, at, target, to, probes, columns, center, above, below, left, right):
    for first in range(0, probes, 8):
        octet = slice(first, first + 8)
        middle = source[at, octet, :]
        target[to, octet, :] = (
            center * middle
            + above * source[at - 1, octet, :]
            + below * source[at + 1, octet, :]
            + left * rolled(middle, 1)
            + right * rolled(middle, -1)
        )


def forward_row(source, at, target, to, weights, w_at, probes, columns):
    like = (8, columns)
    sweep_row(
        source, at, target, to, probes, columns,
        *[weight_row(weights, w_at, layer, like) for layer in range(5)],
    )


def adjoint_row(source, at, target, to, weights, w_at, probes, columns):
    like = (8, columns)
    sweep_row(
        source, at, target, to, probes, columns,
        weight_row(weights, w_at, 0, like),
        weight_row(weights, w_at - 1, 2, like),
        weight_row(weights, w_at + 1, 1, like),
        rolled(weight_row(weights, w_at, 4, like), 1),
        rolled(weight_row(weights, w_at, 3, like), -1),
    )


def add_impulses(sites, target, first_row, row_count, base, probes, columns, strength):
    column_ids = lax.broadcasted_iota(jnp.int32, (1, columns), 1)

    def one(k, carry):
        site = sites[k]
        row = site // columns - first_row

        @pl.when((row >= 0) & (row < row_count))
        def _():
            hit = jnp.where(column_ids == site % columns, strength, 0.0)
            target[base + row, pl.ds(k, 1), :] += hit

        return carry

    lax.fori_loop(0, probes, one, 0)


def pack_kernel(cells, kappa, speed, friction, upwind, weights, to_below, to_above, sems):
    probes, rows, columns = cells.shape
    copies = []
    for r in range(DEPTH):
        for side, target in enumerate((to_above, to_below)):
            row = r if side == 0 else rows - DEPTH + r
            copies.append(
                pltpu.make_async_copy(cells.at[:, row, :], target.at[r, pl.ds(0, probes), :], sems.at[side, r])
            )
    for copy in copies:
        copy.start()
    blocks = upwind.shape[1]
    width = columns // blocks
    spread = (
        lax.broadcasted_iota(jnp.int32, (blocks, columns), 1) // width
        == lax.broadcasted_iota(jnp.int32, (blocks, columns), 0)
    ).astype(jnp.bfloat16)
    directions = jnp.dot(
        upwind[...].astype(jnp.float32).astype(jnp.bfloat16), spread, preferred_element_type=jnp.float32
    )
    column_ids = lax.broadcasted_iota(jnp.int32, (rows, columns), 1)
    k, s = kappa[...], speed[...]
    layers = [1.0 - TIME_STEP * (4.0 * k + s + friction[...])]
    for direction in range(4):
        chosen = jnp.where(jnp.abs(directions - direction) < 0.5, s, 0.0)
        layers.append(TIME_STEP * (k + chosen))
    layers[3] = jnp.where(column_ids == 0, 0.0, layers[3])
    layers[4] = jnp.where(column_ids == columns - 1, 0.0, layers[4])
    for index in range(PACK):
        layer = layers[index] if index < 5 else jnp.zeros((rows, columns), jnp.float32)
        for r in range(rows):
            weights[r, index : index + 1, :] = layer[r : r + 1, :]
    for r in range(DEPTH):
        to_above[r, probes:, :] = weights[r]
        to_below[r, probes:, :] = weights[rows - DEPTH + r]
    for copy in copies:
        copy.wait()


def inner_kernel(strength, sites, cells, weights, response, top, bottom, v, f1, f2, a1, sems):
    rows, probes, columns = v.shape
    first_row = lax.axis_index(AXIS) * rows

    copies = [pltpu.make_async_copy(cells.at[:, r, :], v.at[r], sems.at[r]) for r in range(rows)]
    for copy in copies:
        copy.start()
    for copy in copies:
        copy.wait()
    add_impulses(sites, v, first_row, rows, 0, probes, columns, strength)

    def sweep(row_fn, source, target, first, last):
        def body(r, carry):
            row_fn(source, r, target, r, weights, r, probes, columns)
            return carry

        lax.fori_loop(first, last, body, 0)

    sweep(forward_row, v, f1, 1, rows - 1)
    sweep(forward_row, f1, f2, 2, rows - 2)
    sweep(adjoint_row, f2, a1, 3, rows - 3)

    def body(r, carry):
        adjoint_row(a1, r, response, r - DEPTH, weights, r, probes, columns)
        return carry

    lax.fori_loop(DEPTH, rows - DEPTH, body, 0)
    for level, field in enumerate((v, f1, f2, a1)):
        for j in range(2):
            top[level, j] = field[level + j]
            bottom[level, j] = field[rows - 2 - level + j]


def edge_kernel(strength, rows, sites, above, below, weights, top, bottom, out_top, out_bottom, w, va, vb, la, lb):
    probes, columns = top.shape[2:]
    first_row = lax.axis_index(AXIS) * rows
    half = 3 * DEPTH
    for r in range(DEPTH):
        w[r] = above[r, probes:, :]
        w[half + 2 * DEPTH + r] = below[r, probes:, :]
        va[r] = above[r, :probes, :]
        vb[2 + r] = below[r, :probes, :]
    for r in range(2 * DEPTH):
        w[DEPTH + r] = weights[r]
        w[half + r] = weights[rows - 2 * DEPTH + r]
    for j in range(2):
        va[DEPTH + j] = top[0, j]
        vb[j] = bottom[0, j]
        for level in range(1, 4):
            la[level - 1, DEPTH + j] = top[level, j]
            lb[level - 1, j] = bottom[level, j]
    add_impulses(sites, va, first_row - DEPTH, DEPTH, 0, probes, columns, strength)
    add_impulses(sites, vb, first_row + rows, DEPTH, 2, probes, columns, strength)
    chain_a = [va, la.at[0], la.at[1], la.at[2], out_top]
    chain_b = [vb, lb.at[0], lb.at[1], lb.at[2], out_bottom]
    for level in range(4):
        row_fn = forward_row if level < 2 else adjoint_row

        def body(j, carry, level=level, row_fn=row_fn):
            row_fn(chain_a[level], j + 1, chain_a[level + 1], j, w, level + 1 + j, probes, columns)
            to = j if level == 3 else j + 2
            row_fn(chain_b[level], j + 1, chain_b[level + 1], to, w, half + 2 * DEPTH - 1 - level + j, probes, columns)
            return carry

        lax.fori_loop(0, DEPTH, body, 0)


def whole(memory=pltpu.VMEM):
    return pl.BlockSpec(memory_space=memory)


def summed(value):
    count = lax.axis_size(AXIS)
    if count & (count - 1):
        return lax.psum(value, AXIS)
    distance = 1
    while distance < count:
        value = value + lax.ppermute(value, AXIS, [(i, i ^ distance) for i in range(count)])
        distance *= 2
    return value


def responses(probes, kappa, speed, friction, upwind, probe_sites):
    count, rows, columns = probes.shape
    strength = IMPULSE_GAIN * math.sqrt(rows * columns * lax.axis_size(AXIS))
    f32 = jnp.float32
    params = pltpu.CompilerParams(vmem_limit_bytes=56 * MIB)
    halo = jax.ShapeDtypeStruct((DEPTH, count + PACK, columns), f32)
    weights, to_below, to_above = pl.pallas_call(
        pack_kernel,
        out_shape=(jax.ShapeDtypeStruct((rows, PACK, columns), f32), halo, halo),
        in_specs=[whole(pl.ANY), whole(), whole(), whole(), whole()],
        out_specs=(whole(), whole(), whole()),
        scratch_shapes=[pltpu.SemaphoreType.DMA((2, DEPTH))],
        compiler_params=params,
        name="pack",
    )(probes, kappa, speed, friction, upwind)
    size = lax.axis_size(AXIS)
    from_above = lax.ppermute(to_below, AXIS, [(i, i + 1) for i in range(size - 1)])
    from_below = lax.ppermute(to_above, AXIS, [(i + 1, i) for i in range(size - 1)])
    kept = jax.ShapeDtypeStruct((4, 2, count, columns), f32)
    field = pltpu.VMEM((rows, count, columns), f32)
    inner, top, bottom = pl.pallas_call(
        functools.partial(inner_kernel, strength),
        out_shape=(jax.ShapeDtypeStruct((rows - 2 * DEPTH, count, columns), f32), kept, kept),
        in_specs=[whole(pltpu.SMEM), whole(pl.ANY), whole()],
        out_specs=(whole(), whole(), whole()),
        scratch_shapes=[field] * 4 + [pltpu.SemaphoreType.DMA((rows,))],
        compiler_params=params,
        cost_estimate=pl.CostEstimate(flops=10**10, bytes_accessed=16 * MIB, transcendentals=0),
        name="inner_rows",
    )(probe_sites, probes, weights)
    outer = jax.ShapeDtypeStruct((DEPTH, count, columns), f32)
    fields = pltpu.VMEM((DEPTH + 2, count, columns), f32)
    levels = pltpu.VMEM((3, DEPTH + 2, count, columns), f32)
    out_top, out_bottom = pl.pallas_call(
        functools.partial(edge_kernel, strength, rows),
        out_shape=(outer, outer),
        in_specs=[whole(pltpu.SMEM)] + [whole()] * 5,
        out_specs=(whole(), whole()),
        scratch_shapes=[pltpu.VMEM((6 * DEPTH, PACK, columns), f32), fields, fields, levels, levels],
        compiler_params=params,
        name="edge_rows",
    )(probe_sites, from_above, from_below, weights, top, bottom)
    return out_top, inner, out_bottom


def gram_factor(field):
    local_gram = jnp.einsum("rkc,rlc->kl", field, field, precision=lax.Precision.HIGHEST)
    return jnp.linalg.cholesky(summed(local_gram))


def on_device(probes, kappa, speed, friction, upwind, probe_sites):
    count, rows, columns = probes.shape
    field = jnp.concatenate(responses(probes, kappa, speed, friction, upwind, probe_sites), axis=0)
    cell_scale = math.sqrt(rows * columns * lax.axis_size(AXIS))
    identity = jnp.eye(count, dtype=jnp.float32)
    lowers = []
    for _ in range(2):
        lower = gram_factor(field)
        inverse = jax.scipy.linalg.solve_triangular(lower, identity, lower=True)
        field = jnp.einsum("kl,rlc->rkc", inverse, field, precision=lax.Precision.HIGHEST)
        lowers.append(lower)
    factor = jnp.dot(lowers[0], lowers[1], precision=lax.Precision.HIGHEST).T / cell_scale
    return (jnp.swapaxes(field, 0, 1) * cell_scale, factor)


def solution(mesh):
    return jax.shard_map(
        on_device,
        mesh=mesh,
        in_specs=(
            P(None, ("groups", "gx"), None),
            P(("groups", "gx"), None),
            P(("groups", "gx"), None),
            P(("groups", "gx"), None),
            P(("groups", "gx"), None),
            P("groups"),
        ),
        out_specs=(P(None, ("groups", "gx"), None), P("groups", None)),
        check_vma=False,
    )
```

```python
import functools
import math

import jax
import jax.numpy as jnp
from jax import lax
from jax.experimental import pallas as pl
from jax.experimental.pallas import tpu as pltpu
from jax.sharding import PartitionSpec as P

TIME_STEP = 0.2
IMPULSE_GAIN = 3.0
AXIS = "gx"
DEPTH = 4
PACK = 8
MIB = 1024 * 1024


def rolled(row, by):
    return pltpu.roll(row, by % row.shape[-1], row.ndim - 1)


def weight_row(weights, row, layer, like):
    return jnp.broadcast_to(weights[layer, pl.ds(row, 1), :], like)


def in_steps(first, last, body, step=6):
    whole_steps = (last - first) // step

    def several(index, carry):
        for j in range(step):
            body(first + index * step + j)
        return carry

    lax.fori_loop(0, whole_steps, several, 0)
    for r in range(first + whole_steps * step, last):
        body(r)


def sweep_row(source, at, target, to, probes, columns, center, above, below, left, right):
    for first in range(0, probes, 8):
        octet = slice(first, first + 8)
        middle = source[at, octet, :]
        target[to, octet, :] = (
            center * middle
            + above * source[at - 1, octet, :]
            + below * source[at + 1, octet, :]
            + left * rolled(middle, 1)
            + right * rolled(middle, -1)
        )


def forward_row(source, at, target, to, weights, w_at, probes, columns):
    like = (8, columns)
    sweep_row(
        source, at, target, to, probes, columns,
        *[weight_row(weights, w_at, layer, like) for layer in range(5)],
    )


def adjoint_row(source, at, target, to, weights, w_at, probes, columns):
    like = (8, columns)
    sweep_row(
        source, at, target, to, probes, columns,
        weight_row(weights, w_at, 0, like),
        weight_row(weights, w_at - 1, 2, like),
        weight_row(weights, w_at + 1, 1, like),
        rolled(weight_row(weights, w_at, 4, like), 1),
        rolled(weight_row(weights, w_at, 3, like), -1),
    )


def add_impulses(sites, target, place_of, probes, columns, strength):
    column_ids = lax.broadcasted_iota(jnp.int32, (1, columns), 1)

    def one(k, carry):
        site = sites[k]
        held, place = place_of(lax.div(site, columns))

        @pl.when(held)
        def _():
            hit = jnp.where(column_ids == lax.rem(site, columns), strength, 0.0)
            target[place, pl.ds(k, 1), :] += hit

        return carry

    lax.fori_loop(0, probes, one, 0)


def pack_kernel(cells, kappa, speed, friction, upwind, weights, to_below, to_above, sems):
    probes, rows, columns = cells.shape
    copies = []
    for r in range(DEPTH):
        for side, target in enumerate((to_above, to_below)):
            row = r if side == 0 else rows - DEPTH + r
            copies.append(
                pltpu.make_async_copy(cells.at[:, row, :], target.at[r, pl.ds(0, probes), :], sems.at[side, r])
            )
    for copy in copies:
        copy.start()
    blocks = upwind.shape[0]
    width = columns // blocks
    spread = (
        lax.broadcasted_iota(jnp.int32, (blocks, columns), 1) // width
        == lax.broadcasted_iota(jnp.int32, (blocks, columns), 0)
    ).astype(jnp.bfloat16)
    directions = lax.dot_general(
        upwind[...].astype(jnp.float32).astype(jnp.bfloat16), spread, (((0,), (0,)), ((), ())),
        preferred_element_type=jnp.float32,
    )
    column_ids = lax.broadcasted_iota(jnp.int32, (rows, columns), 1)
    k, s = kappa[...], speed[...]
    layers = [1.0 - TIME_STEP * (4.0 * k + s + friction[...])]
    for direction in range(4):
        chosen = jnp.where(jnp.abs(directions - direction) < 0.5, s, 0.0)
        layers.append(TIME_STEP * (k + chosen))
    layers[3] = jnp.where(column_ids == 0, 0.0, layers[3])
    layers[4] = jnp.where(column_ids == columns - 1, 0.0, layers[4])
    for index, layer in enumerate(layers):
        weights[index] = layer
        for r in range(DEPTH):
            to_above[r, probes + index : probes + index + 1, :] = layer[r : r + 1]
            to_below[r, probes + index : probes + index + 1, :] = layer[rows - DEPTH + r : rows - DEPTH + r + 1]
    for r in range(DEPTH):
        for side in (to_above, to_below):
            side[r, probes + 5 :, :] = jnp.zeros((PACK - 5, columns), jnp.float32)
    for copy in copies:
        copy.wait()


def inner_kernel(
    strength, sites, cells, weights, digits, scale, pairs, top, bottom, v, f1, f2, a1, response, kept, sums, sems, out_sems
):
    rows, probes, columns = v.shape
    first_row = lax.axis_index(AXIS) * rows

    copies = [pltpu.make_async_copy(cells.at[:, r, :], v.at[r], sems.at[r]) for r in range(rows)]
    for copy in copies:
        copy.start()
    for copy in copies:
        copy.wait()
    add_impulses(
        sites, v, lambda row: ((row >= first_row) & (row < first_row + rows), row - first_row), probes, columns, strength
    )

    def sweep(row_fn, source, target, first, shift=0):
        def body(r):
            row_fn(source, r, target, r - shift, weights, r, probes, columns)

        in_steps(first, rows - first, body)

    sweep(forward_row, v, f1, 1)
    sweep(forward_row, f1, f2, 2)
    sweep(adjoint_row, f2, a1, 3)
    sweep(adjoint_row, a1, response, DEPTH, DEPTH)
    for level, field in enumerate((v, f1, f2, a1)):
        for j in range(2):
            top[level, j] = field[level + j]
            bottom[level, j] = field[rows - 2 - level + j]
    high, low = gram_pair(response, rows - 2 * DEPTH, digits, scale, kept, sums, out_sems)
    pairs[...] = jnp.concatenate([folded(high), folded(low)], axis=0)


def edge_kernel(
    strength, rows, sites, above, below, weights, top, bottom, inner_pairs, digits, scale, pairs,
    w, va, la, lb, response, kept, sums, out_sems,
):
    probes, columns = top.shape[2:]
    first_row = lax.axis_index(AXIS) * rows
    start_a, start_b = 2 * DEPTH, 4 * DEPTH
    vb = va.at[DEPTH + 2 :]
    for layer in range(5):
        for r in range(DEPTH):
            w[layer, DEPTH + r : DEPTH + r + 1, :] = above[r, probes + layer : probes + layer + 1, :]
            w[layer, start_b + 2 * DEPTH + r : start_b + 2 * DEPTH + r + 1, :] = below[
                r, probes + layer : probes + layer + 1, :
            ]
        w[layer, start_a : start_a + 8, :] = weights[layer, :8, :]
        w[layer, start_b : start_b + 8, :] = weights[layer, rows - 8 :, :]
    for r in range(DEPTH):
        va[r] = above[r, :probes, :]
        vb[2 + r] = below[r, :probes, :]
    for j in range(2):
        va[DEPTH + j] = top[0, j]
        vb[j] = bottom[0, j]
        for level in range(1, 4):
            la[level - 1, DEPTH + j] = top[level, j]
            lb[level - 1, j] = bottom[level, j]

    def place_of(row):
        near = row - first_row
        is_above = (near >= -DEPTH) & (near < 0)
        is_below = (near >= rows) & (near < rows + DEPTH)
        return is_above | is_below, jnp.where(is_above, near + DEPTH, near - rows + DEPTH + 4)

    add_impulses(sites, va, place_of, probes, columns, strength)
    chain_a = [va, la.at[0], la.at[1], la.at[2], response]
    chain_b = [vb, lb.at[0], lb.at[1], lb.at[2], response]
    for level in range(4):
        row_fn = forward_row if level < 2 else adjoint_row
        for j in range(DEPTH):
            row_fn(chain_a[level], j + 1, chain_a[level + 1], j, w, start_a + level - 3 + j, probes, columns)
            to = j + (DEPTH if level == 3 else 2)
            row_fn(chain_b[level], j + 1, chain_b[level + 1], to, w, start_b + 7 - level + j, probes, columns)
    ours = gram_pair(response, 2 * DEPTH, digits, scale, kept, sums, out_sems)
    half = probes // 2
    high, low = pair_sum(ours, (unfolded(inner_pairs[:half, :]), unfolded(inner_pairs[half:, :])))
    pairs[...] = jnp.concatenate([folded(high), folded(low)], axis=0)


DIGITS = 4
ROUNDER = 12582912.0


def rounded(value):
    return (value + ROUNDER) - ROUNDER


def digits_of(value):
    out = []
    for position in range(DIGITS):
        digit = rounded(value)
        out.append(digit)
        if position < DIGITS - 1:
            value = (value - digit) * 256.0
    return out


def largest_power(fits, like):
    power = jnp.full(like, 2.0**-63, jnp.float32)
    for step in (64, 32, 16, 8, 4, 2, 1):
        candidate = power * 2.0**step
        power = jnp.where((candidate <= 2.0**63) & fits(candidate), candidate, power)
    return power


def unit(size):
    return lax.broadcasted_iota(jnp.int32, (size, size), 0) == lax.broadcasted_iota(jnp.int32, (size, size), 1)


def as_row(column):
    size = column.shape[0]
    return jnp.sum(jnp.where(unit(size), jnp.broadcast_to(column, (size, size)), 0.0), axis=0, keepdims=True)


def pair_of(high, low):
    total = high + low
    return total, low - (total - high)


def pair_sum(a, b):
    (a_high, a_low), (b_high, b_low) = a, b
    total = a_high + b_high
    back = total - a_high
    error = (a_high - (total - back)) + (b_high - back)
    return pair_of(total, error + (a_low + b_low))


def gram_pair(field, rows, cells_out, scale_out, cells, sums, sems):
    probes, columns = field.shape[1:]

    def largest(index, so_far):
        for r in (2 * index, 2 * index + 1):
            so_far = tuple(jnp.maximum(m, jnp.abs(field[r, 8 * o : 8 * o + 8, :])) for o, m in enumerate(so_far))
        return so_far

    tops = lax.fori_loop(0, rows // 2, largest, tuple(jnp.zeros((8, columns), jnp.float32) for _ in range(probes // 8)))
    top = jnp.concatenate([jnp.max(m, axis=1, keepdims=True) for m in tops], axis=0)
    scale = largest_power(lambda power: top * power <= 128.0, (probes, 1))
    inverse = 1.0 / scale
    scale_out[...] = jnp.broadcast_to(inverse, scale_out.shape)
    sums[...] = jnp.zeros_like(sums)

    def cut(index, carry):
        for pair in range(2):
            for r in (4 * index + 2 * pair, 4 * index + 2 * pair + 1):
                parts = digits_of(field[r] * scale)
                cells[r] = jnp.concatenate([part.astype(jnp.bfloat16) for part in parts], axis=0)
                pltpu.make_async_copy(cells.at[r], cells_out.at[r], sems.at[r]).start()
        total = sums[...]
        for pair in range(2):
            r = 4 * index + 2 * pair
            two = jnp.concatenate([cells[r], cells[r + 1]], axis=1)
            product = lax.dot_general(two, two, (((1,), (1,)), ((), ())), preferred_element_type=jnp.float32)
            total = total + product.astype(jnp.int32)
        sums[...] = total
        return carry

    lax.fori_loop(0, rows // 4, cut, 0)
    places = []
    for place in range(2 * DIGITS - 1):
        terms = [
            sums[a * probes : (a + 1) * probes, (place - a) * probes : (place - a + 1) * probes]
            for a in range(DIGITS)
            if 0 <= place - a < DIGITS
        ]
        places.append(functools.reduce(lambda x, y: x + y, terms))
    for place in range(2 * DIGITS - 2, 0, -1):
        places[place - 1] = places[place - 1] + (places[place] >> 8)
        places[place] = places[place] & 255
    f32 = jnp.float32
    high = (places[0] >> 8).astype(f32) * 256.0
    middle = ((places[0] & 255) * 65536 + places[1] * 256 + places[2]).astype(f32) * 2.0**-16
    low = (places[3] * 65536 + places[4] * 256 + places[5]).astype(f32) * 2.0**-40
    total, rest = pair_of(high, middle)
    total, rest = pair_of(total, rest + low)
    across = as_row(inverse)
    def wait(r, carry):
        pltpu.make_async_copy(cells.at[r], cells_out.at[r], sems.at[r]).wait()
        return carry

    lax.fori_loop(0, rows, wait, 0)
    return total * inverse * across, rest * inverse * across


def folded(square):
    half = square.shape[0] // 2
    return jnp.concatenate([square[:half], square[half:]], axis=1)


def unfolded(block):
    half = block.shape[1] // 2
    return jnp.concatenate([block[:, :half], block[:, half:]], axis=0)


def dot(a, b, dims=((1,), (0,))):
    return lax.dot_general(
        a, b, (dims, ((), ())), precision=lax.Precision.HIGHEST, preferred_element_type=jnp.float32
    )


def turned_over(block):
    size, wide = block.shape
    square = jnp.concatenate([block, jnp.zeros((wide - size, wide), jnp.float32)], axis=0)
    return jnp.transpose(square)[:, :size]


def eliminated(block):
    size, wide = block.shape
    groups = [block[8 * g : 8 * g + 8] for g in range(size // 8)]
    like = (8, wide)
    below = lax.broadcasted_iota(jnp.int32, like, 0)
    for j in range(size):
        g, s = divmod(j, 8)
        row = jnp.broadcast_to(groups[g][s : s + 1], like)
        scaled = row / jnp.broadcast_to(row[:, j : j + 1], like)
        for other in range(g, size // 8):
            column = jnp.broadcast_to(groups[other][:, j : j + 1], like)
            if other == g:
                if s == 7:
                    continue
                column = jnp.where(below > s, column, 0.0)
            groups[other] = groups[other] - column * scaled
    return normalised(jnp.concatenate(groups, axis=0))


def normalised(block):
    size, wide = block.shape
    row_ids = lax.broadcasted_iota(jnp.int32, block.shape, 0)
    lanes = lax.broadcasted_iota(jnp.int32, block.shape, 1)
    pivots = jnp.sum(jnp.where(row_ids == lanes, block, 0.0), axis=1, keepdims=True)
    scale = lax.rsqrt(pivots)
    scale = scale * (1.5 - 0.5 * pivots * scale * scale)
    block = block * scale
    keep = (lanes >= row_ids) & ((lanes < size) | (lanes - size <= row_ids))
    return jnp.where(keep, block, 0.0)


def eliminated_slowly(block, work):
    size, wide = block.shape
    work[...] = block
    row_ids = lax.broadcasted_iota(jnp.int32, (size, 1), 0)
    lanes = lax.broadcasted_iota(jnp.int32, (1, wide), 1)

    def step(j, carry):
        row = work[pl.ds(j, 1), :]
        pivot = jnp.sum(jnp.where(lanes == j, row, 0.0), axis=1, keepdims=True)
        column = jnp.sum(jnp.where(lanes == j, work[...], 0.0), axis=1, keepdims=True)
        work[...] = work[...] - jnp.where(row_ids > j, column, 0.0) * (row / pivot)
        return carry

    lax.fori_loop(0, size, step, 0)
    return normalised(work[...])


def stacked_digits(value):
    return jnp.concatenate([part.astype(jnp.bfloat16) for part in digits_of(value)], axis=0)


def residual(high, low, left, right):
    size = high.shape[0]
    product = lax.dot_general(left, right, (((1,), (1,)), ((), ())), preferred_element_type=jnp.float32)
    places = []
    for place in range(2 * DIGITS - 1):
        terms = [
            product[a * size : (a + 1) * size, (place - a) * size : (place - a + 1) * size]
            for a in range(DIGITS)
            if 0 <= place - a < DIGITS
        ]
        places.append(functools.reduce(lambda x, y: x + y, terms))
    rest = high
    total = jnp.zeros_like(high)
    for place in range(5):
        if place == 2:
            rest = rest + low * 2.0**16
        digit = rounded(rest) if place < 4 else rest
        rest = (rest - digit) * 256.0
        total = total * 256.0 + (digit - places[place])
    total = total - (places[5] * 2.0**-8 + places[6] * 2.0**-16)
    return total * 2.0**-32


def solve_kernel(
    cell_scale, pairs, inner_scale, edge_scale, inner, edge, basis, factor,
    inner_cells, edge_cells, rows_out, work, change, change_inverse, in_sems, out_sems,
):
    size = pairs.shape[0]
    inner_rows, edge_rows = inner.shape[0], edge.shape[0]
    rows = inner_rows + edge_rows
    loads = [
        pltpu.make_async_copy(inner, inner_cells, in_sems.at[0]),
        pltpu.make_async_copy(edge, edge_cells, in_sems.at[1]),
    ]
    for copy in loads:
        copy.start()
    high, low = unfolded(pairs[: size // 2, :]), unfolded(pairs[size // 2 :, :])
    is_diagonal = unit(size)
    diagonal = jnp.sum(jnp.where(is_diagonal, high, 0.0), axis=1, keepdims=True)
    scale = largest_power(lambda power: diagonal * power * power < 1.0, (size, 1))
    across = as_row(scale)
    high, low = high * scale * across, low * scale * across
    identity = jnp.where(is_diagonal, 1.0, 0.0)
    first = eliminated(jnp.concatenate([high, identity], axis=1))
    inverse = first[:, size:]
    lower = turned_over(first)[:size]
    lower_digits = stacked_digits(lower * 128.0)
    missed = residual(high * 2.0**14, low * 2.0**14, lower_digits, lower_digits) * 2.0**-14
    inverse_top = jnp.max(jnp.abs(inverse), axis=1, keepdims=True)
    inverse_scale = largest_power(lambda power: inverse_top * power <= 128.0, (size, 1))
    goal = identity * (inverse_scale * 128.0)
    skew = residual(
        goal, jnp.zeros_like(goal), stacked_digits(inverse * inverse_scale), stacked_digits(first[:, :size] * 128.0)
    ) * (-1.0 / 128.0 / inverse_scale)
    near = identity + skew
    error = dot(dot(inverse, missed), inverse, ((1,), (1,))) + (dot(near, near, ((1,), (1,))) - identity)
    weight = jnp.where(
        is_diagonal, 0.5,
        jnp.where(
            lax.broadcasted_iota(jnp.int32, (size, size), 0) > lax.broadcasted_iota(jnp.int32, (size, size), 1), 1.0, 0.0
        ),
    )
    spread = jnp.sum(error * error)
    is_small = spread < 4e-4

    @pl.when(is_small)
    def _():
        y = weight * error
        for _ in range(4):
            y = weight * (error - dot(y, y, ((1,), (1,))))
        change[...] = y
        square = dot(y, y)
        change_inverse[...] = (identity - y) + dot(identity - y, square)

    @pl.when(jnp.logical_not(is_small))
    def _():
        second = eliminated_slowly(jnp.concatenate([identity + error, identity], axis=1), work)
        change[...] = turned_over(second)[:size] - identity
        change_inverse[...] = second[:, size:]

    turn = change[...] - skew
    full = lower + dot(lower, turn - dot(skew, turn))
    full = jnp.concatenate([full, jnp.zeros_like(full)], axis=1)
    factor[...] = turned_over(full)[:size] / across * (1.0 / cell_scale)
    mixing = dot(change_inverse[...], inverse) * across * cell_scale

    def stacked(cut):
        whole_part = mixing * as_row(cut[:, :1])
        pieces = []
        for _ in range(3):
            piece = whole_part.astype(jnp.bfloat16)
            whole_part = whole_part - piece.astype(jnp.float32)
            pieces.append(piece.astype(jnp.float32))
        tall = jnp.concatenate(pieces, axis=0)
        return jnp.concatenate([tall * 256.0**-a for a in range(DIGITS)], axis=1).astype(jnp.bfloat16)

    def finish(matrix, cells, first_row, count, shift):
        def one(r, carry):
            product = jnp.dot(matrix, cells[r + shift], preferred_element_type=jnp.float32)
            rows_out[r + first_row] = product[:size] + (product[size : 2 * size] + product[2 * size :])
            pltpu.make_async_copy(rows_out.at[r + first_row], basis.at[:, r + first_row, :], out_sems.at[r + first_row]).start()
            return carry

        lax.fori_loop(0, count, one, 0, unroll=4)

    for copy in loads:
        copy.wait()
    finish(stacked(inner_scale), inner_cells, DEPTH, inner_rows, 0)
    matrix = stacked(edge_scale)
    finish(matrix, edge_cells, 0, DEPTH, 0)
    finish(matrix, edge_cells, rows - DEPTH, DEPTH, DEPTH)

    def wait(r, carry):
        pltpu.make_async_copy(rows_out.at[r], basis.at[:, r, :], out_sems.at[r]).wait()
        return carry

    lax.fori_loop(0, rows, wait, 0)


def whole(memory=pltpu.VMEM):
    return pl.BlockSpec(memory_space=memory)


def call(kernel, name, out_shape, in_specs, out_specs, scratch_shapes=(), cost=None):
    return pl.pallas_call(
        kernel,
        out_shape=out_shape,
        in_specs=in_specs,
        out_specs=out_specs,
        scratch_shapes=scratch_shapes,
        compiler_params=pltpu.CompilerParams(vmem_limit_bytes=56 * MIB),
        cost_estimate=cost,
        name=name,
    )


def summed(pairs):
    count = lax.axis_size(AXIS)
    half = pairs.shape[0] // 2

    def add(a, b):
        return jnp.concatenate(pair_sum((a[:half], a[half:]), (b[:half], b[half:])), axis=0)

    if count & (count - 1):
        total = pairs
        for step in range(1, count):
            total = add(total, lax.ppermute(pairs, AXIS, [(i, (i + step) % count) for i in range(count)]))
        return total
    distance = 1
    while distance < count:
        pairs = add(pairs, lax.ppermute(pairs, AXIS, [(i, i ^ distance) for i in range(count)]))
        distance *= 2
    return pairs


def on_device(probes, kappa, speed, friction, upwind, probe_sites):
    count, rows, columns = probes.shape
    size = lax.axis_size(AXIS)
    f32 = jnp.float32
    cell_scale = math.sqrt(rows * columns * size)
    strength = IMPULSE_GAIN * cell_scale
    shape = jax.ShapeDtypeStruct
    halo = shape((DEPTH, count + PACK, columns), f32)
    weights, to_below, to_above = call(
        pack_kernel,
        "pack",
        (shape((5, rows, columns), f32), halo, halo),
        [whole(pl.ANY), whole(), whole(), whole(), whole()],
        (whole(), whole(), whole()),
        [pltpu.SemaphoreType.DMA((2, DEPTH))],
    )(probes, kappa, speed, friction, upwind.T)
    from_above = lax.ppermute(to_below, AXIS, [(i, i + 1) for i in range(size - 1)])
    from_below = lax.ppermute(to_above, AXIS, [(i + 1, i) for i in range(size - 1)])
    edge_count = 2 * DEPTH
    inner_count = rows - edge_count
    tall = DIGITS * count

    def digit_rows(number):
        return shape((number, tall, columns), jnp.bfloat16), shape((count, 128), f32), shape((count, 2 * count), f32)

    def digit_scratch(number):
        return [
            pltpu.VMEM((number, count, columns), f32),
            pltpu.VMEM((number, tall, columns), jnp.bfloat16),
            pltpu.VMEM((tall, tall), jnp.int32),
        ]

    kept = shape((4, 2, count, columns), f32)
    field = pltpu.VMEM((rows, count, columns), f32)
    inner, inner_scale, pairs, top, bottom = call(
        functools.partial(inner_kernel, strength),
        "inner_rows",
        digit_rows(inner_count) + (kept, kept),
        [whole(pltpu.SMEM), whole(pl.ANY), whole()],
        (whole(pl.ANY), whole(), whole(), whole(), whole()),
        [field] * 4
        + digit_scratch(inner_count)
        + [pltpu.SemaphoreType.DMA((rows,)), pltpu.SemaphoreType.DMA((inner_count,))],
        pl.CostEstimate(flops=10**10, bytes_accessed=16 * MIB, transcendentals=0),
    )(probe_sites, probes, weights)
    fields = pltpu.VMEM((2 * DEPTH + 4, count, columns), f32)
    levels = pltpu.VMEM((3, DEPTH + 2, count, columns), f32)
    edge, edge_scale, pairs = call(
        functools.partial(edge_kernel, strength, rows),
        "edge_rows",
        digit_rows(edge_count),
        [whole(pltpu.SMEM)] + [whole()] * 6,
        (whole(pl.ANY), whole(), whole()),
        [pltpu.VMEM((5, 8 * DEPTH, columns), f32), fields, levels, levels]
        + digit_scratch(edge_count)
        + [pltpu.SemaphoreType.DMA((edge_count,))],
    )(probe_sites, from_above, from_below, weights, top, bottom, pairs)
    pairs = summed(pairs)
    square = pltpu.VMEM((count, count), f32)
    return call(
        functools.partial(solve_kernel, cell_scale),
        "solve",
        (shape((count, rows, columns), f32), shape((count, count), f32)),
        [whole(), whole(), whole(), whole(pl.ANY), whole(pl.ANY)],
        (whole(pl.ANY), whole()),
        [
            pltpu.VMEM((inner_count, tall, columns), jnp.bfloat16),
            pltpu.VMEM((edge_count, tall, columns), jnp.bfloat16),
            pltpu.VMEM((rows, count, columns), f32),
            pltpu.VMEM((count, 2 * count), f32),
            square,
            square,
            pltpu.SemaphoreType.DMA((2,)),
            pltpu.SemaphoreType.DMA((rows,)),
        ],
    )(pairs, inner_scale, edge_scale, inner, edge)


def solution(mesh):
    return jax.shard_map(
        on_device,
        mesh=mesh,
        in_specs=(
            P(None, ("groups", "gx"), None),
            P(("groups", "gx"), None),
            P(("groups", "gx"), None),
            P(("groups", "gx"), None),
            P(("groups", "gx"), None),
            P("groups"),
        ),
        out_specs=(P(None, ("groups", "gx"), None), P("groups", None)),
        check_vma=False,
    )
```

```python
import functools
import math

import jax
import jax.numpy as jnp
from jax import lax
from jax.experimental import pallas as pl
from jax.experimental.pallas import tpu as pltpu
from jax.sharding import PartitionSpec as P

TIME_STEP = 0.2
IMPULSE_GAIN = 3.0
AXIS = "gx"
DEPTH = 4
PACK = 8
MIB = 1024 * 1024


def rolled(row, by):
    return pltpu.roll(row, by % row.shape[-1], row.ndim - 1)


def weight_row(weights, row, layer, like):
    return jnp.broadcast_to(weights[layer, pl.ds(row, 1), :], like)


def in_steps(first, last, body, step=6):
    whole_steps = (last - first) // step

    def several(index, carry):
        for j in range(step):
            body(first + index * step + j)
        return carry

    lax.fori_loop(0, whole_steps, several, 0)
    for r in range(first + whole_steps * step, last):
        body(r)


def sweep_row(source, at, target, to, probes, columns, center, above, below, left, right):
    for first in range(0, probes, 8):
        octet = slice(first, first + 8)
        middle = source[at, octet, :]
        target[to, octet, :] = (
            center * middle
            + above * source[at - 1, octet, :]
            + below * source[at + 1, octet, :]
            + left * rolled(middle, 1)
            + right * rolled(middle, -1)
        )


def forward_row(source, at, target, to, weights, w_at, probes, columns):
    like = (8, columns)
    sweep_row(
        source, at, target, to, probes, columns,
        *[weight_row(weights, w_at, layer, like) for layer in range(5)],
    )


def adjoint_row(source, at, target, to, weights, w_at, probes, columns):
    like = (8, columns)
    sweep_row(
        source, at, target, to, probes, columns,
        weight_row(weights, w_at, 0, like),
        weight_row(weights, w_at - 1, 2, like),
        weight_row(weights, w_at + 1, 1, like),
        rolled(weight_row(weights, w_at, 4, like), 1),
        rolled(weight_row(weights, w_at, 3, like), -1),
    )


def find_impulses(sites, found, held, probes, columns):
    def one(k, count):
        found[count] = k
        return count + held(lax.div(sites[k], columns)).astype(jnp.int32)

    return lax.fori_loop(0, probes, one, 0)


def add_impulses(sites, found, count, target, place_of, columns, strength):
    column_ids = lax.broadcasted_iota(jnp.int32, (1, columns), 1)

    def one(index, carry):
        k = found[index]
        site = sites[k]
        hit = jnp.where(column_ids == lax.rem(site, columns), strength, 0.0)
        target[place_of(lax.div(site, columns)), pl.ds(k, 1), :] += hit
        return carry

    lax.fori_loop(0, count, one, 0)


def pack_kernel(cells, kappa, speed, friction, upwind, weights, to_below, to_above, behind, sems):
    probes, rows, columns = cells.shape
    copies = []
    for r in range(DEPTH):
        for side, target in enumerate((to_above, to_below)):
            row = r if side == 0 else rows - DEPTH + r
            copies.append(
                pltpu.make_async_copy(cells.at[:, row, :], target.at[r, pl.ds(0, probes), :], sems.at[side, r])
            )
    for copy in copies:
        copy.start()
    blocks = upwind.shape[0]
    width = columns // blocks
    spread = (
        lax.broadcasted_iota(jnp.int32, (blocks, columns), 1) // width
        == lax.broadcasted_iota(jnp.int32, (blocks, columns), 0)
    ).astype(jnp.bfloat16)
    directions = lax.dot_general(
        upwind[...].astype(jnp.float32).astype(jnp.bfloat16), spread, (((0,), (0,)), ((), ())),
        preferred_element_type=jnp.float32,
    )
    column_ids = lax.broadcasted_iota(jnp.int32, (rows, columns), 1)
    k, s = kappa[...], speed[...]
    layers = [1.0 - TIME_STEP * (4.0 * k + s + friction[...])]
    for direction in range(4):
        chosen = jnp.where(jnp.abs(directions - direction) < 0.5, s, 0.0)
        layers.append(TIME_STEP * (k + chosen))
    layers[3] = jnp.where(column_ids == 0, 0.0, layers[3])
    layers[4] = jnp.where(column_ids == columns - 1, 0.0, layers[4])
    for index, layer in enumerate(layers):
        weights[index] = layer
        for r in range(DEPTH):
            behind[0, r, index : index + 1, :] = layer[r : r + 1]
            behind[1, r, index : index + 1, :] = layer[rows - DEPTH + r : rows - DEPTH + r + 1]
    behind[:, :, 5:, :] = jnp.zeros((2, DEPTH, PACK - 5, columns), jnp.float32)
    for side, target in enumerate((to_above, to_below)):
        copies.append(
            pltpu.make_async_copy(behind.at[side], target.at[:, pl.ds(probes, PACK), :], sems.at[side, DEPTH])
        )
        copies[-1].start()
    for copy in copies:
        copy.wait()


def inner_kernel(
    strength, sites, cells, weights, digits, scale, pairs, top, bottom, v, f1, f2, a1, response, kept, sums, found, sems, out_sems
):
    rows, probes, columns = v.shape
    first_row = lax.axis_index(AXIS) * rows

    copies = [pltpu.make_async_copy(cells.at[:, r, :], v.at[r], sems.at[r]) for r in range(rows)]
    for copy in copies:
        copy.start()
    hits = find_impulses(
        sites, found, lambda row: (row >= first_row) & (row < first_row + rows), probes, columns
    )
    for copy in copies:
        copy.wait()
    add_impulses(sites, found, hits, v, lambda row: row - first_row, columns, strength)

    def sweep(row_fn, source, target, first, shift=0):
        def body(r):
            row_fn(source, r, target, r - shift, weights, r, probes, columns)

        in_steps(first, rows - first, body)

    sweep(forward_row, v, f1, 1)
    sweep(forward_row, f1, f2, 2)
    sweep(adjoint_row, f2, a1, 3)
    sweep(adjoint_row, a1, response, DEPTH, DEPTH)
    for level, field in enumerate((v, f1, f2, a1)):
        for j in range(2):
            top[level, j] = field[level + j]
            bottom[level, j] = field[rows - 2 - level + j]
    high, low = gram_pair(response, rows - 2 * DEPTH, digits, scale, kept, sums, out_sems)
    pairs[...] = jnp.concatenate([folded(high), folded(low)], axis=0)


def edge_kernel(
    strength, rows, sites, above, below, weights, top, bottom, inner_pairs, digits, scale, pairs,
    w, va, la, lb, behind, response, kept, sums, found, sems, out_sems,
):
    probes, columns = top.shape[2:]
    first_row = lax.axis_index(AXIS) * rows
    start_a, start_b = 2 * DEPTH, 4 * DEPTH
    vb = va.at[DEPTH + 2 :]
    copies = [
        (above.at[:, pl.ds(probes, PACK), :], behind.at[0]),
        (below.at[:, pl.ds(probes, PACK), :], behind.at[1]),
        (weights.at[:, pl.ds(0, 8), :], w.at[:, pl.ds(start_a, 8), :]),
        (weights.at[:, pl.ds(rows - 8, 8), :], w.at[:, pl.ds(start_b, 8), :]),
        (above.at[:, pl.ds(0, probes), :], va.at[pl.ds(0, DEPTH)]),
        (below.at[:, pl.ds(0, probes), :], va.at[pl.ds(DEPTH + 4, DEPTH)]),
        (top.at[0], va.at[pl.ds(DEPTH, 2)]),
        (bottom.at[0], va.at[pl.ds(DEPTH + 2, 2)]),
        (top.at[pl.ds(1, 3)], la.at[:, pl.ds(DEPTH, 2)]),
        (bottom.at[pl.ds(1, 3)], lb.at[:, pl.ds(0, 2)]),
    ]
    copies = [pltpu.make_async_copy(source, target, sems.at[i]) for i, (source, target) in enumerate(copies)]
    for copy in copies:
        copy.start()

    def is_above(row):
        return (row >= first_row - DEPTH) & (row < first_row)

    def held(row):
        return is_above(row) | ((row >= first_row + rows) & (row < first_row + rows + DEPTH))

    hits = find_impulses(sites, found, held, probes, columns)
    for copy in copies:
        copy.wait()
    for layer in range(5):
        for r in range(DEPTH):
            w[layer, DEPTH + r : DEPTH + r + 1, :] = behind[0, r, layer : layer + 1, :]
            w[layer, start_b + 2 * DEPTH + r : start_b + 2 * DEPTH + r + 1, :] = behind[1, r, layer : layer + 1, :]
    add_impulses(
        sites, found, hits, va,
        lambda row: jnp.where(is_above(row), row - first_row + DEPTH, row - first_row - rows + DEPTH + 4), columns, strength,
    )
    chain_a = [va, la.at[0], la.at[1], la.at[2], response]
    chain_b = [vb, lb.at[0], lb.at[1], lb.at[2], response]
    for level in range(4):
        row_fn = forward_row if level < 2 else adjoint_row
        for j in range(DEPTH):
            row_fn(chain_a[level], j + 1, chain_a[level + 1], j, w, start_a + level - 3 + j, probes, columns)
            to = j + (DEPTH if level == 3 else 2)
            row_fn(chain_b[level], j + 1, chain_b[level + 1], to, w, start_b + 7 - level + j, probes, columns)
    ours = gram_pair(response, 2 * DEPTH, digits, scale, kept, sums, out_sems)
    half = probes // 2
    high, low = pair_sum(ours, (unfolded(inner_pairs[:half, :]), unfolded(inner_pairs[half:, :])))
    pairs[...] = jnp.concatenate([folded(high), folded(low)], axis=0)


DIGITS = 4
ROUNDER = 12582912.0


def rounded(value):
    return (value + ROUNDER) - ROUNDER


def digits_of(value):
    out = []
    for position in range(DIGITS):
        digit = rounded(value)
        out.append(digit)
        if position < DIGITS - 1:
            value = (value - digit) * 256.0
    return out


def largest_power(fits, like):
    power = jnp.full(like, 2.0**-63, jnp.float32)
    for step in (64, 32, 16, 8, 4, 2, 1):
        candidate = power * 2.0**step
        power = jnp.where((candidate <= 2.0**63) & fits(candidate), candidate, power)
    return power


def unit(size):
    return lax.broadcasted_iota(jnp.int32, (size, size), 0) == lax.broadcasted_iota(jnp.int32, (size, size), 1)


def as_row(column):
    size = column.shape[0]
    return jnp.sum(jnp.where(unit(size), jnp.broadcast_to(column, (size, size)), 0.0), axis=0, keepdims=True)


def pair_of(high, low):
    total = high + low
    return total, low - (total - high)


def pair_sum(a, b):
    (a_high, a_low), (b_high, b_low) = a, b
    total = a_high + b_high
    back = total - a_high
    error = (a_high - (total - back)) + (b_high - back)
    return pair_of(total, error + (a_low + b_low))


def gram_pair(field, rows, cells_out, scale_out, cells, sums, sems):
    probes, columns = field.shape[1:]

    def largest(index, so_far):
        for r in (2 * index, 2 * index + 1):
            so_far = tuple(jnp.maximum(m, jnp.abs(field[r, 8 * o : 8 * o + 8, :])) for o, m in enumerate(so_far))
        return so_far

    tops = lax.fori_loop(0, rows // 2, largest, tuple(jnp.zeros((8, columns), jnp.float32) for _ in range(probes // 8)))
    top = jnp.concatenate([jnp.max(m, axis=1, keepdims=True) for m in tops], axis=0)
    scale = largest_power(lambda power: top * power <= 128.0, (probes, 1))
    inverse = 1.0 / scale
    scale_out[...] = jnp.broadcast_to(inverse, scale_out.shape)
    sums[...] = jnp.zeros_like(sums)

    def cut(index, carry):
        for pair in range(2):
            for r in (4 * index + 2 * pair, 4 * index + 2 * pair + 1):
                parts = digits_of(field[r] * scale)
                cells[r] = jnp.concatenate([part.astype(jnp.bfloat16) for part in parts], axis=0)
        total = sums[...]
        for pair in range(2):
            r = 4 * index + 2 * pair
            two = jnp.concatenate([cells[r], cells[r + 1]], axis=1)
            product = lax.dot_general(two, two, (((1,), (1,)), ((), ())), preferred_element_type=jnp.float32)
            total = total + product.astype(jnp.int32)
        sums[...] = total
        for r in range(4):
            pltpu.make_async_copy(cells.at[4 * index + r], cells_out.at[4 * index + r], sems.at[4 * index + r]).start()
        return carry

    lax.fori_loop(0, rows // 4, cut, 0)
    places = []
    for place in range(2 * DIGITS - 1):
        terms = [
            sums[a * probes : (a + 1) * probes, (place - a) * probes : (place - a + 1) * probes]
            for a in range(DIGITS)
            if 0 <= place - a < DIGITS
        ]
        places.append(functools.reduce(lambda x, y: x + y, terms))
    for place in range(2 * DIGITS - 2, 0, -1):
        places[place - 1] = places[place - 1] + (places[place] >> 8)
        places[place] = places[place] & 255
    f32 = jnp.float32
    high = (places[0] >> 8).astype(f32) * 256.0
    middle = ((places[0] & 255) * 65536 + places[1] * 256 + places[2]).astype(f32) * 2.0**-16
    low = (places[3] * 65536 + places[4] * 256 + places[5]).astype(f32) * 2.0**-40
    total, rest = pair_of(high, middle)
    total, rest = pair_of(total, rest + low)
    across = as_row(inverse)
    def wait(r, carry):
        pltpu.make_async_copy(cells.at[r], cells_out.at[r], sems.at[r]).wait()
        return carry

    lax.fori_loop(0, rows, wait, 0)
    return total * inverse * across, rest * inverse * across


def folded(square):
    half = square.shape[0] // 2
    return jnp.concatenate([square[:half], square[half:]], axis=1)


def unfolded(block):
    half = block.shape[1] // 2
    return jnp.concatenate([block[:, :half], block[:, half:]], axis=0)


def dot(a, b, dims=((1,), (0,))):
    return lax.dot_general(
        a, b, (dims, ((), ())), precision=lax.Precision.HIGHEST, preferred_element_type=jnp.float32
    )


def turned_over(block):
    size, wide = block.shape
    square = jnp.concatenate([block, jnp.zeros((wide - size, wide), jnp.float32)], axis=0)
    return jnp.transpose(square)[:, :size]


PANEL = 4


def eliminated(block):
    size, wide = block.shape
    count = size // 8
    groups = [block[8 * g : 8 * g + 8] for g in range(count)]
    like = (8, wide)
    below = lax.broadcasted_iota(jnp.int32, like, 0)
    for first in range(0, size, PANEL):
        g, start = divmod(first, 8)
        columns = {
            o: [jnp.broadcast_to(groups[o][:, first + t : first + t + 1], like) for t in range(PANEL)]
            for o in range(g, count)
        }
        for t in range(PANEL):
            s = start + t
            across = [jnp.broadcast_to(columns[g][u][s : s + 1], like) for u in range(t, PANEL)]
            inverse = 1.0 / across[0]
            row = jnp.broadcast_to(groups[g][s : s + 1], like) * inverse
            across = [value * inverse for value in across]
            for o in range(g, count):
                if o == g and s == 7:
                    continue
                column = columns[o][t]
                if o == g:
                    column = jnp.where(below > s, column, 0.0)
                groups[o] = groups[o] - column * row
                for u in range(t + 1, PANEL):
                    columns[o][u] = columns[o][u] - column * across[u - t]
    return normalised(jnp.concatenate(groups, axis=0))


def normalised(block):
    size, wide = block.shape
    row_ids = lax.broadcasted_iota(jnp.int32, block.shape, 0)
    lanes = lax.broadcasted_iota(jnp.int32, block.shape, 1)
    pivots = jnp.sum(jnp.where(row_ids == lanes, block, 0.0), axis=1, keepdims=True)
    scale = lax.rsqrt(pivots)
    scale = scale * (1.5 - 0.5 * pivots * scale * scale)
    block = block * scale
    keep = (lanes >= row_ids) & ((lanes < size) | (lanes - size <= row_ids))
    return jnp.where(keep, block, 0.0)


def eliminated_slowly(block, work):
    size, wide = block.shape
    work[...] = block
    row_ids = lax.broadcasted_iota(jnp.int32, (size, 1), 0)
    lanes = lax.broadcasted_iota(jnp.int32, (1, wide), 1)

    def step(j, carry):
        row = work[pl.ds(j, 1), :]
        pivot = jnp.sum(jnp.where(lanes == j, row, 0.0), axis=1, keepdims=True)
        column = jnp.sum(jnp.where(lanes == j, work[...], 0.0), axis=1, keepdims=True)
        work[...] = work[...] - jnp.where(row_ids > j, column, 0.0) * (row / pivot)
        return carry

    lax.fori_loop(0, size, step, 0)
    return normalised(work[...])


def stacked_digits(value):
    return jnp.concatenate([part.astype(jnp.bfloat16) for part in digits_of(value)], axis=0)


def residual(high, low, left, right):
    size = high.shape[0]
    product = lax.dot_general(left, right, (((1,), (1,)), ((), ())), preferred_element_type=jnp.float32)
    places = []
    for place in range(2 * DIGITS - 1):
        terms = [
            product[a * size : (a + 1) * size, (place - a) * size : (place - a + 1) * size]
            for a in range(DIGITS)
            if 0 <= place - a < DIGITS
        ]
        places.append(functools.reduce(lambda x, y: x + y, terms))
    rest = high
    total = jnp.zeros_like(high)
    for place in range(5):
        if place == 2:
            rest = rest + low * 2.0**16
        digit = rounded(rest) if place < 4 else rest
        rest = (rest - digit) * 256.0
        total = total * 256.0 + (digit - places[place])
    total = total - (places[5] * 2.0**-8 + places[6] * 2.0**-16)
    return total * 2.0**-32


def solve_kernel(
    cell_scale, pairs, inner_scale, edge_scale, inner, edge, basis, factor,
    inner_cells, edge_cells, rows_out, work, change, change_inverse, in_sems, out_sems,
):
    size = pairs.shape[0]
    inner_rows, edge_rows = inner.shape[0], edge.shape[0]
    rows = inner_rows + edge_rows
    loads = [
        pltpu.make_async_copy(inner, inner_cells, in_sems.at[0]),
        pltpu.make_async_copy(edge, edge_cells, in_sems.at[1]),
    ]
    for copy in loads:
        copy.start()
    high, low = unfolded(pairs[: size // 2, :]), unfolded(pairs[size // 2 :, :])
    is_diagonal = unit(size)
    diagonal = jnp.sum(jnp.where(is_diagonal, high, 0.0), axis=1, keepdims=True)
    scale = largest_power(lambda power: diagonal * power * power < 1.0, (size, 1))
    across = as_row(scale)
    high, low = high * scale * across, low * scale * across
    identity = jnp.where(is_diagonal, 1.0, 0.0)
    first = eliminated(jnp.concatenate([high, identity], axis=1))
    inverse = first[:, size:]
    lower = turned_over(first)[:size]
    lower_digits = stacked_digits(lower * 128.0)
    missed = residual(high * 2.0**14, low * 2.0**14, lower_digits, lower_digits) * 2.0**-14
    inverse_top = jnp.max(jnp.abs(inverse), axis=1, keepdims=True)
    inverse_scale = largest_power(lambda power: inverse_top * power <= 128.0, (size, 1))
    goal = identity * (inverse_scale * 128.0)
    skew = residual(
        goal, jnp.zeros_like(goal), stacked_digits(inverse * inverse_scale), stacked_digits(first[:, :size] * 128.0)
    ) * (-1.0 / 128.0 / inverse_scale)
    near = identity + skew
    error = dot(dot(inverse, missed), inverse, ((1,), (1,))) + (dot(near, near, ((1,), (1,))) - identity)
    weight = jnp.where(
        is_diagonal, 0.5,
        jnp.where(
            lax.broadcasted_iota(jnp.int32, (size, size), 0) > lax.broadcasted_iota(jnp.int32, (size, size), 1), 1.0, 0.0
        ),
    )
    spread = jnp.sum(error * error)
    is_small = spread < 4e-4

    @pl.when(is_small)
    def _():
        y = weight * error
        for _ in range(4):
            y = weight * (error - dot(y, y, ((1,), (1,))))
        change[...] = y
        square = dot(y, y)
        change_inverse[...] = (identity - y) + dot(identity - y, square)

    @pl.when(jnp.logical_not(is_small))
    def _():
        second = eliminated_slowly(jnp.concatenate([identity + error, identity], axis=1), work)
        change[...] = turned_over(second)[:size] - identity
        change_inverse[...] = second[:, size:]

    turn = change[...] - skew
    full = lower + dot(lower, turn - dot(skew, turn))
    full = jnp.concatenate([full, jnp.zeros_like(full)], axis=1)
    factor[...] = turned_over(full)[:size] / across * (1.0 / cell_scale)
    mixing = dot(change_inverse[...], inverse) * across * cell_scale

    def stacked(cut):
        whole_part = mixing * as_row(cut[:, :1])
        pieces = []
        for _ in range(3):
            piece = whole_part.astype(jnp.bfloat16)
            whole_part = whole_part - piece.astype(jnp.float32)
            pieces.append(piece.astype(jnp.float32))
        tall = jnp.concatenate(pieces, axis=0)
        return jnp.concatenate([tall * 256.0**-a for a in range(DIGITS)], axis=1).astype(jnp.bfloat16)

    def finish(matrix, cells, first_row, count, shift):
        def four(index, carry):
            for j in range(4):
                r = 4 * index + j
                product = jnp.dot(matrix, cells[r + shift], preferred_element_type=jnp.float32)
                rows_out[r + first_row] = product[:size] + (product[size : 2 * size] + product[2 * size :])
            for j in range(4):
                at = 4 * index + j + first_row
                pltpu.make_async_copy(rows_out.at[at], basis.at[:, at, :], out_sems.at[at]).start()
            return carry

        lax.fori_loop(0, count // 4, four, 0)

    for copy in loads:
        copy.wait()
    finish(stacked(inner_scale), inner_cells, DEPTH, inner_rows, 0)
    matrix = stacked(edge_scale)
    finish(matrix, edge_cells, 0, DEPTH, 0)
    finish(matrix, edge_cells, rows - DEPTH, DEPTH, DEPTH)

    def wait(r, carry):
        pltpu.make_async_copy(rows_out.at[r], basis.at[:, r, :], out_sems.at[r]).wait()
        return carry

    lax.fori_loop(0, rows, wait, 0)


def whole(memory=pltpu.VMEM):
    return pl.BlockSpec(memory_space=memory)


def call(kernel, name, out_shape, in_specs, out_specs, scratch_shapes=(), cost=None):
    return pl.pallas_call(
        kernel,
        out_shape=out_shape,
        in_specs=in_specs,
        out_specs=out_specs,
        scratch_shapes=scratch_shapes,
        compiler_params=pltpu.CompilerParams(vmem_limit_bytes=56 * MIB),
        cost_estimate=cost,
        name=name,
    )


def summed(pairs):
    count = lax.axis_size(AXIS)
    half = pairs.shape[0] // 2

    def add(a, b):
        return jnp.concatenate(pair_sum((a[:half], a[half:]), (b[:half], b[half:])), axis=0)

    if count & (count - 1):
        total = pairs
        for step in range(1, count):
            total = add(total, lax.ppermute(pairs, AXIS, [(i, (i + step) % count) for i in range(count)]))
        return total
    distance = 1
    while distance < count:
        pairs = add(pairs, lax.ppermute(pairs, AXIS, [(i, i ^ distance) for i in range(count)]))
        distance *= 2
    return pairs


def on_device(probes, kappa, speed, friction, upwind, probe_sites):
    count, rows, columns = probes.shape
    size = lax.axis_size(AXIS)
    f32 = jnp.float32
    cell_scale = math.sqrt(rows * columns * size)
    strength = IMPULSE_GAIN * cell_scale
    shape = jax.ShapeDtypeStruct
    halo = shape((DEPTH, count + PACK, columns), f32)
    weights, to_below, to_above = call(
        pack_kernel,
        "pack",
        (shape((5, rows, columns), f32), halo, halo),
        [whole(pl.ANY), whole(), whole(), whole(), whole()],
        (whole(), whole(pl.ANY), whole(pl.ANY)),
        [pltpu.VMEM((2, DEPTH, PACK, columns), f32), pltpu.SemaphoreType.DMA((2, DEPTH + 1))],
    )(probes, kappa, speed, friction, upwind.T)
    from_above = lax.ppermute(to_below, AXIS, [(i, i + 1) for i in range(size - 1)])
    from_below = lax.ppermute(to_above, AXIS, [(i + 1, i) for i in range(size - 1)])
    edge_count = 2 * DEPTH
    inner_count = rows - edge_count
    tall = DIGITS * count

    def digit_rows(number):
        return shape((number, tall, columns), jnp.bfloat16), shape((count, 128), f32), shape((count, 2 * count), f32)

    def digit_scratch(number):
        return [
            pltpu.VMEM((number, count, columns), f32),
            pltpu.VMEM((number, tall, columns), jnp.bfloat16),
            pltpu.VMEM((tall, tall), jnp.int32),
        ]

    kept = shape((4, 2, count, columns), f32)
    field = pltpu.VMEM((rows, count, columns), f32)
    inner, inner_scale, pairs, top, bottom = call(
        functools.partial(inner_kernel, strength),
        "inner_rows",
        digit_rows(inner_count) + (kept, kept),
        [whole(pltpu.SMEM), whole(pl.ANY), whole()],
        (whole(pl.ANY), whole(), whole(), whole(), whole()),
        [field] * 4
        + digit_scratch(inner_count)
        + [pltpu.SMEM((count + 1,), jnp.int32)]
        + [pltpu.SemaphoreType.DMA((rows,)), pltpu.SemaphoreType.DMA((inner_count,))],
        pl.CostEstimate(flops=10**10, bytes_accessed=16 * MIB, transcendentals=0),
    )(probe_sites, probes, weights)
    fields = pltpu.VMEM((2 * DEPTH + 4, count, columns), f32)
    levels = pltpu.VMEM((3, DEPTH + 2, count, columns), f32)
    edge, edge_scale, pairs = call(
        functools.partial(edge_kernel, strength, rows),
        "edge_rows",
        digit_rows(edge_count),
        [whole(pltpu.SMEM)] + [whole(pl.ANY)] * 5 + [whole()],
        (whole(pl.ANY), whole(), whole()),
        [
            pltpu.VMEM((5, 8 * DEPTH, columns), f32), fields, levels, levels,
            pltpu.VMEM((2, DEPTH, PACK, columns), f32),
        ]
        + digit_scratch(edge_count)
        + [pltpu.SMEM((count + 1,), jnp.int32), pltpu.SemaphoreType.DMA((10,)), pltpu.SemaphoreType.DMA((edge_count,))],
    )(probe_sites, from_above, from_below, weights, top, bottom, pairs)
    pairs = summed(pairs)
    square = pltpu.VMEM((count, count), f32)
    return call(
        functools.partial(solve_kernel, cell_scale),
        "solve",
        (shape((count, rows, columns), f32), shape((count, count), f32)),
        [whole(), whole(), whole(), whole(pl.ANY), whole(pl.ANY)],
        (whole(pl.ANY), whole()),
        [
            pltpu.VMEM((inner_count, tall, columns), jnp.bfloat16),
            pltpu.VMEM((edge_count, tall, columns), jnp.bfloat16),
            pltpu.VMEM((rows, count, columns), f32),
            pltpu.VMEM((count, 2 * count), f32),
            square,
            square,
            pltpu.SemaphoreType.DMA((2,)),
            pltpu.SemaphoreType.DMA((rows,)),
        ],
    )(pairs, inner_scale, edge_scale, inner, edge)


def solution(mesh):
    return jax.shard_map(
        on_device,
        mesh=mesh,
        in_specs=(
            P(None, ("groups", "gx"), None),
            P(("groups", "gx"), None),
            P(("groups", "gx"), None),
            P(("groups", "gx"), None),
            P(("groups", "gx"), None),
            P("groups"),
        ),
        out_specs=(P(None, ("groups", "gx"), None), P("groups", None)),
        check_vma=False,
    )
```

```python
import functools
import math

import jax
import jax.numpy as jnp
from jax import lax
from jax.experimental import pallas as pl
from jax.experimental.pallas import tpu as pltpu
from jax.sharding import PartitionSpec as P

TIME_STEP = 0.2
IMPULSE_GAIN = 3.0
AXIS = "gx"
DEPTH = 4
PACK = 8
MIB = 1024 * 1024


def rolled(row, by):
    return pltpu.roll(row, by % row.shape[-1], row.ndim - 1)


def weight_row(weights, row, layer, like):
    return jnp.broadcast_to(weights[layer, pl.ds(row, 1), :], like)


def in_steps(first, last, body, step=6):
    whole_steps = (last - first) // step

    def several(index, carry):
        for j in range(step):
            body(first + index * step + j)
        return carry

    lax.fori_loop(0, whole_steps, several, 0)
    for r in range(first + whole_steps * step, last):
        body(r)


def sweep_row(source, at, target, to, probes, columns, center, above, below, left, right):
    for first in range(0, probes, 8):
        octet = slice(first, first + 8)
        middle = source[at, octet, :]
        target[to, octet, :] = (
            center * middle
            + above * source[at - 1, octet, :]
            + below * source[at + 1, octet, :]
            + left * rolled(middle, 1)
            + right * rolled(middle, -1)
        )


def forward_row(source, at, target, to, weights, w_at, probes, columns):
    like = (8, columns)
    sweep_row(
        source, at, target, to, probes, columns,
        *[weight_row(weights, w_at, layer, like) for layer in range(5)],
    )


def adjoint_row(source, at, target, to, weights, w_at, probes, columns):
    like = (8, columns)
    sweep_row(
        source, at, target, to, probes, columns,
        weight_row(weights, w_at, 0, like),
        weight_row(weights, w_at - 1, 2, like),
        weight_row(weights, w_at + 1, 1, like),
        rolled(weight_row(weights, w_at, 4, like), 1),
        rolled(weight_row(weights, w_at, 3, like), -1),
    )


def find_impulses(sites, found, held, probes, columns):
    def one(k, count):
        found[count] = k
        return count + held(lax.div(sites[k], columns)).astype(jnp.int32)

    return lax.fori_loop(0, probes, one, 0)


def add_impulses(sites, found, count, target, place_of, columns, strength):
    column_ids = lax.broadcasted_iota(jnp.int32, (1, columns), 1)

    def one(index, carry):
        k = found[index]
        site = sites[k]
        hit = jnp.where(column_ids == lax.rem(site, columns), strength, 0.0)
        target[place_of(lax.div(site, columns)), pl.ds(k, 1), :] += hit
        return carry

    lax.fori_loop(0, count, one, 0)


def pack_kernel(cells, kappa, speed, friction, upwind, weights, to_below, to_above, sems):
    probes, rows, columns = cells.shape
    copies = []
    for r in range(DEPTH):
        for side, target in enumerate((to_above, to_below)):
            row = r if side == 0 else rows - DEPTH + r
            copies.append(
                pltpu.make_async_copy(cells.at[:, row, :], target.at[r, pl.ds(0, probes), :], sems.at[side, r])
            )
    for copy in copies:
        copy.start()
    blocks = upwind.shape[0]
    width = columns // blocks
    spread = (
        lax.broadcasted_iota(jnp.int32, (blocks, columns), 1) // width
        == lax.broadcasted_iota(jnp.int32, (blocks, columns), 0)
    ).astype(jnp.bfloat16)
    directions = lax.dot_general(
        upwind[...].astype(jnp.float32).astype(jnp.bfloat16), spread, (((0,), (0,)), ((), ())),
        preferred_element_type=jnp.float32,
    )
    column_ids = lax.broadcasted_iota(jnp.int32, (rows, columns), 1)
    k, s = kappa[...], speed[...]
    layers = [1.0 - TIME_STEP * (4.0 * k + s + friction[...])]
    for direction in range(4):
        chosen = jnp.where(jnp.abs(directions - direction) < 0.5, s, 0.0)
        layers.append(TIME_STEP * (k + chosen))
    layers[3] = jnp.where(column_ids == 0, 0.0, layers[3])
    layers[4] = jnp.where(column_ids == columns - 1, 0.0, layers[4])
    for index, layer in enumerate(layers):
        weights[index] = layer
        for r in range(DEPTH):
            place = probes + index
            to_above[r, place : place + 1, :] = layer[r : r + 1]
            to_below[r, place : place + 1, :] = layer[rows - DEPTH + r : rows - DEPTH + r + 1]
    for side in (to_above, to_below):
        side[:, probes + 5 :, :] = jnp.zeros((DEPTH, PACK - 5, columns), jnp.float32)
    for copy in copies:
        copy.wait()


def inner_kernel(
    strength, sites, cells, weights, digits, scale, pairs, top, bottom, v, f1, f2, a1, response, sums, found, sems
):
    rows, probes, columns = v.shape
    first_row = lax.axis_index(AXIS) * rows

    copies = [pltpu.make_async_copy(cells.at[:, r, :], v.at[r], sems.at[r]) for r in range(rows)]
    for copy in copies:
        copy.start()
    hits = find_impulses(
        sites, found, lambda row: (row >= first_row) & (row < first_row + rows), probes, columns
    )
    for copy in copies:
        copy.wait()
    add_impulses(sites, found, hits, v, lambda row: row - first_row, columns, strength)

    def sweep(row_fn, source, target, first, shift=0):
        def body(r):
            row_fn(source, r, target, r - shift, weights, r, probes, columns)

        in_steps(first, rows - first, body)

    sweep(forward_row, v, f1, 1)
    sweep(forward_row, f1, f2, 2)
    sweep(adjoint_row, f2, a1, 3)
    sweep(adjoint_row, a1, response, DEPTH, DEPTH)
    for level, field in enumerate((v, f1, f2, a1)):
        for j in range(2):
            top[level, j] = field[level + j]
            bottom[level, j] = field[rows - 2 - level + j]
    high, low = gram_pair(response, rows - 2 * DEPTH, digits, scale, sums)
    pairs[...] = jnp.concatenate([folded(high), folded(low)], axis=0)


def edge_kernel(
    strength, rows, sites, above, below, weights, top, bottom, inner_pairs, digits, scale, pairs,
    w, va, la, lb, behind, response, sums, found, sems,
):
    probes, columns = top.shape[2:]
    first_row = lax.axis_index(AXIS) * rows
    start_a, start_b = 2 * DEPTH, 4 * DEPTH
    vb = va.at[DEPTH + 2 :]
    copies = [
        (above.at[:, pl.ds(probes, PACK), :], behind.at[0]),
        (below.at[:, pl.ds(probes, PACK), :], behind.at[1]),
        (weights.at[:, pl.ds(0, 8), :], w.at[:, pl.ds(start_a, 8), :]),
        (weights.at[:, pl.ds(rows - 8, 8), :], w.at[:, pl.ds(start_b, 8), :]),
        (above.at[:, pl.ds(0, probes), :], va.at[pl.ds(0, DEPTH)]),
        (below.at[:, pl.ds(0, probes), :], va.at[pl.ds(DEPTH + 4, DEPTH)]),
        (top.at[0], va.at[pl.ds(DEPTH, 2)]),
        (bottom.at[0], va.at[pl.ds(DEPTH + 2, 2)]),
        (top.at[pl.ds(1, 3)], la.at[:, pl.ds(DEPTH, 2)]),
        (bottom.at[pl.ds(1, 3)], lb.at[:, pl.ds(0, 2)]),
    ]
    copies = [pltpu.make_async_copy(source, target, sems.at[i]) for i, (source, target) in enumerate(copies)]
    for copy in copies:
        copy.start()

    def is_above(row):
        return (row >= first_row - DEPTH) & (row < first_row)

    def held(row):
        return is_above(row) | ((row >= first_row + rows) & (row < first_row + rows + DEPTH))

    hits = find_impulses(sites, found, held, probes, columns)
    for copy in copies:
        copy.wait()
    for layer in range(5):
        for r in range(DEPTH):
            w[layer, DEPTH + r : DEPTH + r + 1, :] = behind[0, r, layer : layer + 1, :]
            w[layer, start_b + 2 * DEPTH + r : start_b + 2 * DEPTH + r + 1, :] = behind[1, r, layer : layer + 1, :]
    add_impulses(
        sites, found, hits, va,
        lambda row: jnp.where(is_above(row), row - first_row + DEPTH, row - first_row - rows + DEPTH + 4), columns, strength,
    )
    chain_a = [va, la.at[0], la.at[1], la.at[2], response]
    chain_b = [vb, lb.at[0], lb.at[1], lb.at[2], response]
    for level in range(4):
        row_fn = forward_row if level < 2 else adjoint_row
        for j in range(DEPTH):
            row_fn(chain_a[level], j + 1, chain_a[level + 1], j, w, start_a + level - 3 + j, probes, columns)
            to = j + (DEPTH if level == 3 else 2)
            row_fn(chain_b[level], j + 1, chain_b[level + 1], to, w, start_b + 7 - level + j, probes, columns)
    ours = gram_pair(response, 2 * DEPTH, digits, scale, sums)
    half = probes // 2
    high, low = pair_sum(ours, (unfolded(inner_pairs[:half, :]), unfolded(inner_pairs[half:, :])))
    pairs[...] = jnp.concatenate([folded(high), folded(low)], axis=0)


DIGITS = 4
ROUNDER = 12582912.0


def rounded(value):
    return (value + ROUNDER) - ROUNDER


def digits_of(value):
    out = []
    for position in range(DIGITS):
        digit = rounded(value)
        out.append(digit)
        if position < DIGITS - 1:
            value = (value - digit) * 256.0
    return out


def largest_power(fits, like):
    power = jnp.full(like, 2.0**-63, jnp.float32)
    for step in (64, 32, 16, 8, 4, 2, 1):
        candidate = power * 2.0**step
        power = jnp.where((candidate <= 2.0**63) & fits(candidate), candidate, power)
    return power


def unit(size):
    return lax.broadcasted_iota(jnp.int32, (size, size), 0) == lax.broadcasted_iota(jnp.int32, (size, size), 1)


def as_row(column):
    size = column.shape[0]
    return jnp.sum(jnp.where(unit(size), jnp.broadcast_to(column, (size, size)), 0.0), axis=0, keepdims=True)


def pair_of(high, low):
    total = high + low
    return total, low - (total - high)


def pair_sum(a, b):
    (a_high, a_low), (b_high, b_low) = a, b
    total = a_high + b_high
    back = total - a_high
    error = (a_high - (total - back)) + (b_high - back)
    return pair_of(total, error + (a_low + b_low))


def gram_pair(field, rows, cells, scale_out, sums):
    probes, columns = field.shape[1:]

    def largest(index, so_far):
        for r in (2 * index, 2 * index + 1):
            so_far = tuple(jnp.maximum(m, jnp.abs(field[r, 8 * o : 8 * o + 8, :])) for o, m in enumerate(so_far))
        return so_far

    tops = lax.fori_loop(0, rows // 2, largest, tuple(jnp.zeros((8, columns), jnp.float32) for _ in range(probes // 8)))
    top = jnp.concatenate([jnp.max(m, axis=1, keepdims=True) for m in tops], axis=0)
    scale = largest_power(lambda power: top * power <= 128.0, (probes, 1))
    inverse = 1.0 / scale
    scale_out[...] = jnp.broadcast_to(inverse, scale_out.shape)
    sums[...] = jnp.zeros_like(sums)

    def cut(index, carry):
        for pair in range(2):
            for r in (4 * index + 2 * pair, 4 * index + 2 * pair + 1):
                parts = digits_of(field[r] * scale)
                cells[r] = jnp.concatenate([part.astype(jnp.bfloat16) for part in parts], axis=0)
        total = sums[...]
        for pair in range(2):
            r = 4 * index + 2 * pair
            two = jnp.concatenate([cells[r], cells[r + 1]], axis=1)
            product = lax.dot_general(two, two, (((1,), (1,)), ((), ())), preferred_element_type=jnp.float32)
            total = total + product.astype(jnp.int32)
        sums[...] = total
        return carry

    lax.fori_loop(0, rows // 4, cut, 0)
    places = []
    for place in range(2 * DIGITS - 1):
        terms = [
            sums[a * probes : (a + 1) * probes, (place - a) * probes : (place - a + 1) * probes]
            for a in range(DIGITS)
            if 0 <= place - a < DIGITS
        ]
        places.append(functools.reduce(lambda x, y: x + y, terms))
    for place in range(2 * DIGITS - 2, 0, -1):
        places[place - 1] = places[place - 1] + (places[place] >> 8)
        places[place] = places[place] & 255
    f32 = jnp.float32
    high = (places[0] >> 8).astype(f32) * 256.0
    middle = ((places[0] & 255) * 65536 + places[1] * 256 + places[2]).astype(f32) * 2.0**-16
    low = (places[3] * 65536 + places[4] * 256 + places[5]).astype(f32) * 2.0**-40
    total, rest = pair_of(high, middle)
    total, rest = pair_of(total, rest + low)
    across = as_row(inverse)
    return total * inverse * across, rest * inverse * across


def folded(square):
    half = square.shape[0] // 2
    return jnp.concatenate([square[:half], square[half:]], axis=1)


def unfolded(block):
    half = block.shape[1] // 2
    return jnp.concatenate([block[:, :half], block[:, half:]], axis=0)


def dot(a, b, dims=((1,), (0,))):
    return lax.dot_general(
        a, b, (dims, ((), ())), precision=lax.Precision.HIGHEST, preferred_element_type=jnp.float32
    )


def turned_over(block):
    size, wide = block.shape
    square = jnp.concatenate([block, jnp.zeros((wide - size, wide), jnp.float32)], axis=0)
    return jnp.transpose(square)[:, :size]


PANEL = 4


def eliminated(block):
    size, wide = block.shape
    count = size // 8
    groups = [block[8 * g : 8 * g + 8] for g in range(count)]
    like = (8, wide)
    below = lax.broadcasted_iota(jnp.int32, like, 0)
    for first in range(0, size, PANEL):
        g, start = divmod(first, 8)
        columns = {
            o: [jnp.broadcast_to(groups[o][:, first + t : first + t + 1], like) for t in range(PANEL)]
            for o in range(g, count)
        }
        for t in range(PANEL):
            s = start + t
            across = [jnp.broadcast_to(columns[g][u][s : s + 1], like) for u in range(t, PANEL)]
            inverse = 1.0 / across[0]
            row = jnp.broadcast_to(groups[g][s : s + 1], like) * inverse
            across = [value * inverse for value in across]
            for o in range(g, count):
                if o == g and s == 7:
                    continue
                column = columns[o][t]
                if o == g:
                    column = jnp.where(below > s, column, 0.0)
                groups[o] = groups[o] - column * row
                for u in range(t + 1, PANEL):
                    columns[o][u] = columns[o][u] - column * across[u - t]
    return normalised(jnp.concatenate(groups, axis=0))


def normalised(block):
    size, wide = block.shape
    row_ids = lax.broadcasted_iota(jnp.int32, block.shape, 0)
    lanes = lax.broadcasted_iota(jnp.int32, block.shape, 1)
    pivots = jnp.sum(jnp.where(row_ids == lanes, block, 0.0), axis=1, keepdims=True)
    scale = lax.rsqrt(pivots)
    scale = scale * (1.5 - 0.5 * pivots * scale * scale)
    block = block * scale
    keep = (lanes >= row_ids) & ((lanes < size) | (lanes - size <= row_ids))
    return jnp.where(keep, block, 0.0)


def eliminated_slowly(block, work):
    size, wide = block.shape
    work[...] = block
    row_ids = lax.broadcasted_iota(jnp.int32, (size, 1), 0)
    lanes = lax.broadcasted_iota(jnp.int32, (1, wide), 1)

    def step(j, carry):
        row = work[pl.ds(j, 1), :]
        pivot = jnp.sum(jnp.where(lanes == j, row, 0.0), axis=1, keepdims=True)
        column = jnp.sum(jnp.where(lanes == j, work[...], 0.0), axis=1, keepdims=True)
        work[...] = work[...] - jnp.where(row_ids > j, column, 0.0) * (row / pivot)
        return carry

    lax.fori_loop(0, size, step, 0)
    return normalised(work[...])


def stacked_digits(value):
    return jnp.concatenate([part.astype(jnp.bfloat16) for part in digits_of(value)], axis=0)


def residual(high, low, left, right):
    size = high.shape[0]
    product = lax.dot_general(left, right, (((1,), (1,)), ((), ())), preferred_element_type=jnp.float32)
    places = []
    for place in range(2 * DIGITS - 1):
        terms = [
            product[a * size : (a + 1) * size, (place - a) * size : (place - a + 1) * size]
            for a in range(DIGITS)
            if 0 <= place - a < DIGITS
        ]
        places.append(functools.reduce(lambda x, y: x + y, terms))
    rest = high
    total = jnp.zeros_like(high)
    for place in range(5):
        if place == 2:
            rest = rest + low * 2.0**16
        digit = rounded(rest) if place < 4 else rest
        rest = (rest - digit) * 256.0
        total = total * 256.0 + (digit - places[place])
    total = total - (places[5] * 2.0**-8 + places[6] * 2.0**-16)
    return total * 2.0**-32


def solve_kernel(
    cell_scale, pairs, inner_scale, edge_scale, inner, edge, basis, factor,
    rows_out, work, change, change_inverse, out_sems,
):
    size = pairs.shape[0]
    inner_rows, edge_rows = inner.shape[0], edge.shape[0]
    rows = inner_rows + edge_rows
    high, low = unfolded(pairs[: size // 2, :]), unfolded(pairs[size // 2 :, :])
    is_diagonal = unit(size)
    diagonal = jnp.sum(jnp.where(is_diagonal, high, 0.0), axis=1, keepdims=True)
    scale = largest_power(lambda power: diagonal * power * power < 1.0, (size, 1))
    across = as_row(scale)
    high, low = high * scale * across, low * scale * across
    identity = jnp.where(is_diagonal, 1.0, 0.0)
    first = eliminated(jnp.concatenate([high, identity], axis=1))
    inverse = first[:, size:]
    lower = turned_over(first)[:size]
    lower_digits = stacked_digits(lower * 128.0)
    missed = residual(high * 2.0**14, low * 2.0**14, lower_digits, lower_digits) * 2.0**-14
    inverse_top = jnp.max(jnp.abs(inverse), axis=1, keepdims=True)
    inverse_scale = largest_power(lambda power: inverse_top * power <= 128.0, (size, 1))
    goal = identity * (inverse_scale * 128.0)
    skew = residual(
        goal, jnp.zeros_like(goal), stacked_digits(inverse * inverse_scale), stacked_digits(first[:, :size] * 128.0)
    ) * (-1.0 / 128.0 / inverse_scale)
    near = identity + skew
    error = dot(dot(inverse, missed), inverse, ((1,), (1,))) + (dot(near, near, ((1,), (1,))) - identity)
    weight = jnp.where(
        is_diagonal, 0.5,
        jnp.where(
            lax.broadcasted_iota(jnp.int32, (size, size), 0) > lax.broadcasted_iota(jnp.int32, (size, size), 1), 1.0, 0.0
        ),
    )
    spread = jnp.sum(error * error)
    is_small = spread < 4e-4

    @pl.when(is_small)
    def _():
        y = weight * error
        for _ in range(4):
            y = weight * (error - dot(y, y, ((1,), (1,))))
        change[...] = y
        square = dot(y, y)
        change_inverse[...] = (identity - y) + dot(identity - y, square)

    @pl.when(jnp.logical_not(is_small))
    def _():
        second = eliminated_slowly(jnp.concatenate([identity + error, identity], axis=1), work)
        change[...] = turned_over(second)[:size] - identity
        change_inverse[...] = second[:, size:]

    turn = change[...] - skew
    full = lower + dot(lower, turn - dot(skew, turn))
    full = jnp.concatenate([full, jnp.zeros_like(full)], axis=1)
    factor[...] = turned_over(full)[:size] / across * (1.0 / cell_scale)
    mixing = dot(change_inverse[...], inverse) * across * cell_scale

    def stacked(cut):
        whole_part = mixing * as_row(cut[:, :1])
        pieces = []
        for _ in range(3):
            piece = whole_part.astype(jnp.bfloat16)
            whole_part = whole_part - piece.astype(jnp.float32)
            pieces.append(piece.astype(jnp.float32))
        tall = jnp.concatenate(pieces, axis=0)
        return jnp.concatenate([tall * 256.0**-a for a in range(DIGITS)], axis=1).astype(jnp.bfloat16)

    def finish(matrix, cells, first_row, count, shift):
        def four(index, carry):
            for j in range(4):
                r = 4 * index + j
                product = jnp.dot(matrix, cells[r + shift], preferred_element_type=jnp.float32)
                rows_out[r + first_row] = product[:size] + (product[size : 2 * size] + product[2 * size :])
            for j in range(4):
                at = 4 * index + j + first_row
                pltpu.make_async_copy(rows_out.at[at], basis.at[:, at, :], out_sems.at[at]).start()
            return carry

        lax.fori_loop(0, count // 4, four, 0)

    finish(stacked(inner_scale), inner, DEPTH, inner_rows, 0)
    matrix = stacked(edge_scale)
    finish(matrix, edge, 0, DEPTH, 0)
    finish(matrix, edge, rows - DEPTH, DEPTH, DEPTH)

    def wait(r, carry):
        pltpu.make_async_copy(rows_out.at[r], basis.at[:, r, :], out_sems.at[r]).wait()
        return carry

    lax.fori_loop(0, rows, wait, 0)


def whole(memory=pltpu.VMEM):
    return pl.BlockSpec(memory_space=memory)


def call(kernel, name, out_shape, in_specs, out_specs, scratch_shapes=(), cost=None, vmem=56):
    return pl.pallas_call(
        kernel,
        out_shape=out_shape,
        in_specs=in_specs,
        out_specs=out_specs,
        scratch_shapes=scratch_shapes,
        compiler_params=pltpu.CompilerParams(vmem_limit_bytes=vmem * MIB),
        cost_estimate=cost,
        name=name,
    )


def summed(pairs):
    count = lax.axis_size(AXIS)
    half = pairs.shape[0] // 2

    def add(a, b):
        return jnp.concatenate(pair_sum((a[:half], a[half:]), (b[:half], b[half:])), axis=0)

    if count & (count - 1):
        total = pairs
        for step in range(1, count):
            total = add(total, lax.ppermute(pairs, AXIS, [(i, (i + step) % count) for i in range(count)]))
        return total
    distance = 1
    while distance < count:
        pairs = add(pairs, lax.ppermute(pairs, AXIS, [(i, i ^ distance) for i in range(count)]))
        distance *= 2
    return pairs


def on_device(probes, kappa, speed, friction, upwind, probe_sites):
    count, rows, columns = probes.shape
    size = lax.axis_size(AXIS)
    f32 = jnp.float32
    cell_scale = math.sqrt(rows * columns * size)
    strength = IMPULSE_GAIN * cell_scale
    shape = jax.ShapeDtypeStruct
    halo = shape((DEPTH, count + PACK, columns), f32)
    weights, to_below, to_above = call(
        pack_kernel,
        "pack",
        (shape((5, rows, columns), f32), halo, halo),
        [whole(pl.ANY), whole(), whole(), whole(), whole()],
        (whole(), whole(), whole()),
        [pltpu.SemaphoreType.DMA((2, DEPTH))],
        vmem=56,
    )(probes, kappa, speed, friction, upwind.T)
    from_above = lax.ppermute(to_below, AXIS, [(i, i + 1) for i in range(size - 1)])
    from_below = lax.ppermute(to_above, AXIS, [(i + 1, i) for i in range(size - 1)])
    edge_count = 2 * DEPTH
    inner_count = rows - edge_count
    tall = DIGITS * count

    def digit_rows(number):
        return shape((number, tall, columns), jnp.bfloat16), shape((count, 128), f32), shape((count, 2 * count), f32)

    def digit_scratch(number):
        return [
            pltpu.VMEM((number, count, columns), f32),
            pltpu.VMEM((tall, tall), jnp.int32),
        ]

    kept = shape((4, 2, count, columns), f32)
    field = pltpu.VMEM((rows, count, columns), f32)
    inner, inner_scale, pairs, top, bottom = call(
        functools.partial(inner_kernel, strength),
        "inner_rows",
        digit_rows(inner_count) + (kept, kept),
        [whole(pltpu.SMEM), whole(pl.ANY), whole()],
        (whole(), whole(), whole(), whole(), whole()),
        [field] * 4
        + digit_scratch(inner_count)
        + [pltpu.SMEM((count + 1,), jnp.int32)]
        + [pltpu.SemaphoreType.DMA((rows,))],
        pl.CostEstimate(flops=10**10, bytes_accessed=16 * MIB, transcendentals=0),
        vmem=32,
    )(probe_sites, probes, weights)
    fields = pltpu.VMEM((2 * DEPTH + 4, count, columns), f32)
    levels = pltpu.VMEM((3, DEPTH + 2, count, columns), f32)
    edge, edge_scale, pairs = call(
        functools.partial(edge_kernel, strength, rows),
        "edge_rows",
        digit_rows(edge_count),
        [whole(pltpu.SMEM)] + [whole(pl.ANY)] * 5 + [whole()],
        (whole(), whole(), whole()),
        [
            pltpu.VMEM((5, 8 * DEPTH, columns), f32), fields, levels, levels,
            pltpu.VMEM((2, DEPTH, PACK, columns), f32),
        ]
        + digit_scratch(edge_count)
        + [pltpu.SMEM((count + 1,), jnp.int32), pltpu.SemaphoreType.DMA((10,))],
        vmem=16,
    )(probe_sites, from_above, from_below, weights, top, bottom, pairs)
    pairs = summed(pairs)
    square = pltpu.VMEM((count, count), f32)
    return call(
        functools.partial(solve_kernel, cell_scale),
        "solve",
        (shape((count, rows, columns), f32), shape((count, count), f32)),
        [whole()] * 5,
        (whole(pl.ANY), whole()),
        [
            pltpu.VMEM((rows, count, columns), f32),
            pltpu.VMEM((count, 2 * count), f32),
            square,
            square,
            pltpu.SemaphoreType.DMA((rows,)),
        ],
        vmem=24,
    )(pairs, inner_scale, edge_scale, inner, edge)


def solution(mesh):
    return jax.shard_map(
        on_device,
        mesh=mesh,
        in_specs=(
            P(None, ("groups", "gx"), None),
            P(("groups", "gx"), None),
            P(("groups", "gx"), None),
            P(("groups", "gx"), None),
            P(("groups", "gx"), None),
            P("groups"),
        ),
        out_specs=(P(None, ("groups", "gx"), None), P("groups", None)),
        check_vma=False,
    )
```

```python
import functools
import math

import jax
import jax.numpy as jnp
from jax import lax
from jax.experimental import pallas as pl
from jax.experimental.pallas import tpu as pltpu
from jax.sharding import PartitionSpec as P

TIME_STEP = 0.2
IMPULSE_GAIN = 3.0
AXIS = "gx"
DEPTH = 4
PACK = 8
MIB = 1024 * 1024


def rolled(row, by):
    return pltpu.roll(row, by % row.shape[-1], row.ndim - 1)


def weight_row(weights, row, layer, like):
    return jnp.broadcast_to(weights[layer, pl.ds(row, 1), :], like)


def in_steps(first, last, body, step=10):
    whole_steps = (last - first) // step

    def several(index, carry):
        for j in range(step):
            body(first + index * step + j)
        return carry

    lax.fori_loop(0, whole_steps, several, 0)
    for r in range(first + whole_steps * step, last):
        body(r)


def sweep_row(source, at, target, to, probes, columns, center, above, below, left, right):
    for first in range(0, probes, 8):
        octet = slice(first, first + 8)
        middle = source[at, octet, :]
        target[to, octet, :] = (
            center * middle
            + above * source[at - 1, octet, :]
            + below * source[at + 1, octet, :]
            + left * rolled(middle, 1)
            + right * rolled(middle, -1)
        )


def forward_row(source, at, target, to, weights, w_at, probes, columns):
    like = (8, columns)
    sweep_row(
        source, at, target, to, probes, columns,
        *[weight_row(weights, w_at, layer, like) for layer in range(5)],
    )


def adjoint_row(source, at, target, to, weights, w_at, probes, columns):
    like = (8, columns)
    sweep_row(
        source, at, target, to, probes, columns,
        weight_row(weights, w_at, 0, like),
        weight_row(weights, w_at - 1, 2, like),
        weight_row(weights, w_at + 1, 1, like),
        rolled(weight_row(weights, w_at, 4, like), 1),
        rolled(weight_row(weights, w_at, 3, like), -1),
    )


def find_impulses(sites, found, held, probes):
    unroll = 8

    def several(index, count):
        for j in range(unroll):
            k = index * unroll + j
            found[count] = k
            count = jnp.where(held(sites[k]), count + 1, count)
        return count

    return lax.fori_loop(0, probes // unroll, several, 0)


def row_and_column(site, columns):
    if columns & (columns - 1):
        return lax.div(site, columns), lax.rem(site, columns)
    return site >> (columns.bit_length() - 1), site & (columns - 1)


def add_impulses(sites, found, count, target, place_of, columns, strength):
    column_ids = lax.broadcasted_iota(jnp.int32, (1, columns), 1)

    def one(index, carry):
        k = found[index]
        row, column = row_and_column(sites[k], columns)
        target[place_of(row), pl.ds(k, 1), :] += jnp.where(column_ids == column, strength, 0.0)
        return carry

    lax.fori_loop(0, count, one, 0)


def weight_layers(kappa, speed, friction, upwind):
    rows, columns = kappa.shape
    blocks = upwind.shape[0]
    width = columns // blocks
    spread = (
        lax.broadcasted_iota(jnp.int32, (blocks, columns), 1) // width
        == lax.broadcasted_iota(jnp.int32, (blocks, columns), 0)
    ).astype(jnp.bfloat16)
    directions = lax.dot_general(
        upwind.astype(jnp.float32).astype(jnp.bfloat16), spread, (((0,), (0,)), ((), ())),
        preferred_element_type=jnp.float32,
    )
    column_ids = lax.broadcasted_iota(jnp.int32, (rows, columns), 1)
    layers = [1.0 - TIME_STEP * (4.0 * kappa + speed + friction)]
    for direction in range(4):
        chosen = jnp.where(jnp.abs(directions - direction) < 0.5, speed, 0.0)
        layers.append(TIME_STEP * (kappa + chosen))
    layers[3] = jnp.where(column_ids == 0, 0.0, layers[3])
    layers[4] = jnp.where(column_ids == columns - 1, 0.0, layers[4])
    return layers


def pack_kernel(cells, kappa, speed, friction, upwind, to_below, to_above, cell_rows, directions, sems, cell_sems):
    probes, rows, columns = cells.shape
    copies = []
    for r in range(DEPTH):
        for side, target in enumerate((to_above, to_below)):
            row = r if side == 0 else rows - DEPTH + r
            copies.append(
                pltpu.make_async_copy(cells.at[:, row, :], target.at[r, pl.ds(0, probes), :], sems.at[side, r])
            )
    small = [pltpu.make_async_copy(upwind, directions, cell_sems.at[3, 0])]
    for index, source in enumerate((kappa, speed, friction)):
        for side, row in enumerate((0, rows - 8)):
            small.append(
                pltpu.make_async_copy(
                    source.at[pl.ds(row, 8)], cell_rows.at[index, pl.ds(8 * side, 8)], cell_sems.at[index, side]
                )
            )
    for copy in copies + small:
        copy.start()
    for copy in small:
        copy.wait()
    ends = jnp.concatenate([directions[:, :8], directions[:, rows - 8 :]], axis=1)
    for index, layer in enumerate(weight_layers(cell_rows[0], cell_rows[1], cell_rows[2], ends)):
        place = probes + index
        for r in range(DEPTH):
            to_above[r, place : place + 1, :] = layer[r : r + 1]
            to_below[r, place : place + 1, :] = layer[16 - DEPTH + r : 16 - DEPTH + r + 1]
    for side in (to_above, to_below):
        side[:, probes + 5 :, :] = jnp.zeros((DEPTH, PACK - 5, columns), jnp.float32)
    for copy in copies:
        copy.wait()


def inner_kernel(
    strength, sites, cells, kappa, speed, friction, upwind, digits, scale, pairs, top, bottom, weights, v, f1, f2, a1, response, sums, found, sems
):
    rows, probes, columns = v.shape
    first_row = lax.axis_index(AXIS) * rows

    copies = [pltpu.make_async_copy(cells.at[:, r, :], v.at[r], sems.at[r]) for r in range(rows)]
    for copy in copies:
        copy.start()
    for index, layer in enumerate(weight_layers(kappa[...], speed[...], friction[...], upwind[...])):
        weights[index] = layer
    first_cell, end_cell = first_row * columns, (first_row + rows) * columns
    hits = find_impulses(sites, found, lambda site: (site >= first_cell) & (site < end_cell), probes)
    for copy in copies:
        copy.wait()
    add_impulses(sites, found, hits, v, lambda row: row - first_row, columns, strength)

    def sweep(row_fn, source, target, first, shift=0):
        def body(r):
            row_fn(source, r, target, r - shift, weights, r, probes, columns)

        in_steps(first, rows - first, body)

    sweep(forward_row, v, f1, 1)
    sweep(forward_row, f1, f2, 2)
    sweep(adjoint_row, f2, a1, 3)
    sweep(adjoint_row, a1, response, DEPTH, DEPTH)
    for level, field in enumerate((v, f1, f2, a1)):
        for j in range(2):
            top[level, j] = field[level + j]
            bottom[level, j] = field[rows - 2 - level + j]
    high, low = gram_pair(response, rows - 2 * DEPTH, digits, scale, sums)
    pairs[...] = jnp.concatenate([folded(high), folded(low)], axis=0)


def edge_kernel(
    strength, rows, sites, above, below, weights, top, bottom, inner_pairs, digits, scale, pairs,
    w, va, la, lb, behind, response, sums, found, sems,
):
    probes, columns = top.shape[2:]
    first_row = lax.axis_index(AXIS) * rows
    start_a, start_b = 2 * DEPTH, 4 * DEPTH
    vb = va.at[DEPTH + 2 :]
    copies = [
        (above.at[:, pl.ds(probes, PACK), :], behind.at[0]),
        (below.at[:, pl.ds(probes, PACK), :], behind.at[1]),
        (weights.at[:, pl.ds(0, 8), :], w.at[:, pl.ds(start_a, 8), :]),
        (weights.at[:, pl.ds(rows - 8, 8), :], w.at[:, pl.ds(start_b, 8), :]),
        (above.at[:, pl.ds(0, probes), :], va.at[pl.ds(0, DEPTH)]),
        (below.at[:, pl.ds(0, probes), :], va.at[pl.ds(DEPTH + 4, DEPTH)]),
        (top.at[0], va.at[pl.ds(DEPTH, 2)]),
        (bottom.at[0], va.at[pl.ds(DEPTH + 2, 2)]),
        (top.at[pl.ds(1, 3)], la.at[:, pl.ds(DEPTH, 2)]),
        (bottom.at[pl.ds(1, 3)], lb.at[:, pl.ds(0, 2)]),
    ]
    copies = [pltpu.make_async_copy(source, target, sems.at[i]) for i, (source, target) in enumerate(copies)]
    for copy in copies:
        copy.start()

    cells = rows * columns
    first_cell = first_row * columns

    def held(site):
        near = site - first_cell
        is_above = (near >= -DEPTH * columns) & (near < 0)
        return is_above | ((near >= cells) & (near < cells + DEPTH * columns))

    hits = find_impulses(sites, found, held, probes)
    for copy in copies:
        copy.wait()
    for layer in range(5):
        for r in range(DEPTH):
            w[layer, DEPTH + r : DEPTH + r + 1, :] = behind[0, r, layer : layer + 1, :]
            w[layer, start_b + 2 * DEPTH + r : start_b + 2 * DEPTH + r + 1, :] = behind[1, r, layer : layer + 1, :]
    add_impulses(
        sites, found, hits, va,
        lambda row: jnp.where(row < first_row, row - first_row + DEPTH, row - first_row - rows + DEPTH + 4), columns, strength,
    )
    chain_a = [va, la.at[0], la.at[1], la.at[2], response]
    chain_b = [vb, lb.at[0], lb.at[1], lb.at[2], response]
    for level in range(4):
        row_fn = forward_row if level < 2 else adjoint_row
        for j in range(DEPTH):
            row_fn(chain_a[level], j + 1, chain_a[level + 1], j, w, start_a + level - 3 + j, probes, columns)
            to = j + (DEPTH if level == 3 else 2)
            row_fn(chain_b[level], j + 1, chain_b[level + 1], to, w, start_b + 7 - level + j, probes, columns)
    ours = gram_pair(response, 2 * DEPTH, digits, scale, sums)
    half = probes // 2
    high, low = pair_sum(ours, (unfolded(inner_pairs[:half, :]), unfolded(inner_pairs[half:, :])))
    pairs[...] = jnp.concatenate([folded(high), folded(low)], axis=0)


DIGITS = 4
ROUNDER = 12582912.0


def rounded(value):
    return (value + ROUNDER) - ROUNDER


def digits_of(value):
    out = []
    for position in range(DIGITS):
        digit = rounded(value)
        out.append(digit)
        if position < DIGITS - 1:
            value = (value - digit) * 256.0
    return out


def largest_power(fits, like):
    power = jnp.full(like, 2.0**-63, jnp.float32)
    for step in (64, 32, 16, 8, 4, 2, 1):
        candidate = power * 2.0**step
        power = jnp.where((candidate <= 2.0**63) & fits(candidate), candidate, power)
    return power


def unit(size):
    return lax.broadcasted_iota(jnp.int32, (size, size), 0) == lax.broadcasted_iota(jnp.int32, (size, size), 1)


def as_row(column):
    size = column.shape[0]
    return jnp.sum(jnp.where(unit(size), jnp.broadcast_to(column, (size, size)), 0.0), axis=0, keepdims=True)


def pair_of(high, low):
    total = high + low
    return total, low - (total - high)


def pair_sum(a, b):
    (a_high, a_low), (b_high, b_low) = a, b
    total = a_high + b_high
    back = total - a_high
    error = (a_high - (total - back)) + (b_high - back)
    return pair_of(total, error + (a_low + b_low))


def gram_pair(field, rows, cells, scale_out, sums):
    probes, columns = field.shape[1:]

    def largest(index, so_far):
        for r in (2 * index, 2 * index + 1):
            so_far = tuple(jnp.maximum(m, jnp.abs(field[r, 8 * o : 8 * o + 8, :])) for o, m in enumerate(so_far))
        return so_far

    tops = lax.fori_loop(0, rows // 2, largest, tuple(jnp.zeros((8, columns), jnp.float32) for _ in range(probes // 8)))
    top = jnp.concatenate([jnp.max(m, axis=1, keepdims=True) for m in tops], axis=0)
    scale = largest_power(lambda power: top * power <= 128.0, (probes, 1))
    inverse = 1.0 / scale
    scale_out[...] = jnp.broadcast_to(inverse, scale_out.shape)
    sums[...] = jnp.zeros_like(sums)

    def cut(index, carry):
        for pair in range(2):
            for r in (4 * index + 2 * pair, 4 * index + 2 * pair + 1):
                parts = digits_of(field[r] * scale)
                cells[r] = jnp.concatenate([part.astype(jnp.bfloat16) for part in parts], axis=0)
        total = sums[...]
        for pair in range(2):
            r = 4 * index + 2 * pair
            two = jnp.concatenate([cells[r], cells[r + 1]], axis=1)
            product = lax.dot_general(two, two, (((1,), (1,)), ((), ())), preferred_element_type=jnp.float32)
            total = total + product.astype(jnp.int32)
        sums[...] = total
        return carry

    lax.fori_loop(0, rows // 4, cut, 0)
    places = []
    for place in range(2 * DIGITS - 1):
        terms = [
            sums[a * probes : (a + 1) * probes, (place - a) * probes : (place - a + 1) * probes]
            for a in range(DIGITS)
            if 0 <= place - a < DIGITS
        ]
        places.append(functools.reduce(lambda x, y: x + y, terms))
    for place in range(2 * DIGITS - 2, 0, -1):
        places[place - 1] = places[place - 1] + (places[place] >> 8)
        places[place] = places[place] & 255
    f32 = jnp.float32
    high = (places[0] >> 8).astype(f32) * 256.0
    middle = ((places[0] & 255) * 65536 + places[1] * 256 + places[2]).astype(f32) * 2.0**-16
    low = (places[3] * 65536 + places[4] * 256 + places[5]).astype(f32) * 2.0**-40
    total, rest = pair_of(high, middle)
    total, rest = pair_of(total, rest + low)
    across = as_row(inverse)
    return total * inverse * across, rest * inverse * across


def folded(square):
    half = square.shape[0] // 2
    return jnp.concatenate([square[:half], square[half:]], axis=1)


def unfolded(block):
    half = block.shape[1] // 2
    return jnp.concatenate([block[:, :half], block[:, half:]], axis=0)


def dot(a, b, dims=((1,), (0,))):
    return lax.dot_general(
        a, b, (dims, ((), ())), precision=lax.Precision.HIGHEST, preferred_element_type=jnp.float32
    )


def turned_over(block):
    size, wide = block.shape
    square = jnp.concatenate([block, jnp.zeros((wide - size, wide), jnp.float32)], axis=0)
    return jnp.transpose(square)[:, :size]


PANEL = 4


def eliminated(block):
    size, wide = block.shape
    count = size // 8
    groups = [block[8 * g : 8 * g + 8] for g in range(count)]
    like = (8, wide)
    below = lax.broadcasted_iota(jnp.int32, like, 0)
    for first in range(0, size, PANEL):
        g, start = divmod(first, 8)
        columns = {
            o: [jnp.broadcast_to(groups[o][:, first + t : first + t + 1], like) for t in range(PANEL)]
            for o in range(g, count)
        }
        for t in range(PANEL):
            s = start + t
            across = [jnp.broadcast_to(columns[g][u][s : s + 1], like) for u in range(t, PANEL)]
            inverse = 1.0 / across[0]
            row = jnp.broadcast_to(groups[g][s : s + 1], like) * inverse
            across = [value * inverse for value in across]
            for o in range(g, count):
                if o == g and s == 7:
                    continue
                column = columns[o][t]
                if o == g:
                    column = jnp.where(below > s, column, 0.0)
                groups[o] = groups[o] - column * row
                for u in range(t + 1, PANEL):
                    columns[o][u] = columns[o][u] - column * across[u - t]
    return normalised(jnp.concatenate(groups, axis=0))


def normalised(block):
    size, wide = block.shape
    row_ids = lax.broadcasted_iota(jnp.int32, block.shape, 0)
    lanes = lax.broadcasted_iota(jnp.int32, block.shape, 1)
    pivots = jnp.sum(jnp.where(row_ids == lanes, block, 0.0), axis=1, keepdims=True)
    scale = lax.rsqrt(pivots)
    scale = scale * (1.5 - 0.5 * pivots * scale * scale)
    block = block * scale
    keep = (lanes >= row_ids) & ((lanes < size) | (lanes - size <= row_ids))
    return jnp.where(keep, block, 0.0)


def eliminated_slowly(block, work):
    size, wide = block.shape
    work[...] = block
    row_ids = lax.broadcasted_iota(jnp.int32, (size, 1), 0)
    lanes = lax.broadcasted_iota(jnp.int32, (1, wide), 1)

    def step(j, carry):
        row = work[pl.ds(j, 1), :]
        pivot = jnp.sum(jnp.where(lanes == j, row, 0.0), axis=1, keepdims=True)
        column = jnp.sum(jnp.where(lanes == j, work[...], 0.0), axis=1, keepdims=True)
        work[...] = work[...] - jnp.where(row_ids > j, column, 0.0) * (row / pivot)
        return carry

    lax.fori_loop(0, size, step, 0)
    return normalised(work[...])


def stacked_digits(value):
    return jnp.concatenate([part.astype(jnp.bfloat16) for part in digits_of(value)], axis=0)


def residual(high, low, left, right):
    size = high.shape[0]
    product = lax.dot_general(left, right, (((1,), (1,)), ((), ())), preferred_element_type=jnp.float32)
    places = []
    for place in range(2 * DIGITS - 1):
        terms = [
            product[a * size : (a + 1) * size, (place - a) * size : (place - a + 1) * size]
            for a in range(DIGITS)
            if 0 <= place - a < DIGITS
        ]
        places.append(functools.reduce(lambda x, y: x + y, terms))
    rest = high
    total = jnp.zeros_like(high)
    for place in range(5):
        if place == 2:
            rest = rest + low * 2.0**16
        digit = rounded(rest) if place < 4 else rest
        rest = (rest - digit) * 256.0
        total = total * 256.0 + (digit - places[place])
    total = total - (places[5] * 2.0**-8 + places[6] * 2.0**-16)
    return total * 2.0**-32


def solve_kernel(
    cell_scale, pairs, inner_scale, edge_scale, inner, edge, basis, factor,
    rows_out, work, change, change_inverse, out_sems,
):
    size = pairs.shape[0]
    inner_rows, edge_rows = inner.shape[0], edge.shape[0]
    rows = inner_rows + edge_rows
    high, low = unfolded(pairs[: size // 2, :]), unfolded(pairs[size // 2 :, :])
    is_diagonal = unit(size)
    diagonal = jnp.sum(jnp.where(is_diagonal, high, 0.0), axis=1, keepdims=True)
    scale = largest_power(lambda power: diagonal * power * power < 1.0, (size, 1))
    across = as_row(scale)
    high, low = high * scale * across, low * scale * across
    identity = jnp.where(is_diagonal, 1.0, 0.0)
    first = eliminated(jnp.concatenate([high, identity], axis=1))
    inverse = first[:, size:]
    lower = turned_over(first)[:size]
    lower_digits = stacked_digits(lower * 128.0)
    missed = residual(high * 2.0**14, low * 2.0**14, lower_digits, lower_digits) * 2.0**-14
    inverse_top = jnp.max(jnp.abs(inverse), axis=1, keepdims=True)
    inverse_scale = largest_power(lambda power: inverse_top * power <= 128.0, (size, 1))
    goal = identity * (inverse_scale * 128.0)
    skew = residual(
        goal, jnp.zeros_like(goal), stacked_digits(inverse * inverse_scale), stacked_digits(first[:, :size] * 128.0)
    ) * (-1.0 / 128.0 / inverse_scale)
    near = identity + skew
    error = dot(dot(inverse, missed), inverse, ((1,), (1,))) + (dot(near, near, ((1,), (1,))) - identity)
    weight = jnp.where(
        is_diagonal, 0.5,
        jnp.where(
            lax.broadcasted_iota(jnp.int32, (size, size), 0) > lax.broadcasted_iota(jnp.int32, (size, size), 1), 1.0, 0.0
        ),
    )
    spread = jnp.sum(error * error)
    is_small = spread < 4e-4

    @pl.when(is_small)
    def _():
        y = weight * error
        for _ in range(4):
            y = weight * (error - dot(y, y, ((1,), (1,))))
        change[...] = y
        square = dot(y, y)
        change_inverse[...] = (identity - y) + dot(identity - y, square)

    @pl.when(jnp.logical_not(is_small))
    def _():
        second = eliminated_slowly(jnp.concatenate([identity + error, identity], axis=1), work)
        change[...] = turned_over(second)[:size] - identity
        change_inverse[...] = second[:, size:]

    turn = change[...] - skew
    full = lower + dot(lower, turn - dot(skew, turn))
    full = jnp.concatenate([full, jnp.zeros_like(full)], axis=1)
    factor[...] = turned_over(full)[:size] / across * (1.0 / cell_scale)
    mixing = dot(change_inverse[...], inverse) * across * cell_scale

    def stacked(cut):
        whole_part = mixing * as_row(cut[:, :1])
        pieces = []
        for _ in range(3):
            piece = whole_part.astype(jnp.bfloat16)
            whole_part = whole_part - piece.astype(jnp.float32)
            pieces.append(piece.astype(jnp.float32))
        tall = jnp.concatenate(pieces, axis=0)
        return jnp.concatenate([tall * 256.0**-a for a in range(DIGITS)], axis=1).astype(jnp.bfloat16)

    def finish(matrix, cells, first_row, count, shift):
        def four(index, carry):
            for j in range(4):
                r = 4 * index + j
                product = jnp.dot(matrix, cells[r + shift], preferred_element_type=jnp.float32)
                rows_out[r + first_row] = product[:size] + (product[size : 2 * size] + product[2 * size :])
            for j in range(4):
                at = 4 * index + j + first_row
                pltpu.make_async_copy(rows_out.at[at], basis.at[:, at, :], out_sems.at[at]).start()
            return carry

        lax.fori_loop(0, count // 4, four, 0)

    finish(stacked(inner_scale), inner, DEPTH, inner_rows, 0)
    matrix = stacked(edge_scale)
    finish(matrix, edge, 0, DEPTH, 0)
    finish(matrix, edge, rows - DEPTH, DEPTH, DEPTH)

    def wait(r, carry):
        pltpu.make_async_copy(rows_out.at[r], basis.at[:, r, :], out_sems.at[r]).wait()
        return carry

    lax.fori_loop(0, rows, wait, 0)


def whole(memory=pltpu.VMEM):
    return pl.BlockSpec(memory_space=memory)


def call(kernel, name, out_shape, in_specs, out_specs, scratch_shapes=(), cost=None, vmem=56):
    return pl.pallas_call(
        kernel,
        out_shape=out_shape,
        in_specs=in_specs,
        out_specs=out_specs,
        scratch_shapes=scratch_shapes,
        compiler_params=pltpu.CompilerParams(vmem_limit_bytes=vmem * MIB),
        cost_estimate=cost,
        name=name,
    )


def summed(pairs):
    count = lax.axis_size(AXIS)
    half = pairs.shape[0] // 2

    def add(a, b):
        return jnp.concatenate(pair_sum((a[:half], a[half:]), (b[:half], b[half:])), axis=0)

    if count & (count - 1):
        total = pairs
        for step in range(1, count):
            total = add(total, lax.ppermute(pairs, AXIS, [(i, (i + step) % count) for i in range(count)]))
        return total
    distance = 1
    while distance < count:
        pairs = add(pairs, lax.ppermute(pairs, AXIS, [(i, i ^ distance) for i in range(count)]))
        distance *= 2
    return pairs


def on_device(probes, kappa, speed, friction, upwind, probe_sites):
    count, rows, columns = probes.shape
    size = lax.axis_size(AXIS)
    f32 = jnp.float32
    cell_scale = math.sqrt(rows * columns * size)
    strength = IMPULSE_GAIN * cell_scale
    shape = jax.ShapeDtypeStruct
    halo = shape((DEPTH, count + PACK, columns), f32)
    to_below, to_above = call(
        pack_kernel,
        "pack",
        (halo, halo),
        [whole(pl.ANY)] * 5,
        (whole(), whole()),
        [
            pltpu.VMEM((3, 16, columns), f32),
            pltpu.VMEM(upwind.shape[::-1], jnp.int32),
            pltpu.SemaphoreType.DMA((2, DEPTH)),
            pltpu.SemaphoreType.DMA((4, 2)),
        ],
        vmem=56,
    )(probes, kappa, speed, friction, upwind.T)
    from_above = lax.ppermute(to_below, AXIS, [(i, i + 1) for i in range(size - 1)])
    from_below = lax.ppermute(to_above, AXIS, [(i + 1, i) for i in range(size - 1)])
    edge_count = 2 * DEPTH
    inner_count = rows - edge_count
    tall = DIGITS * count

    def digit_rows(number):
        return shape((number, tall, columns), jnp.bfloat16), shape((count, 128), f32), shape((count, 2 * count), f32)

    def digit_scratch(number):
        return [
            pltpu.VMEM((number, count, columns), f32),
            pltpu.VMEM((tall, tall), jnp.int32),
        ]

    kept = shape((4, 2, count, columns), f32)
    field = pltpu.VMEM((rows, count, columns), f32)
    inner, inner_scale, pairs, top, bottom, weights = call(
        functools.partial(inner_kernel, strength),
        "inner_rows",
        digit_rows(inner_count) + (kept, kept, shape((5, rows, columns), f32)),
        [whole(pltpu.SMEM), whole(pl.ANY)] + [whole()] * 4,
        (whole(),) * 6,
        [field] * 4
        + digit_scratch(inner_count)
        + [pltpu.SMEM((count + 1,), jnp.int32)]
        + [pltpu.SemaphoreType.DMA((rows,))],
        pl.CostEstimate(flops=10**10, bytes_accessed=16 * MIB, transcendentals=0),
        vmem=32,
    )(probe_sites, probes, kappa, speed, friction, upwind.T)
    fields = pltpu.VMEM((2 * DEPTH + 4, count, columns), f32)
    levels = pltpu.VMEM((3, DEPTH + 2, count, columns), f32)
    edge, edge_scale, pairs = call(
        functools.partial(edge_kernel, strength, rows),
        "edge_rows",
        digit_rows(edge_count),
        [whole(pltpu.SMEM)] + [whole(pl.ANY)] * 5 + [whole()],
        (whole(), whole(), whole()),
        [
            pltpu.VMEM((5, 8 * DEPTH, columns), f32), fields, levels, levels,
            pltpu.VMEM((2, DEPTH, PACK, columns), f32),
        ]
        + digit_scratch(edge_count)
        + [pltpu.SMEM((count + 1,), jnp.int32), pltpu.SemaphoreType.DMA((10,))],
        vmem=16,
    )(probe_sites, from_above, from_below, weights, top, bottom, pairs)
    pairs = summed(pairs)
    square = pltpu.VMEM((count, count), f32)
    return call(
        functools.partial(solve_kernel, cell_scale),
        "solve",
        (shape((count, rows, columns), f32), shape((count, count), f32)),
        [whole()] * 5,
        (whole(pl.ANY), whole()),
        [
            pltpu.VMEM((rows, count, columns), f32),
            pltpu.VMEM((count, 2 * count), f32),
            square,
            square,
            pltpu.SemaphoreType.DMA((rows,)),
        ],
        vmem=24,
    )(pairs, inner_scale, edge_scale, inner, edge)


def solution(mesh):
    return jax.shard_map(
        on_device,
        mesh=mesh,
        in_specs=(
            P(None, ("groups", "gx"), None),
            P(("groups", "gx"), None),
            P(("groups", "gx"), None),
            P(("groups", "gx"), None),
            P(("groups", "gx"), None),
            P("groups"),
        ),
        out_specs=(P(None, ("groups", "gx"), None), P("groups", None)),
        check_vma=False,
    )
```

```python
import functools
import math

import jax
import jax.numpy as jnp
from jax import lax
from jax.experimental import pallas as pl
from jax.experimental.pallas import tpu as pltpu
from jax.sharding import PartitionSpec as P

TIME_STEP = 0.2
IMPULSE_GAIN = 3.0
AXIS = "gx"
DEPTH = 4
ARRIVALS = 11
PACK = 8
MIB = 1024 * 1024


def rolled(row, by):
    return pltpu.roll(row, by % row.shape[-1], row.ndim - 1)


def weight_row(weights, row, layer, like):
    return jnp.broadcast_to(weights[layer, pl.ds(row, 1), :], like)


def in_steps(first, last, body, step=10):
    whole_steps = (last - first) // step

    def several(index, carry):
        for j in range(step):
            body(first + index * step + j)
        return carry

    lax.fori_loop(0, whole_steps, several, 0)
    for r in range(first + whole_steps * step, last):
        body(r)


def sweep_row(source, at, target, to, probes, columns, center, above, below, left, right):
    for first in range(0, probes, 8):
        octet = slice(first, first + 8)
        middle = source[at, octet, :]
        target[to, octet, :] = (
            center * middle
            + above * source[at - 1, octet, :]
            + below * source[at + 1, octet, :]
            + left * rolled(middle, 1)
            + right * rolled(middle, -1)
        )


def forward_row(source, at, target, to, weights, w_at, probes, columns):
    like = (8, columns)
    sweep_row(
        source, at, target, to, probes, columns,
        *[weight_row(weights, w_at, layer, like) for layer in range(5)],
    )


def adjoint_row(source, at, target, to, weights, w_at, probes, columns):
    like = (8, columns)
    sweep_row(
        source, at, target, to, probes, columns,
        weight_row(weights, w_at, 0, like),
        weight_row(weights, w_at - 1, 2, like),
        weight_row(weights, w_at + 1, 1, like),
        weight_row(weights, w_at, 5, like),
        weight_row(weights, w_at, 6, like),
    )


def find_impulses(sites, found, held, probes):
    unroll = 8

    def several(index, count):
        for j in range(unroll):
            k = index * unroll + j
            found[count] = k
            count = jnp.where(held(sites[k]), count + 1, count)
        return count

    return lax.fori_loop(0, probes // unroll, several, 0)


def row_and_column(site, columns):
    if columns & (columns - 1):
        return lax.div(site, columns), lax.rem(site, columns)
    return site >> (columns.bit_length() - 1), site & (columns - 1)


def add_impulses(sites, found, count, target, place_of, columns, strength, wanted=None):
    column_ids = lax.broadcasted_iota(jnp.int32, (1, columns), 1)

    def one(index, carry):
        k = found[index]
        row, column = row_and_column(sites[k], columns)

        def add():
            target[place_of(row), pl.ds(k, 1), :] += jnp.where(column_ids == column, strength, 0.0)

        if wanted is None:
            add()
        else:
            pl.when(wanted(row))(add)
        return carry

    lax.fori_loop(0, count, one, 0)


def weight_layers(kappa, speed, friction, upwind):
    rows, columns = kappa.shape
    blocks = upwind.shape[0]
    width = columns // blocks
    spread = (
        lax.broadcasted_iota(jnp.int32, (blocks, columns), 1) // width
        == lax.broadcasted_iota(jnp.int32, (blocks, columns), 0)
    ).astype(jnp.bfloat16)
    directions = lax.dot_general(
        upwind.astype(jnp.float32).astype(jnp.bfloat16), spread, (((0,), (0,)), ((), ())),
        preferred_element_type=jnp.float32,
    )
    column_ids = lax.broadcasted_iota(jnp.int32, (rows, columns), 1)
    layers = [1.0 - TIME_STEP * (4.0 * kappa + speed + friction)]
    for direction in range(4):
        chosen = jnp.where(jnp.abs(directions - direction) < 0.5, speed, 0.0)
        layers.append(TIME_STEP * (kappa + chosen))
    layers[3] = jnp.where(column_ids == 0, 0.0, layers[3])
    layers[4] = jnp.where(column_ids == columns - 1, 0.0, layers[4])
    return layers


def turn_weights(weights):
    weights[5] = rolled(weights[4], 1)
    weights[6] = rolled(weights[3], -1)


def pack_kernel(cells, kappa, speed, friction, upwind, to_below, to_above, cell_rows, directions, sems, cell_sems):
    probes, rows, columns = cells.shape
    copies = []
    for r in range(DEPTH):
        for side, target in enumerate((to_above, to_below)):
            row = r if side == 0 else rows - DEPTH + r
            copies.append(
                pltpu.make_async_copy(cells.at[:, row, :], target.at[r, pl.ds(0, probes), :], sems.at[side, r])
            )
    small = [pltpu.make_async_copy(upwind, directions, cell_sems.at[3, 0])]
    for index, source in enumerate((kappa, speed, friction)):
        for side, row in enumerate((0, rows - 8)):
            small.append(
                pltpu.make_async_copy(
                    source.at[pl.ds(row, 8)], cell_rows.at[index, pl.ds(8 * side, 8)], cell_sems.at[index, side]
                )
            )
    for copy in copies + small:
        copy.start()
    for copy in small:
        copy.wait()
    ends = jnp.concatenate([directions[:, :8], directions[:, rows - 8 :]], axis=1)
    for index, layer in enumerate(weight_layers(cell_rows[0], cell_rows[1], cell_rows[2], ends)):
        place = probes + index
        for r in range(DEPTH):
            to_above[r, place : place + 1, :] = layer[r : r + 1]
            to_below[r, place : place + 1, :] = layer[16 - DEPTH + r : 16 - DEPTH + r + 1]
    for side in (to_above, to_below):
        side[:, probes + 5 :, :] = jnp.zeros((DEPTH, PACK - 5, columns), jnp.float32)
    for copy in copies:
        copy.wait()


def inner_kernel(
    strength, sites, cells, kappa, speed, friction, upwind, digits, scale, pairs, top, bottom, weights, v, f1, f2, a1, response, sums, found, sems
):
    rows, probes, columns = v.shape
    first_row = lax.axis_index(AXIS) * rows

    copies = [pltpu.make_async_copy(cells.at[:, r, :], v.at[r], sems.at[r]) for r in range(rows)]
    for copy in copies[:ARRIVALS]:
        copy.start()
    for index, layer in enumerate(weight_layers(kappa[...], speed[...], friction[...], upwind[...])):
        weights[index] = layer
    turn_weights(weights)
    first_cell, end_cell = first_row * columns, (first_row + rows) * columns
    hits = find_impulses(sites, found, lambda site: (site >= first_cell) & (site < end_cell), probes)
    def forward_first(r):
        forward_row(v, r, f1, r, weights, r, probes, columns)

    ready, done = 0, 1
    while ready < rows:
        upto = min(rows, ready + ARRIVALS)
        for copy in copies[upto : upto + ARRIVALS]:
            copy.start()
        for copy in copies[ready:upto]:
            copy.wait()
        low, high = first_row + ready, first_row + upto
        add_impulses(
            sites, found, hits, v, lambda row: row - first_row, columns, strength,
            lambda row, low=low, high=high: (row >= low) & (row < high),
        )
        in_steps(done, upto - 1, forward_first)
        ready, done = upto, upto - 1

    def sweep(row_fn, source, target, first, shift=0):
        def body(r):
            row_fn(source, r, target, r - shift, weights, r, probes, columns)

        in_steps(first, rows - first, body)

    sweep(forward_row, f1, f2, 2)
    sweep(adjoint_row, f2, a1, 3)
    sweep(adjoint_row, a1, response, DEPTH, DEPTH)
    for level, field in enumerate((v, f1, f2, a1)):
        for j in range(2):
            top[level, j] = field[level + j]
            bottom[level, j] = field[rows - 2 - level + j]
    high, low = gram_pair(response, rows - 2 * DEPTH, digits, scale, sums)
    pairs[...] = jnp.concatenate([folded(high), folded(low)], axis=0)


def edge_kernel(
    strength, rows, sites, above, below, weights, top, bottom, inner_pairs, digits, scale, pairs,
    w, va, la, lb, behind, response, sums, found, sems,
):
    probes, columns = top.shape[2:]
    first_row = lax.axis_index(AXIS) * rows
    start_a, start_b = 2 * DEPTH, 4 * DEPTH
    vb = va.at[DEPTH + 2 :]
    copies = [
        (above.at[:, pl.ds(probes, PACK), :], behind.at[0]),
        (below.at[:, pl.ds(probes, PACK), :], behind.at[1]),
        (weights.at[pl.ds(0, 5), pl.ds(0, 8), :], w.at[pl.ds(0, 5), pl.ds(start_a, 8), :]),
        (weights.at[pl.ds(0, 5), pl.ds(rows - 8, 8), :], w.at[pl.ds(0, 5), pl.ds(start_b, 8), :]),
        (above.at[:, pl.ds(0, probes), :], va.at[pl.ds(0, DEPTH)]),
        (below.at[:, pl.ds(0, probes), :], va.at[pl.ds(DEPTH + 4, DEPTH)]),
        (top.at[0], va.at[pl.ds(DEPTH, 2)]),
        (bottom.at[0], va.at[pl.ds(DEPTH + 2, 2)]),
        (top.at[pl.ds(1, 3)], la.at[:, pl.ds(DEPTH, 2)]),
        (bottom.at[pl.ds(1, 3)], lb.at[:, pl.ds(0, 2)]),
    ]
    copies = [pltpu.make_async_copy(source, target, sems.at[i]) for i, (source, target) in enumerate(copies)]
    for copy in copies:
        copy.start()

    cells = rows * columns
    first_cell = first_row * columns

    def held(site):
        near = site - first_cell
        is_above = (near >= -DEPTH * columns) & (near < 0)
        return is_above | ((near >= cells) & (near < cells + DEPTH * columns))

    hits = find_impulses(sites, found, held, probes)
    for copy in copies:
        copy.wait()
    for layer in range(5):
        for r in range(DEPTH):
            w[layer, DEPTH + r : DEPTH + r + 1, :] = behind[0, r, layer : layer + 1, :]
            w[layer, start_b + 2 * DEPTH + r : start_b + 2 * DEPTH + r + 1, :] = behind[1, r, layer : layer + 1, :]
    turn_weights(w)
    add_impulses(
        sites, found, hits, va,
        lambda row: jnp.where(row < first_row, row - first_row + DEPTH, row - first_row - rows + DEPTH + 4), columns, strength,
    )
    chain_a = [va, la.at[0], la.at[1], la.at[2], response]
    chain_b = [vb, lb.at[0], lb.at[1], lb.at[2], response]
    for level in range(4):
        row_fn = forward_row if level < 2 else adjoint_row
        for j in range(DEPTH):
            row_fn(chain_a[level], j + 1, chain_a[level + 1], j, w, start_a + level - 3 + j, probes, columns)
            to = j + (DEPTH if level == 3 else 2)
            row_fn(chain_b[level], j + 1, chain_b[level + 1], to, w, start_b + 7 - level + j, probes, columns)
    ours = gram_pair(response, 2 * DEPTH, digits, scale, sums)
    half = probes // 2
    high, low = pair_sum(ours, (unfolded(inner_pairs[:half, :]), unfolded(inner_pairs[half:, :])))
    pairs[...] = jnp.concatenate([folded(high), folded(low)], axis=0)


DIGITS = 4
ROUNDER = 12582912.0


def rounded(value):
    return (value + ROUNDER) - ROUNDER


def digits_of(value):
    out = []
    for position in range(DIGITS):
        digit = rounded(value)
        out.append(digit)
        if position < DIGITS - 1:
            value = (value - digit) * 256.0
    return out


def largest_power(fits, like):
    power = jnp.full(like, 2.0**-63, jnp.float32)
    for step in (64, 32, 16, 8, 4, 2, 1):
        candidate = power * 2.0**step
        power = jnp.where((candidate <= 2.0**63) & fits(candidate), candidate, power)
    return power


def unit(size):
    return lax.broadcasted_iota(jnp.int32, (size, size), 0) == lax.broadcasted_iota(jnp.int32, (size, size), 1)


def as_row(column):
    size = column.shape[0]
    return jnp.sum(jnp.where(unit(size), jnp.broadcast_to(column, (size, size)), 0.0), axis=0, keepdims=True)


def pair_of(high, low):
    total = high + low
    return total, low - (total - high)


def pair_sum(a, b):
    (a_high, a_low), (b_high, b_low) = a, b
    total = a_high + b_high
    back = total - a_high
    error = (a_high - (total - back)) + (b_high - back)
    return pair_of(total, error + (a_low + b_low))


def gram_pair(field, rows, cells, scale_out, sums):
    probes, columns = field.shape[1:]

    def largest(index, so_far):
        for r in (2 * index, 2 * index + 1):
            so_far = tuple(jnp.maximum(m, jnp.abs(field[r, 8 * o : 8 * o + 8, :])) for o, m in enumerate(so_far))
        return so_far

    tops = lax.fori_loop(0, rows // 2, largest, tuple(jnp.zeros((8, columns), jnp.float32) for _ in range(probes // 8)))
    top = jnp.concatenate([jnp.max(m, axis=1, keepdims=True) for m in tops], axis=0)
    scale = largest_power(lambda power: top * power <= 128.0, (probes, 1))
    inverse = 1.0 / scale
    scale_out[...] = jnp.broadcast_to(inverse, scale_out.shape)
    sums[...] = jnp.zeros_like(sums)

    def cut(index):
        for r in range(4):
            parts = digits_of(field[4 * index + r] * scale)
            cells[4 * index + r] = jnp.concatenate([part.astype(jnp.bfloat16) for part in parts], axis=0)

    def products(index):
        pairs = []
        for pair in range(2):
            r = 4 * index + 2 * pair
            two = jnp.concatenate([cells[r], cells[r + 1]], axis=1)
            pairs.append(lax.dot_general(two, two, (((1,), (1,)), ((), ())), preferred_element_type=jnp.float32))
        return pairs

    def gather(pairs):
        sums[...] += pairs[0].astype(jnp.int32) + pairs[1].astype(jnp.int32)

    def step(index, carry):
        pairs = products(index)
        cut(index + 1)
        gather(pairs)
        return carry

    cut(0)
    lax.fori_loop(0, rows // 4 - 1, step, 0)
    gather(products(rows // 4 - 1))
    places = []
    for place in range(2 * DIGITS - 1):
        terms = [
            sums[a * probes : (a + 1) * probes, (place - a) * probes : (place - a + 1) * probes]
            for a in range(DIGITS)
            if 0 <= place - a < DIGITS
        ]
        places.append(functools.reduce(lambda x, y: x + y, terms))
    for place in range(2 * DIGITS - 2, 0, -1):
        places[place - 1] = places[place - 1] + (places[place] >> 8)
        places[place] = places[place] & 255
    f32 = jnp.float32
    high = (places[0] >> 8).astype(f32) * 256.0
    middle = ((places[0] & 255) * 65536 + places[1] * 256 + places[2]).astype(f32) * 2.0**-16
    low = (places[3] * 65536 + places[4] * 256 + places[5]).astype(f32) * 2.0**-40
    total, rest = pair_of(high, middle)
    total, rest = pair_of(total, rest + low)
    across = as_row(inverse)
    return total * inverse * across, rest * inverse * across


def folded(square):
    half = square.shape[0] // 2
    return jnp.concatenate([square[:half], square[half:]], axis=1)


def unfolded(block):
    half = block.shape[1] // 2
    return jnp.concatenate([block[:, :half], block[:, half:]], axis=0)


def dot(a, b, dims=((1,), (0,))):
    return lax.dot_general(
        a, b, (dims, ((), ())), precision=lax.Precision.HIGHEST, preferred_element_type=jnp.float32
    )


def turned_over(block):
    size, wide = block.shape
    square = jnp.concatenate([block, jnp.zeros((wide - size, wide), jnp.float32)], axis=0)
    return jnp.transpose(square)[:, :size]


PANEL = 8


def eliminated(block):
    size, wide = block.shape
    count = size // 8
    groups = [block[8 * g : 8 * g + 8] for g in range(count)]
    like = (8, wide)
    below = lax.broadcasted_iota(jnp.int32, like, 0)
    for first in range(0, size, PANEL):
        g, start = divmod(first, 8)
        columns = {
            o: [jnp.broadcast_to(groups[o][:, first + t : first + t + 1], like) for t in range(PANEL)]
            for o in range(g, count)
        }
        for t in range(PANEL):
            s = start + t
            across = [jnp.broadcast_to(columns[g][u][s : s + 1], like) for u in range(t, PANEL)]
            inverse = 1.0 / across[0]
            row = jnp.broadcast_to(groups[g][s : s + 1], like) * inverse
            across = [value * inverse for value in across]
            for o in range(g, count):
                if o == g and s == 7:
                    continue
                column = columns[o][t]
                if o == g:
                    column = jnp.where(below > s, column, 0.0)
                groups[o] = groups[o] - column * row
                for u in range(t + 1, PANEL):
                    columns[o][u] = columns[o][u] - column * across[u - t]
    return normalised(jnp.concatenate(groups, axis=0))


def normalised(block):
    size, wide = block.shape
    row_ids = lax.broadcasted_iota(jnp.int32, block.shape, 0)
    lanes = lax.broadcasted_iota(jnp.int32, block.shape, 1)
    pivots = jnp.sum(jnp.where(row_ids == lanes, block, 0.0), axis=1, keepdims=True)
    scale = lax.rsqrt(pivots)
    scale = scale * (1.5 - 0.5 * pivots * scale * scale)
    block = block * scale
    keep = (lanes >= row_ids) & ((lanes < size) | (lanes - size <= row_ids))
    return jnp.where(keep, block, 0.0)


def eliminated_slowly(block, work):
    size, wide = block.shape
    work[...] = block
    row_ids = lax.broadcasted_iota(jnp.int32, (size, 1), 0)
    lanes = lax.broadcasted_iota(jnp.int32, (1, wide), 1)

    def step(j, carry):
        row = work[pl.ds(j, 1), :]
        pivot = jnp.sum(jnp.where(lanes == j, row, 0.0), axis=1, keepdims=True)
        column = jnp.sum(jnp.where(lanes == j, work[...], 0.0), axis=1, keepdims=True)
        work[...] = work[...] - jnp.where(row_ids > j, column, 0.0) * (row / pivot)
        return carry

    lax.fori_loop(0, size, step, 0)
    return normalised(work[...])


def stacked_digits(value):
    return jnp.concatenate([part.astype(jnp.bfloat16) for part in digits_of(value)], axis=0)


def residual(high, low, left, right):
    size = high.shape[0]
    product = lax.dot_general(left, right, (((1,), (1,)), ((), ())), preferred_element_type=jnp.float32)
    places = []
    for place in range(2 * DIGITS - 1):
        terms = [
            product[a * size : (a + 1) * size, (place - a) * size : (place - a + 1) * size]
            for a in range(DIGITS)
            if 0 <= place - a < DIGITS
        ]
        places.append(functools.reduce(lambda x, y: x + y, terms))
    rest = high
    total = jnp.zeros_like(high)
    for place in range(5):
        if place == 2:
            rest = rest + low * 2.0**16
        digit = rounded(rest) if place < 4 else rest
        rest = (rest - digit) * 256.0
        total = total * 256.0 + (digit - places[place])
    total = total - (places[5] * 2.0**-8 + places[6] * 2.0**-16)
    return total * 2.0**-32


def solve_kernel(
    cell_scale, pairs, inner_scale, edge_scale, inner, edge, basis, factor,
    rows_out, work, change, change_inverse, out_sems,
):
    size = pairs.shape[0]
    inner_rows, edge_rows = inner.shape[0], edge.shape[0]
    rows = inner_rows + edge_rows
    high, low = unfolded(pairs[: size // 2, :]), unfolded(pairs[size // 2 :, :])
    is_diagonal = unit(size)
    diagonal = jnp.sum(jnp.where(is_diagonal, high, 0.0), axis=1, keepdims=True)
    scale = largest_power(lambda power: diagonal * power * power < 1.0, (size, 1))
    across = as_row(scale)
    high, low = high * scale * across, low * scale * across
    identity = jnp.where(is_diagonal, 1.0, 0.0)
    first = eliminated(jnp.concatenate([high, identity], axis=1))
    inverse = first[:, size:]
    lower = turned_over(first)[:size]
    lower_digits = stacked_digits(lower * 128.0)
    missed = residual(high * 2.0**14, low * 2.0**14, lower_digits, lower_digits) * 2.0**-14
    inverse_top = jnp.max(jnp.abs(inverse), axis=1, keepdims=True)
    inverse_scale = largest_power(lambda power: inverse_top * power <= 128.0, (size, 1))
    goal = identity * (inverse_scale * 128.0)
    skew = residual(
        goal, jnp.zeros_like(goal), stacked_digits(inverse * inverse_scale), stacked_digits(first[:, :size] * 128.0)
    ) * (-1.0 / 128.0 / inverse_scale)
    near = identity + skew
    error = dot(dot(inverse, missed), inverse, ((1,), (1,))) + (dot(near, near, ((1,), (1,))) - identity)
    weight = jnp.where(
        is_diagonal, 0.5,
        jnp.where(
            lax.broadcasted_iota(jnp.int32, (size, size), 0) > lax.broadcasted_iota(jnp.int32, (size, size), 1), 1.0, 0.0
        ),
    )
    spread = jnp.sum(error * error)
    is_small = spread < 4e-4

    @pl.when(is_small)
    def _():
        y = weight * error
        rounds = jnp.where(spread < 1e-5, 2, 4)
        y = lax.fori_loop(0, rounds, lambda _, y: weight * (error - dot(y, y, ((1,), (1,)))), y)
        change[...] = y
        square = dot(y, y)
        change_inverse[...] = (identity - y) + dot(identity - y, square)

    @pl.when(jnp.logical_not(is_small))
    def _():
        second = eliminated_slowly(jnp.concatenate([identity + error, identity], axis=1), work)
        change[...] = turned_over(second)[:size] - identity
        change_inverse[...] = second[:, size:]

    turn = change[...] - skew
    full = lower + dot(lower, turn - dot(skew, turn))
    full = jnp.concatenate([full, jnp.zeros_like(full)], axis=1)
    factor[...] = turned_over(full)[:size] / across * (1.0 / cell_scale)
    mixing = dot(change_inverse[...], inverse) * across * cell_scale

    def stacked(cut):
        whole_part = mixing * as_row(cut[:, :1])
        pieces = []
        for _ in range(3):
            piece = whole_part.astype(jnp.bfloat16)
            whole_part = whole_part - piece.astype(jnp.float32)
            pieces.append(piece.astype(jnp.float32))
        tall = jnp.concatenate(pieces, axis=0)
        return jnp.concatenate([tall * 256.0**-a for a in range(DIGITS)], axis=1).astype(jnp.bfloat16)

    def finish(matrix, cells, first_row, count, shift):
        def four(index, carry):
            for j in range(4):
                r = 4 * index + j
                product = jnp.dot(matrix, cells[r + shift], preferred_element_type=jnp.float32)
                rows_out[r + first_row] = product[:size] + (product[size : 2 * size] + product[2 * size :])
            for j in range(4):
                at = 4 * index + j + first_row
                pltpu.make_async_copy(rows_out.at[at], basis.at[:, at, :], out_sems.at[at]).start()
            return carry

        lax.fori_loop(0, count // 4, four, 0)

    finish(stacked(inner_scale), inner, DEPTH, inner_rows, 0)
    matrix = stacked(edge_scale)
    finish(matrix, edge, 0, DEPTH, 0)
    finish(matrix, edge, rows - DEPTH, DEPTH, DEPTH)

    def wait(r, carry):
        pltpu.make_async_copy(rows_out.at[r], basis.at[:, r, :], out_sems.at[r]).wait()
        return carry

    lax.fori_loop(0, rows, wait, 0)


def whole(memory=pltpu.VMEM):
    return pl.BlockSpec(memory_space=memory)


def call(kernel, name, out_shape, in_specs, out_specs, scratch_shapes=(), cost=None, vmem=56):
    return pl.pallas_call(
        kernel,
        out_shape=out_shape,
        in_specs=in_specs,
        out_specs=out_specs,
        scratch_shapes=scratch_shapes,
        compiler_params=pltpu.CompilerParams(vmem_limit_bytes=vmem * MIB),
        cost_estimate=cost,
        name=name,
    )


def summed(pairs):
    count = lax.axis_size(AXIS)
    half = pairs.shape[0] // 2

    def add(a, b):
        return jnp.concatenate(pair_sum((a[:half], a[half:]), (b[:half], b[half:])), axis=0)

    if count & (count - 1):
        total = pairs
        for step in range(1, count):
            total = add(total, lax.ppermute(pairs, AXIS, [(i, (i + step) % count) for i in range(count)]))
        return total
    distance = 1
    while distance < count:
        pairs = add(pairs, lax.ppermute(pairs, AXIS, [(i, i ^ distance) for i in range(count)]))
        distance *= 2
    return pairs


def on_device(probes, kappa, speed, friction, upwind, probe_sites):
    count, rows, columns = probes.shape
    size = lax.axis_size(AXIS)
    f32 = jnp.float32
    cell_scale = math.sqrt(rows * columns * size)
    strength = IMPULSE_GAIN * cell_scale
    shape = jax.ShapeDtypeStruct
    halo = shape((DEPTH, count + PACK, columns), f32)
    to_below, to_above = call(
        pack_kernel,
        "pack",
        (halo, halo),
        [whole(pl.ANY)] * 5,
        (whole(), whole()),
        [
            pltpu.VMEM((3, 16, columns), f32),
            pltpu.VMEM(upwind.shape[::-1], jnp.int32),
            pltpu.SemaphoreType.DMA((2, DEPTH)),
            pltpu.SemaphoreType.DMA((4, 2)),
        ],
        vmem=56,
    )(probes, kappa, speed, friction, upwind.T)
    from_above = lax.ppermute(to_below, AXIS, [(i, i + 1) for i in range(size - 1)])
    from_below = lax.ppermute(to_above, AXIS, [(i + 1, i) for i in range(size - 1)])
    edge_count = 2 * DEPTH
    inner_count = rows - edge_count
    tall = DIGITS * count

    def digit_rows(number):
        return shape((number, tall, columns), jnp.bfloat16), shape((count, 128), f32), shape((count, 2 * count), f32)

    def digit_scratch(number):
        return [
            pltpu.VMEM((number, count, columns), f32),
            pltpu.VMEM((tall, tall), jnp.int32),
        ]

    kept = shape((4, 2, count, columns), f32)
    field = pltpu.VMEM((rows, count, columns), f32)
    inner, inner_scale, pairs, top, bottom, weights = call(
        functools.partial(inner_kernel, strength),
        "inner_rows",
        digit_rows(inner_count) + (kept, kept, shape((7, rows, columns), f32)),
        [whole(pltpu.SMEM), whole(pl.ANY)] + [whole()] * 4,
        (whole(),) * 6,
        [field] * 4
        + digit_scratch(inner_count)
        + [pltpu.SMEM((count + 1,), jnp.int32)]
        + [pltpu.SemaphoreType.DMA((rows,))],
        pl.CostEstimate(flops=10**10, bytes_accessed=16 * MIB, transcendentals=0),
        vmem=32,
    )(probe_sites, probes, kappa, speed, friction, upwind.T)
    fields = pltpu.VMEM((2 * DEPTH + 4, count, columns), f32)
    levels = pltpu.VMEM((3, DEPTH + 2, count, columns), f32)
    edge, edge_scale, pairs = call(
        functools.partial(edge_kernel, strength, rows),
        "edge_rows",
        digit_rows(edge_count),
        [whole(pltpu.SMEM)] + [whole(pl.ANY)] * 5 + [whole()],
        (whole(), whole(), whole()),
        [
            pltpu.VMEM((7, 8 * DEPTH, columns), f32), fields, levels, levels,
            pltpu.VMEM((2, DEPTH, PACK, columns), f32),
        ]
        + digit_scratch(edge_count)
        + [pltpu.SMEM((count + 1,), jnp.int32), pltpu.SemaphoreType.DMA((10,))],
        vmem=16,
    )(probe_sites, from_above, from_below, weights, top, bottom, pairs)
    pairs = summed(pairs)
    square = pltpu.VMEM((count, count), f32)
    return call(
        functools.partial(solve_kernel, cell_scale),
        "solve",
        (shape((count, rows, columns), f32), shape((count, count), f32)),
        [whole()] * 5,
        (whole(pl.ANY), whole()),
        [
            pltpu.VMEM((rows, count, columns), f32),
            pltpu.VMEM((count, 2 * count), f32),
            square,
            square,
            pltpu.SemaphoreType.DMA((rows,)),
        ],
        vmem=24,
    )(pairs, inner_scale, edge_scale, inner, edge)


def solution(mesh):
    return jax.shard_map(
        on_device,
        mesh=mesh,
        in_specs=(
            P(None, ("groups", "gx"), None),
            P(("groups", "gx"), None),
            P(("groups", "gx"), None),
            P(("groups", "gx"), None),
            P(("groups", "gx"), None),
            P("groups"),
        ),
        out_specs=(P(None, ("groups", "gx"), None), P("groups", None)),
        check_vma=False,
    )
```

```python
import functools
import math

import jax
import jax.numpy as jnp
from jax import lax
from jax.experimental import pallas as pl
from jax.experimental.pallas import tpu as pltpu
from jax.sharding import PartitionSpec as P

TIME_STEP = 0.2
IMPULSE_GAIN = 3.0
AXIS = "gx"
DEPTH = 4
ARRIVALS = 11
GROUP = 4
PACK = 8
MIB = 1024 * 1024


def rolled(row, by):
    return pltpu.roll(row, by % row.shape[-1], row.ndim - 1)


def weight_row(weights, row, layer, like):
    return jnp.broadcast_to(weights[layer, pl.ds(row, 1), :], like)


def in_steps(first, last, body, step=10):
    whole_steps = (last - first) // step

    def several(index, carry):
        for j in range(step):
            body(first + index * step + j)
        return carry

    lax.fori_loop(0, whole_steps, several, 0)
    for r in range(first + whole_steps * step, last):
        body(r)


def sweep_row(source, at, target, to, probes, columns, center, above, below, left, right, tops=None):
    for first in range(0, probes, 8):
        octet = slice(first, first + 8)
        middle = source[at, octet, :]
        result = (
            center * middle
            + above * source[at - 1, octet, :]
            + below * source[at + 1, octet, :]
            + left * rolled(middle, 1)
            + right * rolled(middle, -1)
        )
        target[to, octet, :] = result
        if tops is not None:
            tops[octet, :] = jnp.maximum(tops[octet, :], jnp.abs(result))


def forward_row(source, at, target, to, weights, w_at, probes, columns):
    like = (8, columns)
    sweep_row(
        source, at, target, to, probes, columns,
        *[weight_row(weights, w_at, layer, like) for layer in range(5)],
    )


def adjoint_row(source, at, target, to, weights, w_at, probes, columns, tops=None):
    like = (8, columns)
    sweep_row(
        source, at, target, to, probes, columns,
        weight_row(weights, w_at, 0, like),
        weight_row(weights, w_at - 1, 2, like),
        weight_row(weights, w_at + 1, 1, like),
        weight_row(weights, w_at, 5, like),
        weight_row(weights, w_at, 6, like),
        tops=tops,
    )


def find_impulses(sites, found, held, probes):
    unroll = 8

    def several(index, count):
        for j in range(unroll):
            k = index * unroll + j
            found[count] = k
            count = jnp.where(held(sites[k]), count + 1, count)
        return count

    return lax.fori_loop(0, probes // unroll, several, 0)


def row_and_column(site, columns):
    if columns & (columns - 1):
        return lax.div(site, columns), lax.rem(site, columns)
    return site >> (columns.bit_length() - 1), site & (columns - 1)


def add_impulses(sites, found, count, target, place_of, columns, strength, wanted=None):
    column_ids = lax.broadcasted_iota(jnp.int32, (1, columns), 1)

    def one(index, carry):
        k = found[index]
        row, column = row_and_column(sites[k], columns)

        def add():
            target[place_of(row), pl.ds(k, 1), :] += jnp.where(column_ids == column, strength, 0.0)

        if wanted is None:
            add()
        else:
            pl.when(wanted(row))(add)
        return carry

    lax.fori_loop(0, count, one, 0)


def weight_layers(kappa, speed, friction, upwind):
    rows, columns = kappa.shape
    blocks = upwind.shape[0]
    width = columns // blocks
    spread = (
        lax.broadcasted_iota(jnp.int32, (blocks, columns), 1) // width
        == lax.broadcasted_iota(jnp.int32, (blocks, columns), 0)
    ).astype(jnp.bfloat16)
    directions = lax.dot_general(
        upwind.astype(jnp.float32).astype(jnp.bfloat16), spread, (((0,), (0,)), ((), ())),
        preferred_element_type=jnp.float32,
    )
    column_ids = lax.broadcasted_iota(jnp.int32, (rows, columns), 1)
    layers = [1.0 - TIME_STEP * (4.0 * kappa + speed + friction)]
    for direction in range(4):
        chosen = jnp.where(jnp.abs(directions - direction) < 0.5, speed, 0.0)
        layers.append(TIME_STEP * (kappa + chosen))
    layers[3] = jnp.where(column_ids == 0, 0.0, layers[3])
    layers[4] = jnp.where(column_ids == columns - 1, 0.0, layers[4])
    return layers


def turn_weights(weights):
    weights[5] = rolled(weights[4], 1)
    weights[6] = rolled(weights[3], -1)


def pack_kernel(cells, kappa, speed, friction, upwind, to_below, to_above, cell_rows, directions, sems, cell_sems):
    probes, rows, columns = cells.shape
    copies = []
    for r in range(DEPTH):
        for side, target in enumerate((to_above, to_below)):
            row = r if side == 0 else rows - DEPTH + r
            copies.append(
                pltpu.make_async_copy(cells.at[:, row, :], target.at[r, pl.ds(0, probes), :], sems.at[side, r])
            )
    small = [pltpu.make_async_copy(upwind, directions, cell_sems.at[3, 0])]
    for index, source in enumerate((kappa, speed, friction)):
        for side, row in enumerate((0, rows - 8)):
            small.append(
                pltpu.make_async_copy(
                    source.at[pl.ds(row, 8)], cell_rows.at[index, pl.ds(8 * side, 8)], cell_sems.at[index, side]
                )
            )
    for copy in copies + small:
        copy.start()
    for copy in small:
        copy.wait()
    ends = jnp.concatenate([directions[:, :8], directions[:, rows - 8 :]], axis=1)
    for index, layer in enumerate(weight_layers(cell_rows[0], cell_rows[1], cell_rows[2], ends)):
        place = probes + index
        for r in range(DEPTH):
            to_above[r, place : place + 1, :] = layer[r : r + 1]
            to_below[r, place : place + 1, :] = layer[16 - DEPTH + r : 16 - DEPTH + r + 1]
    for side in (to_above, to_below):
        side[:, probes + 5 :, :] = jnp.zeros((DEPTH, PACK - 5, columns), jnp.float32)
    for copy in copies:
        copy.wait()


def inner_kernel(
    strength, sites, cells, kappa, speed, friction, upwind, digits, scale, pairs, top, bottom, weights, v, f1, f2, a1, response, sums, tops, found, sems
):
    rows, probes, columns = v.shape
    first_row = lax.axis_index(AXIS) * rows

    copies = [pltpu.make_async_copy(cells.at[:, r, :], v.at[r], sems.at[r]) for r in range(rows)]
    for copy in copies[:ARRIVALS]:
        copy.start()
    for index, layer in enumerate(weight_layers(kappa[...], speed[...], friction[...], upwind[...])):
        weights[index] = layer
    turn_weights(weights)
    first_cell, end_cell = first_row * columns, (first_row + rows) * columns
    hits = find_impulses(sites, found, lambda site: (site >= first_cell) & (site < end_cell), probes)
    def forward_first(r):
        forward_row(v, r, f1, r, weights, r, probes, columns)

    ready, done = 0, 1
    while ready < rows:
        upto = min(rows, ready + ARRIVALS)
        for copy in copies[upto : upto + ARRIVALS]:
            copy.start()
        for copy in copies[ready:upto]:
            copy.wait()
        low, high = first_row + ready, first_row + upto
        add_impulses(
            sites, found, hits, v, lambda row: row - first_row, columns, strength,
            lambda row, low=low, high=high: (row >= low) & (row < high),
        )
        in_steps(done, upto - 1, forward_first)
        ready, done = upto, upto - 1

    def sweep(row_fn, source, target, first, shift=0, **kept):
        def body(r):
            row_fn(source, r, target, r - shift, weights, r, probes, columns, **kept)

        in_steps(first, rows - first, body)

    sweep(forward_row, f1, f2, 2)
    sweep(adjoint_row, f2, a1, 3)
    tops[...] = jnp.zeros_like(tops)
    sweep(adjoint_row, a1, response, DEPTH, DEPTH, tops=tops)
    for level, field in enumerate((v, f1, f2, a1)):
        for j in range(2):
            top[level, j] = field[level + j]
            bottom[level, j] = field[rows - 2 - level + j]
    high, low = gram_pair(response, rows - 2 * DEPTH, tops, digits, scale, sums)
    pairs[...] = jnp.concatenate([folded(high), folded(low)], axis=0)


def edge_kernel(
    strength, rows, sites, above, below, weights, top, bottom, inner_pairs, digits, scale, pairs,
    w, va, la, lb, behind, response, sums, tops, found, sems,
):
    probes, columns = top.shape[2:]
    first_row = lax.axis_index(AXIS) * rows
    start_a, start_b = 2 * DEPTH, 4 * DEPTH
    vb = va.at[DEPTH + 2 :]
    copies = [
        (above.at[:, pl.ds(probes, PACK), :], behind.at[0]),
        (below.at[:, pl.ds(probes, PACK), :], behind.at[1]),
        (weights.at[pl.ds(0, 5), pl.ds(0, 8), :], w.at[pl.ds(0, 5), pl.ds(start_a, 8), :]),
        (weights.at[pl.ds(0, 5), pl.ds(rows - 8, 8), :], w.at[pl.ds(0, 5), pl.ds(start_b, 8), :]),
        (above.at[:, pl.ds(0, probes), :], va.at[pl.ds(0, DEPTH)]),
        (below.at[:, pl.ds(0, probes), :], va.at[pl.ds(DEPTH + 4, DEPTH)]),
        (top.at[0], va.at[pl.ds(DEPTH, 2)]),
        (bottom.at[0], va.at[pl.ds(DEPTH + 2, 2)]),
        (top.at[pl.ds(1, 3)], la.at[:, pl.ds(DEPTH, 2)]),
        (bottom.at[pl.ds(1, 3)], lb.at[:, pl.ds(0, 2)]),
    ]
    copies = [pltpu.make_async_copy(source, target, sems.at[i]) for i, (source, target) in enumerate(copies)]
    for copy in copies:
        copy.start()

    cells = rows * columns
    first_cell = first_row * columns

    def held(site):
        near = site - first_cell
        is_above = (near >= -DEPTH * columns) & (near < 0)
        return is_above | ((near >= cells) & (near < cells + DEPTH * columns))

    hits = find_impulses(sites, found, held, probes)
    for copy in copies:
        copy.wait()
    for layer in range(5):
        for r in range(DEPTH):
            w[layer, DEPTH + r : DEPTH + r + 1, :] = behind[0, r, layer : layer + 1, :]
            w[layer, start_b + 2 * DEPTH + r : start_b + 2 * DEPTH + r + 1, :] = behind[1, r, layer : layer + 1, :]
    turn_weights(w)
    add_impulses(
        sites, found, hits, va,
        lambda row: jnp.where(row < first_row, row - first_row + DEPTH, row - first_row - rows + DEPTH + 4), columns, strength,
    )
    chain_a = [va, la.at[0], la.at[1], la.at[2], response]
    chain_b = [vb, lb.at[0], lb.at[1], lb.at[2], response]
    for level in range(4):
        row_fn = forward_row if level < 2 else adjoint_row
        for j in range(DEPTH):
            row_fn(chain_a[level], j + 1, chain_a[level + 1], j, w, start_a + level - 3 + j, probes, columns)
            to = j + (DEPTH if level == 3 else 2)
            row_fn(chain_b[level], j + 1, chain_b[level + 1], to, w, start_b + 7 - level + j, probes, columns)
    for first in range(0, probes, 8):
        sizes = [jnp.abs(response[r, first : first + 8, :]) for r in range(2 * DEPTH)]
        tops[first : first + 8, :] = functools.reduce(jnp.maximum, sizes)
    ours = gram_pair(response, 2 * DEPTH, tops, digits, scale, sums)
    half = probes // 2
    high, low = pair_sum(ours, (unfolded(inner_pairs[:half, :]), unfolded(inner_pairs[half:, :])))
    pairs[...] = jnp.concatenate([folded(high), folded(low)], axis=0)


DIGITS = 4
ROUNDER = 12582912.0


def rounded(value):
    return (value + ROUNDER) - ROUNDER


def digits_of(value):
    out = []
    for position in range(DIGITS):
        digit = rounded(value)
        out.append(digit)
        if position < DIGITS - 1:
            value = (value - digit) * 256.0
    return out


def largest_power(fits, like):
    power = jnp.full(like, 2.0**-63, jnp.float32)
    for step in (64, 32, 16, 8, 4, 2, 1):
        candidate = power * 2.0**step
        power = jnp.where((candidate <= 2.0**63) & fits(candidate), candidate, power)
    return power


def unit(size):
    return lax.broadcasted_iota(jnp.int32, (size, size), 0) == lax.broadcasted_iota(jnp.int32, (size, size), 1)


def as_row(column):
    size = column.shape[0]
    return jnp.sum(jnp.where(unit(size), jnp.broadcast_to(column, (size, size)), 0.0), axis=0, keepdims=True)


def pair_of(high, low):
    total = high + low
    return total, low - (total - high)


def pair_sum(a, b):
    (a_high, a_low), (b_high, b_low) = a, b
    total = a_high + b_high
    back = total - a_high
    error = (a_high - (total - back)) + (b_high - back)
    return pair_of(total, error + (a_low + b_low))


def gram_pair(field, rows, tops, cells, scale_out, sums):
    probes, columns = field.shape[1:]

    top = jnp.max(tops[...], axis=1, keepdims=True)
    scale = largest_power(lambda power: top * power <= 128.0, (probes, 1))
    inverse = 1.0 / scale
    scale_out[...] = jnp.broadcast_to(inverse, scale_out.shape)
    sums[...] = jnp.zeros_like(sums)

    def cut(index):
        for r in range(GROUP):
            at = GROUP * index + r
            parts = digits_of(field[at] * scale)
            cells[at] = jnp.concatenate([part.astype(jnp.bfloat16) for part in parts], axis=0)

    def products(index):
        total = None
        for pair in range(GROUP // 2):
            r = GROUP * index + 2 * pair
            two = jnp.concatenate([cells[r], cells[r + 1]], axis=1)
            product = lax.dot_general(two, two, (((1,), (1,)), ((), ())), preferred_element_type=jnp.float32)
            product = product.astype(jnp.int32)
            total = product if total is None else total + product
        return total

    def step(index, carry):
        total = products(index)
        cut(index + 1)
        sums[...] += total
        return carry

    cut(0)
    lax.fori_loop(0, rows // GROUP - 1, step, 0)
    sums[...] += products(rows // GROUP - 1)
    places = []
    for place in range(2 * DIGITS - 1):
        terms = [
            sums[a * probes : (a + 1) * probes, (place - a) * probes : (place - a + 1) * probes]
            for a in range(DIGITS)
            if 0 <= place - a < DIGITS
        ]
        places.append(functools.reduce(lambda x, y: x + y, terms))
    for place in range(2 * DIGITS - 2, 0, -1):
        places[place - 1] = places[place - 1] + (places[place] >> 8)
        places[place] = places[place] & 255
    f32 = jnp.float32
    high = (places[0] >> 8).astype(f32) * 256.0
    middle = ((places[0] & 255) * 65536 + places[1] * 256 + places[2]).astype(f32) * 2.0**-16
    low = (places[3] * 65536 + places[4] * 256 + places[5]).astype(f32) * 2.0**-40
    total, rest = pair_of(high, middle)
    total, rest = pair_of(total, rest + low)
    across = as_row(inverse)
    return total * inverse * across, rest * inverse * across


def folded(square):
    half = square.shape[0] // 2
    return jnp.concatenate([square[:half], square[half:]], axis=1)


def unfolded(block):
    half = block.shape[1] // 2
    return jnp.concatenate([block[:, :half], block[:, half:]], axis=0)


def dot(a, b, dims=((1,), (0,))):
    return lax.dot_general(
        a, b, (dims, ((), ())), precision=lax.Precision.HIGHEST, preferred_element_type=jnp.float32
    )


def turned_over(block):
    size, wide = block.shape
    square = jnp.concatenate([block, jnp.zeros((wide - size, wide), jnp.float32)], axis=0)
    return jnp.transpose(square)[:, :size]


PANEL = 8


def eliminated(block):
    size, wide = block.shape
    count = size // 8
    groups = [block[8 * g : 8 * g + 8] for g in range(count)]
    like = (8, wide)
    below = lax.broadcasted_iota(jnp.int32, like, 0)
    for first in range(0, size, PANEL):
        g, start = divmod(first, 8)
        columns = {
            o: [jnp.broadcast_to(groups[o][:, first + t : first + t + 1], like) for t in range(PANEL)]
            for o in range(g, count)
        }
        for t in range(PANEL):
            s = start + t
            across = [jnp.broadcast_to(columns[g][u][s : s + 1], like) for u in range(t, PANEL)]
            inverse = 1.0 / across[0]
            row = jnp.broadcast_to(groups[g][s : s + 1], like) * inverse
            across = [value * inverse for value in across]
            for o in range(g, count):
                if o == g and s == 7:
                    continue
                column = columns[o][t]
                if o == g:
                    column = jnp.where(below > s, column, 0.0)
                groups[o] = groups[o] - column * row
                for u in range(t + 1, PANEL):
                    columns[o][u] = columns[o][u] - column * across[u - t]
    return normalised(jnp.concatenate(groups, axis=0))


def normalised(block):
    size, wide = block.shape
    row_ids = lax.broadcasted_iota(jnp.int32, block.shape, 0)
    lanes = lax.broadcasted_iota(jnp.int32, block.shape, 1)
    pivots = jnp.sum(jnp.where(row_ids == lanes, block, 0.0), axis=1, keepdims=True)
    scale = lax.rsqrt(pivots)
    scale = scale * (1.5 - 0.5 * pivots * scale * scale)
    block = block * scale
    keep = (lanes >= row_ids) & ((lanes < size) | (lanes - size <= row_ids))
    return jnp.where(keep, block, 0.0)


def eliminated_slowly(block, work):
    size, wide = block.shape
    work[...] = block
    row_ids = lax.broadcasted_iota(jnp.int32, (size, 1), 0)
    lanes = lax.broadcasted_iota(jnp.int32, (1, wide), 1)

    def step(j, carry):
        row = work[pl.ds(j, 1), :]
        pivot = jnp.sum(jnp.where(lanes == j, row, 0.0), axis=1, keepdims=True)
        column = jnp.sum(jnp.where(lanes == j, work[...], 0.0), axis=1, keepdims=True)
        work[...] = work[...] - jnp.where(row_ids > j, column, 0.0) * (row / pivot)
        return carry

    lax.fori_loop(0, size, step, 0)
    return normalised(work[...])


def stacked_digits(value):
    return jnp.concatenate([part.astype(jnp.bfloat16) for part in digits_of(value)], axis=0)


def residual(high, low, left, right):
    size = high.shape[0]
    product = lax.dot_general(left, right, (((1,), (1,)), ((), ())), preferred_element_type=jnp.float32)
    places = []
    for place in range(2 * DIGITS - 1):
        terms = [
            product[a * size : (a + 1) * size, (place - a) * size : (place - a + 1) * size]
            for a in range(DIGITS)
            if 0 <= place - a < DIGITS
        ]
        places.append(functools.reduce(lambda x, y: x + y, terms))
    rest = high
    total = jnp.zeros_like(high)
    for place in range(5):
        if place == 2:
            rest = rest + low * 2.0**16
        digit = rounded(rest) if place < 4 else rest
        rest = (rest - digit) * 256.0
        total = total * 256.0 + (digit - places[place])
    total = total - (places[5] * 2.0**-8 + places[6] * 2.0**-16)
    return total * 2.0**-32


def solve_kernel(
    cell_scale, pairs, inner_scale, edge_scale, inner, edge, basis, factor,
    rows_out, work, change, change_inverse, out_sems,
):
    size = pairs.shape[0]
    inner_rows, edge_rows = inner.shape[0], edge.shape[0]
    rows = inner_rows + edge_rows
    high, low = unfolded(pairs[: size // 2, :]), unfolded(pairs[size // 2 :, :])
    is_diagonal = unit(size)
    diagonal = jnp.sum(jnp.where(is_diagonal, high, 0.0), axis=1, keepdims=True)
    scale = largest_power(lambda power: diagonal * power * power < 1.0, (size, 1))
    across = as_row(scale)
    high, low = high * scale * across, low * scale * across
    identity = jnp.where(is_diagonal, 1.0, 0.0)
    first = eliminated(jnp.concatenate([high, identity], axis=1))
    inverse = first[:, size:]
    lower = turned_over(first)[:size]
    lower_digits = stacked_digits(lower * 128.0)
    missed = residual(high * 2.0**14, low * 2.0**14, lower_digits, lower_digits) * 2.0**-14
    inverse_top = jnp.max(jnp.abs(inverse), axis=1, keepdims=True)
    inverse_scale = largest_power(lambda power: inverse_top * power <= 128.0, (size, 1))
    goal = identity * (inverse_scale * 128.0)
    skew = residual(
        goal, jnp.zeros_like(goal), stacked_digits(inverse * inverse_scale), stacked_digits(first[:, :size] * 128.0)
    ) * (-1.0 / 128.0 / inverse_scale)
    near = identity + skew
    error = dot(dot(inverse, missed), inverse, ((1,), (1,))) + (dot(near, near, ((1,), (1,))) - identity)
    weight = jnp.where(
        is_diagonal, 0.5,
        jnp.where(
            lax.broadcasted_iota(jnp.int32, (size, size), 0) > lax.broadcasted_iota(jnp.int32, (size, size), 1), 1.0, 0.0
        ),
    )
    spread = jnp.sum(error * error)
    is_small = spread < 4e-4

    @pl.when(is_small)
    def _():
        y = weight * error
        rounds = jnp.where(spread < 1e-5, 2, 4)
        y = lax.fori_loop(0, rounds, lambda _, y: weight * (error - dot(y, y, ((1,), (1,)))), y)
        change[...] = y
        square = dot(y, y)
        change_inverse[...] = (identity - y) + dot(identity - y, square)

    @pl.when(jnp.logical_not(is_small))
    def _():
        second = eliminated_slowly(jnp.concatenate([identity + error, identity], axis=1), work)
        change[...] = turned_over(second)[:size] - identity
        change_inverse[...] = second[:, size:]

    turn = change[...] - skew
    full = lower + dot(lower, turn - dot(skew, turn))
    full = jnp.concatenate([full, jnp.zeros_like(full)], axis=1)
    factor[...] = turned_over(full)[:size] / across * (1.0 / cell_scale)
    mixing = dot(change_inverse[...], inverse) * across * cell_scale

    def stacked(cut):
        whole_part = mixing * as_row(cut[:, :1])
        pieces = []
        for _ in range(3):
            piece = whole_part.astype(jnp.bfloat16)
            whole_part = whole_part - piece.astype(jnp.float32)
            pieces.append(piece.astype(jnp.float32))
        tall = jnp.concatenate(pieces, axis=0)
        return jnp.concatenate([tall * 256.0**-a for a in range(DIGITS)], axis=1).astype(jnp.bfloat16)

    def finish(matrix, cells, first_row, count, shift):
        group = min(2 * GROUP, count)

        def several(index, carry):
            for j in range(group):
                r = group * index + j
                product = jnp.dot(matrix, cells[r + shift], preferred_element_type=jnp.float32)
                rows_out[r + first_row] = product[:size] + (product[size : 2 * size] + product[2 * size :])
            for j in range(group):
                at = group * index + j + first_row
                pltpu.make_async_copy(rows_out.at[at], basis.at[:, at, :], out_sems.at[at]).start()
            return carry

        lax.fori_loop(0, count // group, several, 0)

    finish(stacked(inner_scale), inner, DEPTH, inner_rows, 0)
    matrix = stacked(edge_scale)
    finish(matrix, edge, 0, DEPTH, 0)
    finish(matrix, edge, rows - DEPTH, DEPTH, DEPTH)

    def wait(r, carry):
        pltpu.make_async_copy(rows_out.at[r], basis.at[:, r, :], out_sems.at[r]).wait()
        return carry

    lax.fori_loop(0, rows, wait, 0)


def whole(memory=pltpu.VMEM):
    return pl.BlockSpec(memory_space=memory)


def call(kernel, name, out_shape, in_specs, out_specs, scratch_shapes=(), cost=None, vmem=56):
    return pl.pallas_call(
        kernel,
        out_shape=out_shape,
        in_specs=in_specs,
        out_specs=out_specs,
        scratch_shapes=scratch_shapes,
        compiler_params=pltpu.CompilerParams(vmem_limit_bytes=vmem * MIB),
        cost_estimate=cost,
        name=name,
    )


def summed(pairs):
    count = lax.axis_size(AXIS)
    half = pairs.shape[0] // 2

    def add(a, b):
        return jnp.concatenate(pair_sum((a[:half], a[half:]), (b[:half], b[half:])), axis=0)

    if count & (count - 1):
        total = pairs
        for step in range(1, count):
            total = add(total, lax.ppermute(pairs, AXIS, [(i, (i + step) % count) for i in range(count)]))
        return total
    distance = 1
    while distance < count:
        pairs = add(pairs, lax.ppermute(pairs, AXIS, [(i, i ^ distance) for i in range(count)]))
        distance *= 2
    return pairs


def on_device(probes, kappa, speed, friction, upwind, probe_sites):
    count, rows, columns = probes.shape
    size = lax.axis_size(AXIS)
    f32 = jnp.float32
    cell_scale = math.sqrt(rows * columns * size)
    strength = IMPULSE_GAIN * cell_scale
    shape = jax.ShapeDtypeStruct
    halo = shape((DEPTH, count + PACK, columns), f32)
    to_below, to_above = call(
        pack_kernel,
        "pack",
        (halo, halo),
        [whole(pl.ANY)] * 5,
        (whole(), whole()),
        [
            pltpu.VMEM((3, 16, columns), f32),
            pltpu.VMEM(upwind.shape[::-1], jnp.int32),
            pltpu.SemaphoreType.DMA((2, DEPTH)),
            pltpu.SemaphoreType.DMA((4, 2)),
        ],
        vmem=56,
    )(probes, kappa, speed, friction, upwind.T)
    from_above = lax.ppermute(to_below, AXIS, [(i, i + 1) for i in range(size - 1)])
    from_below = lax.ppermute(to_above, AXIS, [(i + 1, i) for i in range(size - 1)])
    edge_count = 2 * DEPTH
    inner_count = rows - edge_count
    tall = DIGITS * count

    def digit_rows(number):
        return shape((number, tall, columns), jnp.bfloat16), shape((count, 128), f32), shape((count, 2 * count), f32)

    def digit_scratch(number):
        return [
            pltpu.VMEM((number, count, columns), f32),
            pltpu.VMEM((tall, tall), jnp.int32),
            pltpu.VMEM((count, columns), f32),
        ]

    kept = shape((4, 2, count, columns), f32)
    field = pltpu.VMEM((rows, count, columns), f32)
    inner, inner_scale, pairs, top, bottom, weights = call(
        functools.partial(inner_kernel, strength),
        "inner_rows",
        digit_rows(inner_count) + (kept, kept, shape((7, rows, columns), f32)),
        [whole(pltpu.SMEM), whole(pl.ANY)] + [whole()] * 4,
        (whole(),) * 6,
        [field] * 4
        + digit_scratch(inner_count)
        + [pltpu.SMEM((count + 1,), jnp.int32)]
        + [pltpu.SemaphoreType.DMA((rows,))],
        pl.CostEstimate(flops=10**10, bytes_accessed=16 * MIB, transcendentals=0),
        vmem=32,
    )(probe_sites, probes, kappa, speed, friction, upwind.T)
    fields = pltpu.VMEM((2 * DEPTH + 4, count, columns), f32)
    levels = pltpu.VMEM((3, DEPTH + 2, count, columns), f32)
    edge, edge_scale, pairs = call(
        functools.partial(edge_kernel, strength, rows),
        "edge_rows",
        digit_rows(edge_count),
        [whole(pltpu.SMEM)] + [whole(pl.ANY)] * 5 + [whole()],
        (whole(), whole(), whole()),
        [
            pltpu.VMEM((7, 8 * DEPTH, columns), f32), fields, levels, levels,
            pltpu.VMEM((2, DEPTH, PACK, columns), f32),
        ]
        + digit_scratch(edge_count)
        + [pltpu.SMEM((count + 1,), jnp.int32), pltpu.SemaphoreType.DMA((10,))],
        vmem=16,
    )(probe_sites, from_above, from_below, weights, top, bottom, pairs)
    pairs = summed(pairs)
    square = pltpu.VMEM((count, count), f32)
    return call(
        functools.partial(solve_kernel, cell_scale),
        "solve",
        (shape((count, rows, columns), f32), shape((count, count), f32)),
        [whole()] * 5,
        (whole(pl.ANY), whole()),
        [
            pltpu.VMEM((rows, count, columns), f32),
            pltpu.VMEM((count, 2 * count), f32),
            square,
            square,
            pltpu.SemaphoreType.DMA((rows,)),
        ],
        vmem=24,
    )(pairs, inner_scale, edge_scale, inner, edge)


def solution(mesh):
    return jax.shard_map(
        on_device,
        mesh=mesh,
        in_specs=(
            P(None, ("groups", "gx"), None),
            P(("groups", "gx"), None),
            P(("groups", "gx"), None),
            P(("groups", "gx"), None),
            P(("groups", "gx"), None),
            P("groups"),
        ),
        out_specs=(P(None, ("groups", "gx"), None), P("groups", None)),
        check_vma=False,
    )
```

```python
import functools
import math

import jax
import jax.numpy as jnp
from jax import lax
from jax.experimental import pallas as pl
from jax.experimental.pallas import tpu as pltpu
from jax.sharding import PartitionSpec as P

TIME_STEP = 0.2
IMPULSE_GAIN = 3.0
AXIS = "gx"
DEPTH = 4
ARRIVALS = 11
GROUP = 4
PACK = 8
MIB = 1024 * 1024


def rolled(row, by):
    return pltpu.roll(row, by % row.shape[-1], row.ndim - 1)


def weight_row(weights, row, layer, like):
    return jnp.broadcast_to(weights[layer, pl.ds(row, 1), :], like)


def in_steps(first, last, body, step=10):
    whole_steps = (last - first) // step

    def several(index, carry):
        for j in range(step):
            body(first + index * step + j)
        return carry

    lax.fori_loop(0, whole_steps, several, 0)
    for r in range(first + whole_steps * step, last):
        body(r)


def sweep_row(source, at, target, to, probes, columns, center, above, below, left, right, tops=None):
    for first in range(0, probes, 8):
        octet = slice(first, first + 8)
        middle = source[at, octet, :]
        result = (
            center * middle
            + above * source[at - 1, octet, :]
            + below * source[at + 1, octet, :]
            + left * rolled(middle, 1)
            + right * rolled(middle, -1)
        )
        target[to, octet, :] = result
        if tops is not None:
            tops[octet, :] = jnp.maximum(tops[octet, :], jnp.abs(result))


def forward_row(source, at, target, to, weights, w_at, probes, columns):
    like = (8, columns)
    sweep_row(
        source, at, target, to, probes, columns,
        *[weight_row(weights, w_at, layer, like) for layer in range(5)],
    )


def adjoint_row(source, at, target, to, weights, w_at, probes, columns, tops=None):
    like = (8, columns)
    sweep_row(
        source, at, target, to, probes, columns,
        weight_row(weights, w_at, 0, like),
        weight_row(weights, w_at - 1, 2, like),
        weight_row(weights, w_at + 1, 1, like),
        weight_row(weights, w_at, 5, like),
        weight_row(weights, w_at, 6, like),
        tops=tops,
    )


def find_impulses(sites, found, held, probes):
    unroll = 8

    def several(index, count):
        for j in range(unroll):
            k = index * unroll + j
            found[count] = k
            count = jnp.where(held(sites[k]), count + 1, count)
        return count

    return lax.fori_loop(0, probes // unroll, several, 0)


def row_and_column(site, columns):
    if columns & (columns - 1):
        return lax.div(site, columns), lax.rem(site, columns)
    return site >> (columns.bit_length() - 1), site & (columns - 1)


def add_impulses(sites, found, count, target, place_of, columns, strength, wanted=None):
    column_ids = lax.broadcasted_iota(jnp.int32, (1, columns), 1)

    def one(index, carry):
        k = found[index]
        row, column = row_and_column(sites[k], columns)

        def add():
            target[place_of(row), pl.ds(k, 1), :] += jnp.where(column_ids == column, strength, 0.0)

        if wanted is None:
            add()
        else:
            pl.when(wanted(row))(add)
        return carry

    lax.fori_loop(0, count, one, 0)


def weight_layers(kappa, speed, friction, upwind):
    rows, columns = kappa.shape
    blocks = upwind.shape[0]
    width = columns // blocks
    spread = (
        lax.broadcasted_iota(jnp.int32, (blocks, columns), 1) // width
        == lax.broadcasted_iota(jnp.int32, (blocks, columns), 0)
    ).astype(jnp.bfloat16)
    directions = lax.dot_general(
        upwind.astype(jnp.float32).astype(jnp.bfloat16), spread, (((0,), (0,)), ((), ())),
        preferred_element_type=jnp.float32,
    )
    column_ids = lax.broadcasted_iota(jnp.int32, (rows, columns), 1)
    layers = [1.0 - TIME_STEP * (4.0 * kappa + speed + friction)]
    for direction in range(4):
        chosen = jnp.where(jnp.abs(directions - direction) < 0.5, speed, 0.0)
        layers.append(TIME_STEP * (kappa + chosen))
    layers[3] = jnp.where(column_ids == 0, 0.0, layers[3])
    layers[4] = jnp.where(column_ids == columns - 1, 0.0, layers[4])
    return layers


def turn_weights(weights):
    weights[5] = rolled(weights[4], 1)
    weights[6] = rolled(weights[3], -1)


def pack_kernel(cells, kappa, speed, friction, upwind, to_below, to_above, cell_rows, directions, sems, cell_sems):
    probes, rows, columns = cells.shape
    copies = []
    for r in range(DEPTH):
        for side, target in enumerate((to_above, to_below)):
            row = r if side == 0 else rows - DEPTH + r
            copies.append(
                pltpu.make_async_copy(cells.at[:, row, :], target.at[r, pl.ds(0, probes), :], sems.at[side, r])
            )
    small = [pltpu.make_async_copy(upwind, directions, cell_sems.at[3, 0])]
    for index, source in enumerate((kappa, speed, friction)):
        for side, row in enumerate((0, rows - 8)):
            small.append(
                pltpu.make_async_copy(
                    source.at[pl.ds(row, 8)], cell_rows.at[index, pl.ds(8 * side, 8)], cell_sems.at[index, side]
                )
            )
    for copy in copies + small:
        copy.start()
    for copy in small:
        copy.wait()
    ends = jnp.concatenate([directions[:, :8], directions[:, rows - 8 :]], axis=1)
    for index, layer in enumerate(weight_layers(cell_rows[0], cell_rows[1], cell_rows[2], ends)):
        place = probes + index
        for r in range(DEPTH):
            to_above[r, place : place + 1, :] = layer[r : r + 1]
            to_below[r, place : place + 1, :] = layer[16 - DEPTH + r : 16 - DEPTH + r + 1]
    for side in (to_above, to_below):
        side[:, probes + 5 :, :] = jnp.zeros((DEPTH, PACK - 5, columns), jnp.float32)
    for copy in copies:
        copy.wait()


def inner_kernel(
    strength, sites, cells, kappa, speed, friction, upwind, digits, scale, pairs, top, bottom, weights, v, f1, f2, a1, response, sums, tops, found, sems
):
    rows, probes, columns = v.shape
    first_row = lax.axis_index(AXIS) * rows

    copies = [pltpu.make_async_copy(cells.at[:, r, :], v.at[r], sems.at[r]) for r in range(rows)]
    for copy in copies[:ARRIVALS]:
        copy.start()
    for index, layer in enumerate(weight_layers(kappa[...], speed[...], friction[...], upwind[...])):
        weights[index] = layer
    turn_weights(weights)
    first_cell, end_cell = first_row * columns, (first_row + rows) * columns
    hits = find_impulses(sites, found, lambda site: (site >= first_cell) & (site < end_cell), probes)
    def forward_first(r):
        forward_row(v, r, f1, r, weights, r, probes, columns)

    ready, done = 0, 1
    while ready < rows:
        upto = min(rows, ready + ARRIVALS)
        for copy in copies[upto : upto + ARRIVALS]:
            copy.start()
        for copy in copies[ready:upto]:
            copy.wait()
        low, high = first_row + ready, first_row + upto
        add_impulses(
            sites, found, hits, v, lambda row: row - first_row, columns, strength,
            lambda row, low=low, high=high: (row >= low) & (row < high),
        )
        in_steps(done, upto - 1, forward_first)
        ready, done = upto, upto - 1

    def sweep(row_fn, source, target, first, shift=0, **kept):
        def body(r):
            row_fn(source, r, target, r - shift, weights, r, probes, columns, **kept)

        in_steps(first, rows - first, body)

    sweep(forward_row, f1, f2, 2)
    sweep(adjoint_row, f2, a1, 3)
    tops[...] = jnp.zeros_like(tops)
    sweep(adjoint_row, a1, response, DEPTH, DEPTH, tops=tops)
    for level, field in enumerate((v, f1, f2, a1)):
        for j in range(2):
            top[level, j] = field[level + j]
            bottom[level, j] = field[rows - 2 - level + j]
    high, low = gram_pair(response, rows - 2 * DEPTH, tops, digits, scale, sums)
    pairs[...] = jnp.concatenate([folded(high), folded(low)], axis=0)


def edge_kernel(
    strength, rows, sites, above, below, weights, top, bottom, inner_pairs, digits, scale, pairs,
    w, va, la, lb, behind, response, sums, tops, found, sems,
):
    probes, columns = top.shape[2:]
    first_row = lax.axis_index(AXIS) * rows
    start_a, start_b = 2 * DEPTH, 4 * DEPTH
    vb = va.at[DEPTH + 2 :]
    copies = [
        (above.at[:, pl.ds(probes, PACK), :], behind.at[0]),
        (below.at[:, pl.ds(probes, PACK), :], behind.at[1]),
        (weights.at[pl.ds(0, 5), pl.ds(0, 8), :], w.at[pl.ds(0, 5), pl.ds(start_a, 8), :]),
        (weights.at[pl.ds(0, 5), pl.ds(rows - 8, 8), :], w.at[pl.ds(0, 5), pl.ds(start_b, 8), :]),
        (above.at[:, pl.ds(0, probes), :], va.at[pl.ds(0, DEPTH)]),
        (below.at[:, pl.ds(0, probes), :], va.at[pl.ds(DEPTH + 4, DEPTH)]),
        (top.at[0], va.at[pl.ds(DEPTH, 2)]),
        (bottom.at[0], va.at[pl.ds(DEPTH + 2, 2)]),
        (top.at[pl.ds(1, 3)], la.at[:, pl.ds(DEPTH, 2)]),
        (bottom.at[pl.ds(1, 3)], lb.at[:, pl.ds(0, 2)]),
    ]
    copies = [pltpu.make_async_copy(source, target, sems.at[i]) for i, (source, target) in enumerate(copies)]
    for copy in copies:
        copy.start()

    cells = rows * columns
    first_cell = first_row * columns

    def held(site):
        near = site - first_cell
        is_above = (near >= -DEPTH * columns) & (near < 0)
        return is_above | ((near >= cells) & (near < cells + DEPTH * columns))

    hits = find_impulses(sites, found, held, probes)
    for copy in copies:
        copy.wait()
    for layer in range(5):
        for r in range(DEPTH):
            w[layer, DEPTH + r : DEPTH + r + 1, :] = behind[0, r, layer : layer + 1, :]
            w[layer, start_b + 2 * DEPTH + r : start_b + 2 * DEPTH + r + 1, :] = behind[1, r, layer : layer + 1, :]
    turn_weights(w)
    add_impulses(
        sites, found, hits, va,
        lambda row: jnp.where(row < first_row, row - first_row + DEPTH, row - first_row - rows + DEPTH + 4), columns, strength,
    )
    chain_a = [va, la.at[0], la.at[1], la.at[2], response]
    chain_b = [vb, lb.at[0], lb.at[1], lb.at[2], response]
    for level in range(4):
        row_fn = forward_row if level < 2 else adjoint_row
        for j in range(DEPTH):
            row_fn(chain_a[level], j + 1, chain_a[level + 1], j, w, start_a + level - 3 + j, probes, columns)
            to = j + (DEPTH if level == 3 else 2)
            row_fn(chain_b[level], j + 1, chain_b[level + 1], to, w, start_b + 7 - level + j, probes, columns)
    for first in range(0, probes, 8):
        sizes = [jnp.abs(response[r, first : first + 8, :]) for r in range(2 * DEPTH)]
        tops[first : first + 8, :] = functools.reduce(jnp.maximum, sizes)
    ours = gram_pair(response, 2 * DEPTH, tops, digits, scale, sums)
    half = probes // 2
    high, low = pair_sum(ours, (unfolded(inner_pairs[:half, :]), unfolded(inner_pairs[half:, :])))
    pairs[...] = jnp.concatenate([folded(high), folded(low)], axis=0)


DIGITS = 4
ROUNDER = 12582912.0


def rounded(value):
    return (value + ROUNDER) - ROUNDER


def digits_of(value):
    out = []
    for position in range(DIGITS):
        digit = rounded(value)
        out.append(digit)
        if position < DIGITS - 1:
            value = (value - digit) * 256.0
    return out


def largest_power(fits, like):
    power = jnp.full(like, 2.0**-63, jnp.float32)
    for step in (64, 32, 16, 8, 4, 2, 1):
        candidate = power * 2.0**step
        power = jnp.where((candidate <= 2.0**63) & fits(candidate), candidate, power)
    return power


def unit(size):
    return lax.broadcasted_iota(jnp.int32, (size, size), 0) == lax.broadcasted_iota(jnp.int32, (size, size), 1)


def as_row(column):
    size = column.shape[0]
    return jnp.sum(jnp.where(unit(size), jnp.broadcast_to(column, (size, size)), 0.0), axis=0, keepdims=True)


def pair_of(high, low):
    total = high + low
    return total, low - (total - high)


def pair_sum(a, b):
    (a_high, a_low), (b_high, b_low) = a, b
    total = a_high + b_high
    back = total - a_high
    error = (a_high - (total - back)) + (b_high - back)
    return pair_of(total, error + (a_low + b_low))


def gram_pair(field, rows, tops, cells, scale_out, sums):
    probes, columns = field.shape[1:]

    top = jnp.max(tops[...], axis=1, keepdims=True)
    scale = largest_power(lambda power: top * power <= 128.0, (probes, 1))
    inverse = 1.0 / scale
    scale_out[...] = jnp.broadcast_to(inverse, scale_out.shape)
    sums[...] = jnp.zeros_like(sums)

    def cut(index):
        for r in range(GROUP):
            at = GROUP * index + r
            parts = digits_of(field[at] * scale)
            cells[at] = jnp.concatenate([part.astype(jnp.bfloat16) for part in parts], axis=0)

    def products(index):
        total = None
        for pair in range(GROUP // 2):
            r = GROUP * index + 2 * pair
            two = jnp.concatenate([cells[r], cells[r + 1]], axis=1)
            product = lax.dot_general(two, two, (((1,), (1,)), ((), ())), preferred_element_type=jnp.float32)
            product = product.astype(jnp.int32)
            total = product if total is None else total + product
        return total

    def step(index, carry):
        total = products(index)
        cut(index + 1)
        sums[...] += total
        return carry

    cut(0)
    lax.fori_loop(0, rows // GROUP - 1, step, 0)
    sums[...] += products(rows // GROUP - 1)
    places = []
    for place in range(2 * DIGITS - 1):
        terms = [
            sums[a * probes : (a + 1) * probes, (place - a) * probes : (place - a + 1) * probes]
            for a in range(DIGITS)
            if 0 <= place - a < DIGITS
        ]
        places.append(functools.reduce(lambda x, y: x + y, terms))
    for place in range(2 * DIGITS - 2, 0, -1):
        places[place - 1] = places[place - 1] + (places[place] >> 8)
        places[place] = places[place] & 255
    f32 = jnp.float32
    high = (places[0] >> 8).astype(f32) * 256.0
    middle = ((places[0] & 255) * 65536 + places[1] * 256 + places[2]).astype(f32) * 2.0**-16
    low = (places[3] * 65536 + places[4] * 256 + places[5]).astype(f32) * 2.0**-40
    total, rest = pair_of(high, middle)
    total, rest = pair_of(total, rest + low)
    across = as_row(inverse)
    return total * inverse * across, rest * inverse * across


def folded(square):
    half = square.shape[0] // 2
    return jnp.concatenate([square[:half], square[half:]], axis=1)


def unfolded(block):
    half = block.shape[1] // 2
    return jnp.concatenate([block[:, :half], block[:, half:]], axis=0)


def dot(a, b, dims=((1,), (0,))):
    return lax.dot_general(
        a, b, (dims, ((), ())), precision=lax.Precision.HIGHEST, preferred_element_type=jnp.float32
    )


def turned_over(block):
    size, wide = block.shape
    square = jnp.concatenate([block, jnp.zeros((wide - size, wide), jnp.float32)], axis=0)
    return jnp.transpose(square)[:, :size]


PANEL = 8


def eliminated(block):
    size, wide = block.shape
    count = size // 8
    groups = [block[8 * g : 8 * g + 8] for g in range(count)]
    like = (8, wide)
    below = lax.broadcasted_iota(jnp.int32, like, 0)
    for first in range(0, size, PANEL):
        g, start = divmod(first, 8)
        columns = {
            o: [jnp.broadcast_to(groups[o][:, first + t : first + t + 1], like) for t in range(PANEL)]
            for o in range(g, count)
        }
        for t in range(PANEL):
            s = start + t
            across = [jnp.broadcast_to(columns[g][u][s : s + 1], like) for u in range(t, PANEL)]
            inverse = 1.0 / across[0]
            row = jnp.broadcast_to(groups[g][s : s + 1], like) * inverse
            across = [value * inverse for value in across]
            for o in range(g, count):
                if o == g and s == 7:
                    continue
                column = columns[o][t]
                if o == g:
                    column = jnp.where(below > s, column, 0.0)
                groups[o] = groups[o] - column * row
                for u in range(t + 1, PANEL):
                    columns[o][u] = columns[o][u] - column * across[u - t]
    return normalised(jnp.concatenate(groups, axis=0))


def normalised(block):
    size, wide = block.shape
    row_ids = lax.broadcasted_iota(jnp.int32, block.shape, 0)
    lanes = lax.broadcasted_iota(jnp.int32, block.shape, 1)
    pivots = jnp.sum(jnp.where(row_ids == lanes, block, 0.0), axis=1, keepdims=True)
    scale = lax.rsqrt(pivots)
    scale = scale * (1.5 - 0.5 * pivots * scale * scale)
    block = block * scale
    keep = (lanes >= row_ids) & ((lanes < size) | (lanes - size <= row_ids))
    return jnp.where(keep, block, 0.0)


def eliminated_slowly(block, work):
    size, wide = block.shape
    work[...] = block
    row_ids = lax.broadcasted_iota(jnp.int32, (size, 1), 0)
    lanes = lax.broadcasted_iota(jnp.int32, (1, wide), 1)

    def step(j, carry):
        row = work[pl.ds(j, 1), :]
        pivot = jnp.sum(jnp.where(lanes == j, row, 0.0), axis=1, keepdims=True)
        column = jnp.sum(jnp.where(lanes == j, work[...], 0.0), axis=1, keepdims=True)
        work[...] = work[...] - jnp.where(row_ids > j, column, 0.0) * (row / pivot)
        return carry

    lax.fori_loop(0, size, step, 0)
    return normalised(work[...])


def stacked_digits(value):
    return jnp.concatenate([part.astype(jnp.bfloat16) for part in digits_of(value)], axis=0)


def residual(high, low, left, right):
    size = high.shape[0]
    product = lax.dot_general(left, right, (((1,), (1,)), ((), ())), preferred_element_type=jnp.float32)
    places = []
    for place in range(2 * DIGITS - 1):
        terms = [
            product[a * size : (a + 1) * size, (place - a) * size : (place - a + 1) * size]
            for a in range(DIGITS)
            if 0 <= place - a < DIGITS
        ]
        places.append(functools.reduce(lambda x, y: x + y, terms))
    rest = high
    total = jnp.zeros_like(high)
    for place in range(5):
        if place == 2:
            rest = rest + low * 2.0**16
        digit = rounded(rest) if place < 4 else rest
        rest = (rest - digit) * 256.0
        total = total * 256.0 + (digit - places[place])
    total = total - (places[5] * 2.0**-8 + places[6] * 2.0**-16)
    return total * 2.0**-32


def solve_kernel(
    cell_scale, pairs, inner_scale, edge_scale, inner, edge, basis, factor,
    rows_out, work, change, change_inverse, out_sems,
):
    size = pairs.shape[0]
    inner_rows, edge_rows = inner.shape[0], edge.shape[0]
    rows = inner_rows + edge_rows
    high, low = unfolded(pairs[: size // 2, :]), unfolded(pairs[size // 2 :, :])
    is_diagonal = unit(size)
    diagonal = jnp.sum(jnp.where(is_diagonal, high, 0.0), axis=1, keepdims=True)
    scale = largest_power(lambda power: diagonal * power * power < 1.0, (size, 1))
    across = as_row(scale)
    high, low = high * scale * across, low * scale * across
    identity = jnp.where(is_diagonal, 1.0, 0.0)
    first = eliminated(jnp.concatenate([high, identity], axis=1))
    inverse = first[:, size:]
    lower = turned_over(first)[:size]
    lower_digits = stacked_digits(lower * 128.0)
    missed = residual(high * 2.0**14, low * 2.0**14, lower_digits, lower_digits) * 2.0**-14
    inverse_top = jnp.max(jnp.abs(inverse), axis=1, keepdims=True)
    inverse_scale = largest_power(lambda power: inverse_top * power <= 128.0, (size, 1))
    goal = identity * (inverse_scale * 128.0)
    skew = residual(
        goal, jnp.zeros_like(goal), stacked_digits(inverse * inverse_scale), stacked_digits(first[:, :size] * 128.0)
    ) * (-1.0 / 128.0 / inverse_scale)
    near = identity + skew
    error = dot(dot(inverse, missed), inverse, ((1,), (1,))) + (dot(near, near, ((1,), (1,))) - identity)
    weight = jnp.where(
        is_diagonal, 0.5,
        jnp.where(
            lax.broadcasted_iota(jnp.int32, (size, size), 0) > lax.broadcasted_iota(jnp.int32, (size, size), 1), 1.0, 0.0
        ),
    )
    spread = jnp.sum(error * error)
    is_small = spread < 4e-4

    @pl.when(is_small)
    def _():
        y = weight * error
        rounds = jnp.where(spread < 1e-5, 2, 4)
        y = lax.fori_loop(0, rounds, lambda _, y: weight * (error - dot(y, y, ((1,), (1,)))), y)
        change[...] = y
        square = dot(y, y)
        change_inverse[...] = (identity - y) + dot(identity - y, square)

    @pl.when(jnp.logical_not(is_small))
    def _():
        second = eliminated_slowly(jnp.concatenate([identity + error, identity], axis=1), work)
        change[...] = turned_over(second)[:size] - identity
        change_inverse[...] = second[:, size:]

    turn = change[...] - skew
    full = lower + dot(lower, turn - dot(skew, turn))
    full = jnp.concatenate([full, jnp.zeros_like(full)], axis=1)
    factor[...] = turned_over(full)[:size] / across * (1.0 / cell_scale)
    mixing = dot(change_inverse[...], inverse) * across * cell_scale

    def stacked(cut):
        whole_part = mixing * as_row(cut[:, :1])
        pieces = []
        for _ in range(3):
            piece = whole_part.astype(jnp.bfloat16)
            whole_part = whole_part - piece.astype(jnp.float32)
            pieces.append(piece.astype(jnp.float32))
        tall = jnp.concatenate(pieces, axis=0)
        return jnp.concatenate([tall * 256.0**-a for a in range(DIGITS)], axis=1).astype(jnp.bfloat16)

    def finish(matrix, cells, first_row, count, shift):
        group = math.gcd(count, 6 * GROUP)

        def several(index, carry):
            for j in range(group):
                r = group * index + j
                product = jnp.dot(matrix, cells[r + shift], preferred_element_type=jnp.float32)
                rows_out[r + first_row] = product[:size] + (product[size : 2 * size] + product[2 * size :])
            for j in range(group):
                at = group * index + j + first_row
                pltpu.make_async_copy(rows_out.at[at], basis.at[:, at, :], out_sems.at[at]).start()
            return carry

        lax.fori_loop(0, count // group, several, 0)

    finish(stacked(inner_scale), inner, DEPTH, inner_rows, 0)
    matrix = stacked(edge_scale)
    finish(matrix, edge, 0, DEPTH, 0)
    finish(matrix, edge, rows - DEPTH, DEPTH, DEPTH)

    def wait(r, carry):
        pltpu.make_async_copy(rows_out.at[r], basis.at[:, r, :], out_sems.at[r]).wait()
        return carry

    lax.fori_loop(0, rows, wait, 0)


def whole(memory=pltpu.VMEM):
    return pl.BlockSpec(memory_space=memory)


def call(kernel, name, out_shape, in_specs, out_specs, scratch_shapes=(), cost=None, vmem=56):
    return pl.pallas_call(
        kernel,
        out_shape=out_shape,
        in_specs=in_specs,
        out_specs=out_specs,
        scratch_shapes=scratch_shapes,
        compiler_params=pltpu.CompilerParams(vmem_limit_bytes=vmem * MIB),
        cost_estimate=cost,
        name=name,
    )


def summed(pairs):
    count = lax.axis_size(AXIS)
    half = pairs.shape[0] // 2

    def add(a, b):
        return jnp.concatenate(pair_sum((a[:half], a[half:]), (b[:half], b[half:])), axis=0)

    if count & (count - 1):
        total = pairs
        for step in range(1, count):
            total = add(total, lax.ppermute(pairs, AXIS, [(i, (i + step) % count) for i in range(count)]))
        return total
    distance = 1
    while distance < count:
        pairs = add(pairs, lax.ppermute(pairs, AXIS, [(i, i ^ distance) for i in range(count)]))
        distance *= 2
    return pairs


def on_device(probes, kappa, speed, friction, upwind, probe_sites):
    count, rows, columns = probes.shape
    size = lax.axis_size(AXIS)
    f32 = jnp.float32
    cell_scale = math.sqrt(rows * columns * size)
    strength = IMPULSE_GAIN * cell_scale
    shape = jax.ShapeDtypeStruct
    halo = shape((DEPTH, count + PACK, columns), f32)
    to_below, to_above = call(
        pack_kernel,
        "pack",
        (halo, halo),
        [whole(pl.ANY)] * 5,
        (whole(), whole()),
        [
            pltpu.VMEM((3, 16, columns), f32),
            pltpu.VMEM(upwind.shape[::-1], jnp.int32),
            pltpu.SemaphoreType.DMA((2, DEPTH)),
            pltpu.SemaphoreType.DMA((4, 2)),
        ],
        vmem=56,
    )(probes, kappa, speed, friction, upwind.T)
    from_above = lax.ppermute(to_below, AXIS, [(i, i + 1) for i in range(size - 1)])
    from_below = lax.ppermute(to_above, AXIS, [(i + 1, i) for i in range(size - 1)])
    edge_count = 2 * DEPTH
    inner_count = rows - edge_count
    tall = DIGITS * count

    def digit_rows(number):
        return shape((number, tall, columns), jnp.bfloat16), shape((count, 128), f32), shape((count, 2 * count), f32)

    def digit_scratch(number):
        return [
            pltpu.VMEM((number, count, columns), f32),
            pltpu.VMEM((tall, tall), jnp.int32),
            pltpu.VMEM((count, columns), f32),
        ]

    kept = shape((4, 2, count, columns), f32)
    field = pltpu.VMEM((rows, count, columns), f32)
    inner, inner_scale, pairs, top, bottom, weights = call(
        functools.partial(inner_kernel, strength),
        "inner_rows",
        digit_rows(inner_count) + (kept, kept, shape((7, rows, columns), f32)),
        [whole(pltpu.SMEM), whole(pl.ANY)] + [whole()] * 4,
        (whole(),) * 6,
        [field] * 4
        + digit_scratch(inner_count)
        + [pltpu.SMEM((count + 1,), jnp.int32)]
        + [pltpu.SemaphoreType.DMA((rows,))],
        pl.CostEstimate(flops=10**10, bytes_accessed=16 * MIB, transcendentals=0),
        vmem=32,
    )(probe_sites, probes, kappa, speed, friction, upwind.T)
    fields = pltpu.VMEM((2 * DEPTH + 4, count, columns), f32)
    levels = pltpu.VMEM((3, DEPTH + 2, count, columns), f32)
    edge, edge_scale, pairs = call(
        functools.partial(edge_kernel, strength, rows),
        "edge_rows",
        digit_rows(edge_count),
        [whole(pltpu.SMEM)] + [whole(pl.ANY)] * 5 + [whole()],
        (whole(), whole(), whole()),
        [
            pltpu.VMEM((7, 8 * DEPTH, columns), f32), fields, levels, levels,
            pltpu.VMEM((2, DEPTH, PACK, columns), f32),
        ]
        + digit_scratch(edge_count)
        + [pltpu.SMEM((count + 1,), jnp.int32), pltpu.SemaphoreType.DMA((10,))],
        vmem=16,
    )(probe_sites, from_above, from_below, weights, top, bottom, pairs)
    pairs = summed(pairs)
    square = pltpu.VMEM((count, count), f32)
    return call(
        functools.partial(solve_kernel, cell_scale),
        "solve",
        (shape((count, rows, columns), f32), shape((count, count), f32)),
        [whole()] * 5,
        (whole(pl.ANY), whole()),
        [
            pltpu.VMEM((rows, count, columns), f32),
            pltpu.VMEM((count, 2 * count), f32),
            square,
            square,
            pltpu.SemaphoreType.DMA((rows,)),
        ],
        vmem=24,
    )(pairs, inner_scale, edge_scale, inner, edge)


def solution(mesh):
    return jax.shard_map(
        on_device,
        mesh=mesh,
        in_specs=(
            P(None, ("groups", "gx"), None),
            P(("groups", "gx"), None),
            P(("groups", "gx"), None),
            P(("groups", "gx"), None),
            P(("groups", "gx"), None),
            P("groups"),
        ),
        out_specs=(P(None, ("groups", "gx"), None), P("groups", None)),
        check_vma=False,
    )
```

```python
import functools
import math

import jax
import jax.numpy as jnp
from jax import lax
from jax.experimental import pallas as pl
from jax.experimental.pallas import tpu as pltpu
from jax.sharding import PartitionSpec as P

TIME_STEP = 0.2
IMPULSE_GAIN = 3.0
AXIS = "gx"
DEPTH = 4
ARRIVALS = 11
GROUP = 4
PACK = 8
MIB = 1024 * 1024


def rolled(row, by):
    return pltpu.roll(row, by % row.shape[-1], row.ndim - 1)


def weight_row(weights, row, layer, like):
    return jnp.broadcast_to(weights[layer, pl.ds(row, 1), :], like)


def in_steps(first, last, body, step=15):
    whole_steps = (last - first) // step

    def several(index, carry):
        for j in range(step):
            body(first + index * step + j)
        return carry

    lax.fori_loop(0, whole_steps, several, 0)
    for r in range(first + whole_steps * step, last):
        body(r)


def sweep_row(source, at, target, to, probes, columns, center, above, below, left, right, tops=None):
    for first in range(0, probes, 8):
        octet = slice(first, first + 8)
        middle = source[at, octet, :]
        result = (
            center * middle
            + above * source[at - 1, octet, :]
            + below * source[at + 1, octet, :]
            + left * rolled(middle, 1)
            + right * rolled(middle, -1)
        )
        target[to, octet, :] = result
        if tops is not None:
            tops[octet, :] = jnp.maximum(tops[octet, :], jnp.abs(result))


def forward_row(source, at, target, to, weights, w_at, probes, columns):
    like = (8, columns)
    sweep_row(
        source, at, target, to, probes, columns,
        *[weight_row(weights, w_at, layer, like) for layer in range(5)],
    )


def adjoint_row(source, at, target, to, weights, w_at, probes, columns, tops=None):
    like = (8, columns)
    sweep_row(
        source, at, target, to, probes, columns,
        weight_row(weights, w_at, 0, like),
        weight_row(weights, w_at - 1, 2, like),
        weight_row(weights, w_at + 1, 1, like),
        weight_row(weights, w_at, 5, like),
        weight_row(weights, w_at, 6, like),
        tops=tops,
    )


def find_impulses(sites, found, held, probes):
    unroll = 8

    def several(index, count):
        for j in range(unroll):
            k = index * unroll + j
            found[count] = k
            count = jnp.where(held(sites[k]), count + 1, count)
        return count

    return lax.fori_loop(0, probes // unroll, several, 0)


def row_and_column(site, columns):
    if columns & (columns - 1):
        return lax.div(site, columns), lax.rem(site, columns)
    return site >> (columns.bit_length() - 1), site & (columns - 1)


def add_impulses(sites, found, count, target, place_of, columns, strength, wanted=None):
    column_ids = lax.broadcasted_iota(jnp.int32, (1, columns), 1)

    def one(index, carry):
        k = found[index]
        row, column = row_and_column(sites[k], columns)

        def add():
            target[place_of(row), pl.ds(k, 1), :] += jnp.where(column_ids == column, strength, 0.0)

        if wanted is None:
            add()
        else:
            pl.when(wanted(row))(add)
        return carry

    lax.fori_loop(0, count, one, 0)


def weight_layers(kappa, speed, friction, upwind):
    rows, columns = kappa.shape
    blocks = upwind.shape[0]
    width = columns // blocks
    spread = (
        lax.broadcasted_iota(jnp.int32, (blocks, columns), 1) // width
        == lax.broadcasted_iota(jnp.int32, (blocks, columns), 0)
    ).astype(jnp.bfloat16)
    directions = lax.dot_general(
        upwind.astype(jnp.float32).astype(jnp.bfloat16), spread, (((0,), (0,)), ((), ())),
        preferred_element_type=jnp.float32,
    )
    column_ids = lax.broadcasted_iota(jnp.int32, (rows, columns), 1)
    layers = [1.0 - TIME_STEP * (4.0 * kappa + speed + friction)]
    for direction in range(4):
        chosen = jnp.where(jnp.abs(directions - direction) < 0.5, speed, 0.0)
        layers.append(TIME_STEP * (kappa + chosen))
    layers[3] = jnp.where(column_ids == 0, 0.0, layers[3])
    layers[4] = jnp.where(column_ids == columns - 1, 0.0, layers[4])
    return layers


def turn_weights(weights):
    weights[5] = rolled(weights[4], 1)
    weights[6] = rolled(weights[3], -1)


def pack_kernel(cells, kappa, speed, friction, upwind, to_below, to_above, cell_rows, directions, sems, cell_sems):
    probes, rows, columns = cells.shape
    copies = []
    for r in range(DEPTH):
        for side, target in enumerate((to_above, to_below)):
            row = r if side == 0 else rows - DEPTH + r
            copies.append(
                pltpu.make_async_copy(cells.at[:, row, :], target.at[r, pl.ds(0, probes), :], sems.at[side, r])
            )
    small = [pltpu.make_async_copy(upwind, directions, cell_sems.at[3, 0])]
    for index, source in enumerate((kappa, speed, friction)):
        for side, row in enumerate((0, rows - 8)):
            small.append(
                pltpu.make_async_copy(
                    source.at[pl.ds(row, 8)], cell_rows.at[index, pl.ds(8 * side, 8)], cell_sems.at[index, side]
                )
            )
    for copy in copies + small:
        copy.start()
    for copy in small:
        copy.wait()
    ends = jnp.concatenate([directions[:, :8], directions[:, rows - 8 :]], axis=1)
    for index, layer in enumerate(weight_layers(cell_rows[0], cell_rows[1], cell_rows[2], ends)):
        place = probes + index
        for r in range(DEPTH):
            to_above[r, place : place + 1, :] = layer[r : r + 1]
            to_below[r, place : place + 1, :] = layer[16 - DEPTH + r : 16 - DEPTH + r + 1]
    for side in (to_above, to_below):
        side[:, probes + 5 :, :] = jnp.zeros((DEPTH, PACK - 5, columns), jnp.float32)
    for copy in copies:
        copy.wait()


def inner_kernel(
    strength, sites, cells, kappa, speed, friction, upwind, digits, scale, pairs, top, bottom, weights, v, f1, f2, a1, response, sums, tops, found, sems
):
    rows, probes, columns = v.shape
    first_row = lax.axis_index(AXIS) * rows

    copies = [pltpu.make_async_copy(cells.at[:, r, :], v.at[r], sems.at[r]) for r in range(rows)]
    for copy in copies[:ARRIVALS]:
        copy.start()
    for index, layer in enumerate(weight_layers(kappa[...], speed[...], friction[...], upwind[...])):
        weights[index] = layer
    turn_weights(weights)
    first_cell, end_cell = first_row * columns, (first_row + rows) * columns
    hits = find_impulses(sites, found, lambda site: (site >= first_cell) & (site < end_cell), probes)
    def forward_first(r):
        forward_row(v, r, f1, r, weights, r, probes, columns)

    ready, done = 0, 1
    while ready < rows:
        upto = min(rows, ready + ARRIVALS)
        for copy in copies[upto : upto + ARRIVALS]:
            copy.start()
        for copy in copies[ready:upto]:
            copy.wait()
        low, high = first_row + ready, first_row + upto
        add_impulses(
            sites, found, hits, v, lambda row: row - first_row, columns, strength,
            lambda row, low=low, high=high: (row >= low) & (row < high),
        )
        in_steps(done, upto - 1, forward_first)
        ready, done = upto, upto - 1

    def sweep(row_fn, source, target, first, shift=0, **kept):
        def body(r):
            row_fn(source, r, target, r - shift, weights, r, probes, columns, **kept)

        in_steps(first, rows - first, body)

    sweep(forward_row, f1, f2, 2)
    sweep(adjoint_row, f2, a1, 3)
    tops[...] = jnp.zeros_like(tops)
    sweep(adjoint_row, a1, response, DEPTH, DEPTH, tops=tops)
    for level, field in enumerate((v, f1, f2, a1)):
        for j in range(2):
            top[level, j] = field[level + j]
            bottom[level, j] = field[rows - 2 - level + j]
    high, low = gram_pair(response, rows - 2 * DEPTH, tops, digits, scale, sums)
    pairs[...] = jnp.concatenate([folded(high), folded(low)], axis=0)


def edge_kernel(
    strength, rows, sites, above, below, weights, top, bottom, inner_pairs, digits, scale, pairs,
    w, va, la, lb, behind, response, sums, tops, found, sems,
):
    probes, columns = top.shape[2:]
    first_row = lax.axis_index(AXIS) * rows
    start_a, start_b = 2 * DEPTH, 4 * DEPTH
    vb = va.at[DEPTH + 2 :]
    copies = [
        (above.at[:, pl.ds(probes, PACK), :], behind.at[0]),
        (below.at[:, pl.ds(probes, PACK), :], behind.at[1]),
        (weights.at[pl.ds(0, 5), pl.ds(0, 8), :], w.at[pl.ds(0, 5), pl.ds(start_a, 8), :]),
        (weights.at[pl.ds(0, 5), pl.ds(rows - 8, 8), :], w.at[pl.ds(0, 5), pl.ds(start_b, 8), :]),
        (above.at[:, pl.ds(0, probes), :], va.at[pl.ds(0, DEPTH)]),
        (below.at[:, pl.ds(0, probes), :], va.at[pl.ds(DEPTH + 4, DEPTH)]),
        (top.at[0], va.at[pl.ds(DEPTH, 2)]),
        (bottom.at[0], va.at[pl.ds(DEPTH + 2, 2)]),
        (top.at[pl.ds(1, 3)], la.at[:, pl.ds(DEPTH, 2)]),
        (bottom.at[pl.ds(1, 3)], lb.at[:, pl.ds(0, 2)]),
    ]
    copies = [pltpu.make_async_copy(source, target, sems.at[i]) for i, (source, target) in enumerate(copies)]
    for copy in copies:
        copy.start()

    cells = rows * columns
    first_cell = first_row * columns

    def held(site):
        near = site - first_cell
        is_above = (near >= -DEPTH * columns) & (near < 0)
        return is_above | ((near >= cells) & (near < cells + DEPTH * columns))

    hits = find_impulses(sites, found, held, probes)
    for copy in copies:
        copy.wait()
    for layer in range(5):
        for r in range(DEPTH):
            w[layer, DEPTH + r : DEPTH + r + 1, :] = behind[0, r, layer : layer + 1, :]
            w[layer, start_b + 2 * DEPTH + r : start_b + 2 * DEPTH + r + 1, :] = behind[1, r, layer : layer + 1, :]
    turn_weights(w)
    add_impulses(
        sites, found, hits, va,
        lambda row: jnp.where(row < first_row, row - first_row + DEPTH, row - first_row - rows + DEPTH + 4), columns, strength,
    )
    chain_a = [va, la.at[0], la.at[1], la.at[2], response]
    chain_b = [vb, lb.at[0], lb.at[1], lb.at[2], response]
    for level in range(4):
        row_fn = forward_row if level < 2 else adjoint_row
        for j in range(DEPTH):
            row_fn(chain_a[level], j + 1, chain_a[level + 1], j, w, start_a + level - 3 + j, probes, columns)
            to = j + (DEPTH if level == 3 else 2)
            row_fn(chain_b[level], j + 1, chain_b[level + 1], to, w, start_b + 7 - level + j, probes, columns)
    for first in range(0, probes, 8):
        sizes = [jnp.abs(response[r, first : first + 8, :]) for r in range(2 * DEPTH)]
        tops[first : first + 8, :] = functools.reduce(jnp.maximum, sizes)
    ours = gram_pair(response, 2 * DEPTH, tops, digits, scale, sums)
    half = probes // 2
    high, low = pair_sum(ours, (unfolded(inner_pairs[:half, :]), unfolded(inner_pairs[half:, :])))
    pairs[...] = jnp.concatenate([folded(high), folded(low)], axis=0)


DIGITS = 4
ROUNDER = 12582912.0


def rounded(value):
    return (value + ROUNDER) - ROUNDER


def digits_of(value):
    out = []
    for position in range(DIGITS):
        digit = rounded(value)
        out.append(digit)
        if position < DIGITS - 1:
            value = (value - digit) * 256.0
    return out


def largest_power(fits, like):
    power = jnp.full(like, 2.0**-63, jnp.float32)
    for step in (64, 32, 16, 8, 4, 2, 1):
        candidate = power * 2.0**step
        power = jnp.where((candidate <= 2.0**63) & fits(candidate), candidate, power)
    return power


def unit(size):
    return lax.broadcasted_iota(jnp.int32, (size, size), 0) == lax.broadcasted_iota(jnp.int32, (size, size), 1)


def as_row(column):
    size = column.shape[0]
    return jnp.sum(jnp.where(unit(size), jnp.broadcast_to(column, (size, size)), 0.0), axis=0, keepdims=True)


def pair_of(high, low):
    total = high + low
    return total, low - (total - high)


def pair_sum(a, b):
    (a_high, a_low), (b_high, b_low) = a, b
    total = a_high + b_high
    back = total - a_high
    error = (a_high - (total - back)) + (b_high - back)
    return pair_of(total, error + (a_low + b_low))


def gram_pair(field, rows, tops, cells, scale_out, sums):
    probes, columns = field.shape[1:]

    top = jnp.max(tops[...], axis=1, keepdims=True)
    scale = largest_power(lambda power: top * power <= 128.0, (probes, 1))
    inverse = 1.0 / scale
    scale_out[...] = jnp.broadcast_to(inverse, scale_out.shape)
    sums[...] = jnp.zeros_like(sums)

    def cut(index):
        for r in range(GROUP):
            at = GROUP * index + r
            parts = digits_of(field[at] * scale)
            cells[at] = jnp.concatenate([part.astype(jnp.bfloat16) for part in parts], axis=0)

    def products(index):
        total = None
        for pair in range(GROUP // 2):
            r = GROUP * index + 2 * pair
            two = jnp.concatenate([cells[r], cells[r + 1]], axis=1)
            product = lax.dot_general(two, two, (((1,), (1,)), ((), ())), preferred_element_type=jnp.float32)
            product = product.astype(jnp.int32)
            total = product if total is None else total + product
        return total

    def step(index, carry):
        total = products(index)
        cut(index + 1)
        sums[...] += total
        return carry

    cut(0)
    lax.fori_loop(0, rows // GROUP - 1, step, 0)
    sums[...] += products(rows // GROUP - 1)
    places = []
    for place in range(2 * DIGITS - 1):
        terms = [
            sums[a * probes : (a + 1) * probes, (place - a) * probes : (place - a + 1) * probes]
            for a in range(DIGITS)
            if 0 <= place - a < DIGITS
        ]
        places.append(functools.reduce(lambda x, y: x + y, terms))
    for place in range(2 * DIGITS - 2, 0, -1):
        places[place - 1] = places[place - 1] + (places[place] >> 8)
        places[place] = places[place] & 255
    f32 = jnp.float32
    high = (places[0] >> 8).astype(f32) * 256.0
    middle = ((places[0] & 255) * 65536 + places[1] * 256 + places[2]).astype(f32) * 2.0**-16
    low = (places[3] * 65536 + places[4] * 256 + places[5]).astype(f32) * 2.0**-40
    total, rest = pair_of(high, middle)
    total, rest = pair_of(total, rest + low)
    across = as_row(inverse)
    return total * inverse * across, rest * inverse * across


def folded(square):
    half = square.shape[0] // 2
    return jnp.concatenate([square[:half], square[half:]], axis=1)


def unfolded(block):
    half = block.shape[1] // 2
    return jnp.concatenate([block[:, :half], block[:, half:]], axis=0)


def dot(a, b, dims=((1,), (0,))):
    return lax.dot_general(
        a, b, (dims, ((), ())), precision=lax.Precision.HIGHEST, preferred_element_type=jnp.float32
    )


def turned_over(block):
    size, wide = block.shape
    square = jnp.concatenate([block, jnp.zeros((wide - size, wide), jnp.float32)], axis=0)
    return jnp.transpose(square)[:, :size]


PANEL = 8


def eliminated(block):
    size, wide = block.shape
    count = size // 8
    groups = [block[8 * g : 8 * g + 8] for g in range(count)]
    like = (8, wide)
    below = lax.broadcasted_iota(jnp.int32, like, 0)
    for first in range(0, size, PANEL):
        g, start = divmod(first, 8)
        columns = {
            o: [jnp.broadcast_to(groups[o][:, first + t : first + t + 1], like) for t in range(PANEL)]
            for o in range(g, count)
        }
        for t in range(PANEL):
            s = start + t
            across = [jnp.broadcast_to(columns[g][u][s : s + 1], like) for u in range(t, PANEL)]
            inverse = 1.0 / across[0]
            row = jnp.broadcast_to(groups[g][s : s + 1], like) * inverse
            across = [value * inverse for value in across]
            for o in range(g, count):
                if o == g and s == 7:
                    continue
                column = columns[o][t]
                if o == g:
                    column = jnp.where(below > s, column, 0.0)
                groups[o] = groups[o] - column * row
                for u in range(t + 1, PANEL):
                    columns[o][u] = columns[o][u] - column * across[u - t]
    return normalised(jnp.concatenate(groups, axis=0))


def normalised(block):
    size, wide = block.shape
    row_ids = lax.broadcasted_iota(jnp.int32, block.shape, 0)
    lanes = lax.broadcasted_iota(jnp.int32, block.shape, 1)
    pivots = jnp.sum(jnp.where(row_ids == lanes, block, 0.0), axis=1, keepdims=True)
    scale = lax.rsqrt(pivots)
    scale = scale * (1.5 - 0.5 * pivots * scale * scale)
    block = block * scale
    keep = (lanes >= row_ids) & ((lanes < size) | (lanes - size <= row_ids))
    return jnp.where(keep, block, 0.0)


def eliminated_slowly(block, work):
    size, wide = block.shape
    work[...] = block
    row_ids = lax.broadcasted_iota(jnp.int32, (size, 1), 0)
    lanes = lax.broadcasted_iota(jnp.int32, (1, wide), 1)

    def step(j, carry):
        row = work[pl.ds(j, 1), :]
        pivot = jnp.sum(jnp.where(lanes == j, row, 0.0), axis=1, keepdims=True)
        column = jnp.sum(jnp.where(lanes == j, work[...], 0.0), axis=1, keepdims=True)
        work[...] = work[...] - jnp.where(row_ids > j, column, 0.0) * (row / pivot)
        return carry

    lax.fori_loop(0, size, step, 0)
    return normalised(work[...])


def stacked_digits(value):
    return jnp.concatenate([part.astype(jnp.bfloat16) for part in digits_of(value)], axis=0)


def residual(high, low, left, right):
    size = high.shape[0]
    product = lax.dot_general(left, right, (((1,), (1,)), ((), ())), preferred_element_type=jnp.float32)
    places = []
    for place in range(2 * DIGITS - 1):
        terms = [
            product[a * size : (a + 1) * size, (place - a) * size : (place - a + 1) * size]
            for a in range(DIGITS)
            if 0 <= place - a < DIGITS
        ]
        places.append(functools.reduce(lambda x, y: x + y, terms))
    rest = high
    total = jnp.zeros_like(high)
    for place in range(5):
        if place == 2:
            rest = rest + low * 2.0**16
        digit = rounded(rest) if place < 4 else rest
        rest = (rest - digit) * 256.0
        total = total * 256.0 + (digit - places[place])
    total = total - (places[5] * 2.0**-8 + places[6] * 2.0**-16)
    return total * 2.0**-32


def solve_kernel(
    cell_scale, pairs, inner_scale, edge_scale, inner, edge, basis, factor,
    rows_out, work, change, change_inverse, out_sems,
):
    size = pairs.shape[0]
    inner_rows, edge_rows = inner.shape[0], edge.shape[0]
    rows = inner_rows + edge_rows
    high, low = unfolded(pairs[: size // 2, :]), unfolded(pairs[size // 2 :, :])
    is_diagonal = unit(size)
    diagonal = jnp.sum(jnp.where(is_diagonal, high, 0.0), axis=1, keepdims=True)
    scale = largest_power(lambda power: diagonal * power * power < 1.0, (size, 1))
    across = as_row(scale)
    high, low = high * scale * across, low * scale * across
    identity = jnp.where(is_diagonal, 1.0, 0.0)
    first = eliminated(jnp.concatenate([high, identity], axis=1))
    inverse = first[:, size:]
    lower = turned_over(first)[:size]
    lower_digits = stacked_digits(lower * 128.0)
    missed = residual(high * 2.0**14, low * 2.0**14, lower_digits, lower_digits) * 2.0**-14
    inverse_top = jnp.max(jnp.abs(inverse), axis=1, keepdims=True)
    inverse_scale = largest_power(lambda power: inverse_top * power <= 128.0, (size, 1))
    goal = identity * (inverse_scale * 128.0)
    skew = residual(
        goal, jnp.zeros_like(goal), stacked_digits(inverse * inverse_scale), stacked_digits(first[:, :size] * 128.0)
    ) * (-1.0 / 128.0 / inverse_scale)
    near = identity + skew
    error = dot(dot(inverse, missed), inverse, ((1,), (1,))) + (dot(near, near, ((1,), (1,))) - identity)
    weight = jnp.where(
        is_diagonal, 0.5,
        jnp.where(
            lax.broadcasted_iota(jnp.int32, (size, size), 0) > lax.broadcasted_iota(jnp.int32, (size, size), 1), 1.0, 0.0
        ),
    )
    spread = jnp.sum(error * error)
    is_small = spread < 4e-4

    @pl.when(is_small)
    def _():
        y = weight * error
        rounds = jnp.where(spread < 1e-5, 2, 4)
        y = lax.fori_loop(0, rounds, lambda _, y: weight * (error - dot(y, y, ((1,), (1,)))), y)
        change[...] = y
        square = dot(y, y)
        change_inverse[...] = (identity - y) + dot(identity - y, square)

    @pl.when(jnp.logical_not(is_small))
    def _():
        second = eliminated_slowly(jnp.concatenate([identity + error, identity], axis=1), work)
        change[...] = turned_over(second)[:size] - identity
        change_inverse[...] = second[:, size:]

    turn = change[...] - skew
    full = lower + dot(lower, turn - dot(skew, turn))
    full = jnp.concatenate([full, jnp.zeros_like(full)], axis=1)
    factor[...] = turned_over(full)[:size] / across * (1.0 / cell_scale)
    mixing = dot(change_inverse[...], inverse) * across * cell_scale

    def stacked(cut):
        whole_part = mixing * as_row(cut[:, :1])
        pieces = []
        for _ in range(3):
            piece = whole_part.astype(jnp.bfloat16)
            whole_part = whole_part - piece.astype(jnp.float32)
            pieces.append(piece.astype(jnp.float32))
        tall = jnp.concatenate(pieces, axis=0)
        return jnp.concatenate([tall * 256.0**-a for a in range(DIGITS)], axis=1).astype(jnp.bfloat16)

    def finish(matrix, cells, first_row, count, shift):
        group = math.gcd(count, 6 * GROUP)

        def several(index, carry):
            for j in range(group):
                r = group * index + j
                product = jnp.dot(matrix, cells[r + shift], preferred_element_type=jnp.float32)
                rows_out[r + first_row] = product[:size] + (product[size : 2 * size] + product[2 * size :])
            for j in range(group):
                at = group * index + j + first_row
                pltpu.make_async_copy(rows_out.at[at], basis.at[:, at, :], out_sems.at[at]).start()
            return carry

        lax.fori_loop(0, count // group, several, 0)

    finish(stacked(inner_scale), inner, DEPTH, inner_rows, 0)
    matrix = stacked(edge_scale)
    finish(matrix, edge, 0, DEPTH, 0)
    finish(matrix, edge, rows - DEPTH, DEPTH, DEPTH)

    def wait(r, carry):
        pltpu.make_async_copy(rows_out.at[r], basis.at[:, r, :], out_sems.at[r]).wait()
        return carry

    lax.fori_loop(0, rows, wait, 0)


def whole(memory=pltpu.VMEM):
    return pl.BlockSpec(memory_space=memory)


def call(kernel, name, out_shape, in_specs, out_specs, scratch_shapes=(), cost=None, vmem=56):
    return pl.pallas_call(
        kernel,
        out_shape=out_shape,
        in_specs=in_specs,
        out_specs=out_specs,
        scratch_shapes=scratch_shapes,
        compiler_params=pltpu.CompilerParams(vmem_limit_bytes=vmem * MIB),
        cost_estimate=cost,
        name=name,
    )


def summed(pairs):
    count = lax.axis_size(AXIS)
    half = pairs.shape[0] // 2

    def add(a, b):
        return jnp.concatenate(pair_sum((a[:half], a[half:]), (b[:half], b[half:])), axis=0)

    if count & (count - 1):
        total = pairs
        for step in range(1, count):
            total = add(total, lax.ppermute(pairs, AXIS, [(i, (i + step) % count) for i in range(count)]))
        return total
    distance = 1
    while distance < count:
        pairs = add(pairs, lax.ppermute(pairs, AXIS, [(i, i ^ distance) for i in range(count)]))
        distance *= 2
    return pairs


def on_device(probes, kappa, speed, friction, upwind, probe_sites):
    count, rows, columns = probes.shape
    size = lax.axis_size(AXIS)
    f32 = jnp.float32
    cell_scale = math.sqrt(rows * columns * size)
    strength = IMPULSE_GAIN * cell_scale
    shape = jax.ShapeDtypeStruct
    halo = shape((DEPTH, count + PACK, columns), f32)
    to_below, to_above = call(
        pack_kernel,
        "pack",
        (halo, halo),
        [whole(pl.ANY)] * 5,
        (whole(), whole()),
        [
            pltpu.VMEM((3, 16, columns), f32),
            pltpu.VMEM(upwind.shape[::-1], jnp.int32),
            pltpu.SemaphoreType.DMA((2, DEPTH)),
            pltpu.SemaphoreType.DMA((4, 2)),
        ],
        vmem=56,
    )(probes, kappa, speed, friction, upwind.T)
    from_above = lax.ppermute(to_below, AXIS, [(i, i + 1) for i in range(size - 1)])
    from_below = lax.ppermute(to_above, AXIS, [(i + 1, i) for i in range(size - 1)])
    edge_count = 2 * DEPTH
    inner_count = rows - edge_count
    tall = DIGITS * count

    def digit_rows(number):
        return shape((number, tall, columns), jnp.bfloat16), shape((count, 128), f32), shape((count, 2 * count), f32)

    def digit_scratch(number):
        return [
            pltpu.VMEM((number, count, columns), f32),
            pltpu.VMEM((tall, tall), jnp.int32),
            pltpu.VMEM((count, columns), f32),
        ]

    kept = shape((4, 2, count, columns), f32)
    field = pltpu.VMEM((rows, count, columns), f32)
    inner, inner_scale, pairs, top, bottom, weights = call(
        functools.partial(inner_kernel, strength),
        "inner_rows",
        digit_rows(inner_count) + (kept, kept, shape((7, rows, columns), f32)),
        [whole(pltpu.SMEM), whole(pl.ANY)] + [whole()] * 4,
        (whole(),) * 6,
        [field] * 4
        + digit_scratch(inner_count)
        + [pltpu.SMEM((count + 1,), jnp.int32)]
        + [pltpu.SemaphoreType.DMA((rows,))],
        pl.CostEstimate(flops=10**10, bytes_accessed=16 * MIB, transcendentals=0),
        vmem=32,
    )(probe_sites, probes, kappa, speed, friction, upwind.T)
    fields = pltpu.VMEM((2 * DEPTH + 4, count, columns), f32)
    levels = pltpu.VMEM((3, DEPTH + 2, count, columns), f32)
    edge, edge_scale, pairs = call(
        functools.partial(edge_kernel, strength, rows),
        "edge_rows",
        digit_rows(edge_count),
        [whole(pltpu.SMEM)] + [whole(pl.ANY)] * 5 + [whole()],
        (whole(), whole(), whole()),
        [
            pltpu.VMEM((7, 8 * DEPTH, columns), f32), fields, levels, levels,
            pltpu.VMEM((2, DEPTH, PACK, columns), f32),
        ]
        + digit_scratch(edge_count)
        + [pltpu.SMEM((count + 1,), jnp.int32), pltpu.SemaphoreType.DMA((10,))],
        vmem=16,
    )(probe_sites, from_above, from_below, weights, top, bottom, pairs)
    pairs = summed(pairs)
    square = pltpu.VMEM((count, count), f32)
    return call(
        functools.partial(solve_kernel, cell_scale),
        "solve",
        (shape((count, rows, columns), f32), shape((count, count), f32)),
        [whole()] * 5,
        (whole(pl.ANY), whole()),
        [
            pltpu.VMEM((rows, count, columns), f32),
            pltpu.VMEM((count, 2 * count), f32),
            square,
            square,
            pltpu.SemaphoreType.DMA((rows,)),
        ],
        vmem=24,
    )(pairs, inner_scale, edge_scale, inner, edge)


def solution(mesh):
    return jax.shard_map(
        on_device,
        mesh=mesh,
        in_specs=(
            P(None, ("groups", "gx"), None),
            P(("groups", "gx"), None),
            P(("groups", "gx"), None),
            P(("groups", "gx"), None),
            P(("groups", "gx"), None),
            P("groups"),
        ),
        out_specs=(P(None, ("groups", "gx"), None), P("groups", None)),
        check_vma=False,
    )
```
